128 devices in a mesh: row: 16 (over y_lo, z, core), col: 8 (over x, y_hi).
Axes of the slice: x: 4, y: 4 (y_hi: 2, y_lo: 2; y = y_hi * 2 + y_lo), z: 4, core: 2. Of those that a mesh axis runs over, the one named last changes fastest.
Arguments:
- block_input: bfloat16 [1, 256, 256, 512], P(None, 'row', 'col'), may hold values from -6 to 6
- w_expand: bfloat16 [512, 2048], replicated, may hold values from -0.25 to 0.25
- w_depthwise: bfloat16 [9, 2048], replicated, may hold values from -2 to 2
- w_project: bfloat16 [2048, 512], replicated, may hold values from -0.125 to 0.125
- w_qkv: bfloat16 [512, 1536], replicated, may hold values from -0.25 to 0.25
- w_out: bfloat16 [512, 512], replicated, may hold values from -0.25 to 0.25
- grad_out: bfloat16 [1, 256, 256, 512], P(None, 'row', 'col'), may hold values from -6 to 6
Outputs:
- block_output: bfloat16 [1, 256, 256, 512], P(None, 'row', 'col')
- grad_input: bfloat16 [1, 256, 256, 512], P(None, 'row', 'col')
- grad_expand: float32 [512, 2048], P(None, ('row', 'col'))
- grad_depthwise: float32 [9, 2048], P(None, ('row', 'col'))
- grad_project: float32 [512, 2048], P(None, ('row', 'col'))
- grad_qkv: float32 [512, 1536], P(None, ('row', 'col'))
- grad_outproj: float32 [512, 512], P(None, ('row', 'col'))
The draws below stay inside these ranges and needn't reach their ends.
All inputs are finite; a program needn't handle non-finite values.
Results may differ from the reference program's by a relative error of at most 0.015.
Values may be sent and summed in bfloat16 or wider, within the bound.
No kernel may reach another device: no remote copies, remote signals or barrier semaphores. Data moves between devices by JAX's collectives and lax.ppermute only.
A program may use at most 128 MiB of HBM per device.

```python
import jax
import jax.numpy as jnp
from jax import lax

D = 512
HEADS = 16
HDIM = 32
HID = 2048
GRID = 8
BATCH = 1
H = 256
W = 256


def shard_levels(key, dims, split, least, top_value):
    def one(axis_at, parts):
        heights = jax.random.uniform(jax.random.fold_in(jax.random.fold_in(key, 6), axis_at), (parts,), jnp.float32, least / len(split), top_value / len(split))
        return jnp.repeat(jnp.exp(heights), dims[axis_at] // parts).reshape((-1,) + (1,) * (len(dims) - axis_at - 1))

    level = one(*split[0])
    for cut in split[1:]:
        level = level * one(*cut)
    return level


def gaussian(key, shape, scale, most, pieces=(), kind=jnp.bfloat16):
    loudness = shard_levels(key, shape, pieces, -0.22, 0.18) if pieces else 1.0
    drawn = jax.random.normal(key, shape, jnp.float32) * scale * loudness
    return jnp.minimum(jnp.maximum(drawn, -most), most).astype(kind)


def setup_inputs(seed: int = 0) -> dict:
    seeds = jax.random.split(jax.random.key(seed), 8)
    block_input = gaussian(seeds[0], (BATCH, H, W, D), 1.0, 6.0, ((1, 16), (2, 8)))
    w_expand = gaussian(seeds[1], (D, HID), D ** -0.5, 0.25)
    w_depthwise = gaussian(seeds[2], (9, HID), 9 ** -0.5, 2.0)
    w_project = gaussian(seeds[3], (HID, D), HID ** -0.5, 0.125)
    w_qkv = gaussian(seeds[4], (D, 3 * D), D ** -0.5, 0.25)
    w_out = gaussian(seeds[5], (D, D), D ** -0.5, 0.25)
    grad_out = gaussian(seeds[6], (BATCH, H, W, D), 1.0, 6.0, ((1, 16), (2, 8)))
    return {"block_input": block_input, "w_expand": w_expand, "w_depthwise": w_depthwise, "w_project": w_project, "w_qkv": w_qkv, "w_out": w_out, "grad_out": grad_out}


EPS = 1e-05

def layer_normalize(value_tensor):
    center = value_tensor - lax.optimization_barrier(jnp.mean(value_tensor, -1, keepdims=True))
    expand_ratio = lax.rsqrt(lax.optimization_barrier(jnp.mean(center * center, -1, keepdims=True)) + EPS)
    return (center * expand_ratio, expand_ratio)

def norm_back(value_tensor, gradient_tree):
    centered_scaled, expand_ratio = layer_normalize(value_tensor)
    return (gradient_tree - lax.optimization_barrier(jnp.mean(gradient_tree, -1, keepdims=True)) - centered_scaled * lax.optimization_barrier(jnp.mean(gradient_tree * centered_scaled, -1, keepdims=True))) * expand_ratio

def slope(value_tensor):
    return jax.vjp(jax.nn.gelu, value_tensor)[1](jnp.ones_like(value_tensor))[0]

def attend(qkv, grad_att):
    count = qkv.shape[0]
    members = qkv.shape[1]
    width = grad_att.shape[-1]
    scale = HDIM ** (-0.5)
    query = qkv[..., :width].reshape(count, members, HEADS, HDIM).astype(jnp.float32)
    keys = qkv[..., width:2 * width].reshape(count, members, HEADS, HDIM).astype(jnp.float32)
    value_tensor = qkv[..., 2 * width:].reshape(count, members, HEADS, HDIM).astype(jnp.float32)
    grad_o = grad_att.reshape(count, members, HEADS, HDIM).astype(jnp.float32)
    scores = jnp.einsum('gqhd,gkhd->ghqk', query, keys) * scale
    probs = jax.nn.softmax(scores, axis=-1)
    probs_b = probs.astype(jnp.bfloat16).astype(jnp.float32)
    attended = jnp.einsum('ghqk,gkhd->gqhd', probs_b, value_tensor).astype(jnp.bfloat16)
    grad_probs = jnp.einsum('gqhd,gkhd->ghqk', grad_o, value_tensor)
    grad_scores = (probs * (grad_probs - lax.optimization_barrier(jnp.sum(probs * grad_probs, -1, keepdims=True))) * scale).astype(jnp.bfloat16).astype(jnp.float32)
    grad_query = jnp.einsum('ghqk,gkhd->gqhd', grad_scores, keys)
    grad_key = jnp.einsum('ghqk,gqhd->gkhd', grad_scores, query)
    grad_value = jnp.einsum('ghqk,gqhd->gkhd', probs_b, grad_o)
    joined = jnp.concatenate([grad_query.reshape(count, members, width), grad_key.reshape(count, members, width), grad_value.reshape(count, members, width)], -1)
    return (attended.reshape(count, members, width), joined.astype(jnp.bfloat16))

def single_image(block_input, w_expand, w_depthwise, w_project, w_qkv, w_out, grad_out):
    rows, cols, width = block_input.shape
    tokens = rows * cols
    cell_rows = rows // GRID
    grid_cell_columns = cols // GRID

    def group(value_tensor):
        chans = value_tensor.shape[-1]
        shaped = value_tensor.reshape(GRID, cell_rows, GRID, grid_cell_columns, chans).transpose(1, 3, 0, 2, 4)
        return shaped.reshape(cell_rows * grid_cell_columns, GRID * GRID, chans)

    def ungroup(value_tensor):
        chans = value_tensor.shape[-1]
        shaped = value_tensor.reshape(cell_rows, grid_cell_columns, GRID, GRID, chans).transpose(2, 0, 3, 1, 4)
        return shaped.reshape(rows, cols, chans)
    inputs = block_input.astype(jnp.float32)
    normed_in = layer_normalize(inputs)[0].astype(jnp.bfloat16)
    widened_hidden = jnp.dot(normed_in.reshape(tokens, width), w_expand, preferred_element_type=jnp.float32).reshape(rows, cols, -1)
    activated = jax.nn.gelu(widened_hidden).astype(jnp.bfloat16)
    padded = jnp.pad(activated, ((1, 1), (1, 1), (0, 0)))
    kernel = w_depthwise.astype(jnp.float32)
    conv = jnp.zeros(widened_hidden.shape, jnp.float32)
    for tap in range(9):
        shift_r, shift_c = divmod(tap, 3)
        conv = conv + padded[shift_r:shift_r + rows, shift_c:shift_c + cols].astype(jnp.float32) * kernel[tap]
    mid = jax.nn.gelu(conv).astype(jnp.bfloat16)
    mid_flat = mid.reshape(tokens, -1)
    resid = (inputs + jnp.dot(mid_flat, w_project, preferred_element_type=jnp.float32).reshape(rows, cols, width)).astype(jnp.bfloat16)
    resid_f = resid.astype(jnp.float32)
    normed_mid = layer_normalize(resid_f)[0].astype(jnp.bfloat16).reshape(tokens, width)
    qkv = jnp.dot(normed_mid, w_qkv, preferred_element_type=jnp.float32).astype(jnp.bfloat16)
    grad_flat = grad_out.reshape(tokens, width)
    grad_att = jnp.dot(grad_flat, w_out.T, preferred_element_type=jnp.float32).astype(jnp.bfloat16)
    qkv_groups = group(qkv.reshape(rows, cols, -1))
    grad_groups = group(grad_att.reshape(rows, cols, width))
    count = qkv_groups.shape[0]
    blocks = count // 64
    results = lax.map(lambda pair: attend(pair[0], pair[1]), (qkv_groups.reshape(blocks, 64, GRID * GRID, -1), grad_groups.reshape(blocks, 64, GRID * GRID, width)))
    attended = ungroup(results[0].reshape(count, GRID * GRID, width)).reshape(tokens, width)
    grad_qkvact = ungroup(results[1].reshape(count, GRID * GRID, 3 * width)).reshape(tokens, 3 * width)
    added = jnp.dot(attended, w_out, preferred_element_type=jnp.float32).astype(jnp.bfloat16)
    block_output = (resid_f + added.reshape(rows, cols, width).astype(jnp.float32)).astype(jnp.bfloat16)
    grad_outproj = jnp.dot(attended.T, grad_flat, preferred_element_type=jnp.float32)
    grad_qkv = jnp.dot(normed_mid.T, grad_qkvact, preferred_element_type=jnp.float32)
    grad_normed = jnp.dot(grad_qkvact, w_qkv.T, preferred_element_type=jnp.float32).astype(jnp.bfloat16)
    grad_resid = (grad_out.astype(jnp.float32) + norm_back(resid_f, grad_normed.reshape(rows, cols, width).astype(jnp.float32))).astype(jnp.bfloat16)
    grad_resid_flat = grad_resid.reshape(tokens, width)
    grad_project = jnp.dot(grad_resid_flat.T, mid_flat, preferred_element_type=jnp.float32)
    grad_mid_f = jnp.dot(grad_resid_flat, w_project.T, preferred_element_type=jnp.float32).reshape(rows, cols, -1)
    grad_mid = (grad_mid_f * slope(conv)).astype(jnp.bfloat16)
    grad_pad = jnp.pad(grad_mid, ((1, 1), (1, 1), (0, 0)))
    grad_act = jnp.zeros(widened_hidden.shape, jnp.float32)
    tap_grads = []
    grad_mid_32 = grad_mid.astype(jnp.float32)
    for tap in range(9):
        shift_r, shift_c = divmod(tap, 3)
        grad_act = grad_act + grad_pad[2 - shift_r:2 - shift_r + rows, 2 - shift_c:2 - shift_c + cols].astype(jnp.float32) * kernel[tap]
        tap_grads.append(lax.optimization_barrier(jnp.sum(padded[shift_r:shift_r + rows, shift_c:shift_c + cols].astype(jnp.float32) * grad_mid_32, axis=(0, 1))))
    grad_depthwise = jnp.stack(tap_grads)
    grad_pre = (grad_act * slope(widened_hidden)).astype(jnp.bfloat16).reshape(tokens, -1)
    grad_expand = jnp.dot(normed_in.reshape(tokens, width).T, grad_pre, preferred_element_type=jnp.float32)
    grad_norm_in = jnp.dot(grad_pre, w_expand.T, preferred_element_type=jnp.float32).reshape(rows, cols, width)
    grad_input = (grad_resid.astype(jnp.float32) + norm_back(inputs, grad_norm_in)).astype(jnp.bfloat16)
    return (block_output, grad_input, (grad_expand, grad_depthwise, grad_project, grad_qkv, grad_outproj))

def reference(block_input, w_expand, w_depthwise, w_project, w_qkv, w_out, grad_out):
    outputs = []
    inputs_grads = []
    totals = None
    for image in range(block_input.shape[0]):
        result = single_image(block_input[image], w_expand, w_depthwise, w_project, w_qkv, w_out, grad_out[image])
        outputs.append(result[0])
        inputs_grads.append(result[1])
        if totals is None:
            totals = result[2]
        else:
            totals = tuple((left + right for left, right in zip(totals, result[2])))
    return (jnp.stack(outputs), jnp.stack(inputs_grads), totals[0], totals[1], totals[2], totals[3], totals[4])
```

```python
import functools
import itertools

import jax
import jax.numpy as jnp
from jax import lax
from jax.experimental import pallas as pl
from jax.experimental.pallas import tpu as pltpu
from jax.sharding import PartitionSpec as P

HEADS = 16
HDIM = 32
EPS = 1e-05
BF = jnp.bfloat16
F32 = jnp.float32
AX = ("row", "col")
WIDE = 40
CHUNK = 256

SIZES = dict(y_lo=2, z=4, core=2, x=4, y_hi=2)
STRIDES = dict(y_lo=64, z=16, core=8, x=2, y_hi=1)
CHIPS = ("y_lo", "z", "x", "y_hi")


def device_groups(axes):
    rest = [a for a in SIZES if a not in axes]
    found = []
    for at in itertools.product(*[range(SIZES[a]) for a in rest]):
        base = sum(v * STRIDES[a] for v, a in zip(at, rest))
        found.append(
            [
                base + sum(v * STRIDES[a] for v, a in zip(m, axes))
                for m in itertools.product(*[range(SIZES[a]) for a in axes])
            ]
        )
    return found


def other_core():
    return [(d, d ^ STRIDES["core"]) for d in range(128)]


def across_chips(x):
    return lax.all_to_all(x, AX, 0, 0, tiled=True, axis_index_groups=device_groups(CHIPS))


def shift(x, axis, step):
    n = lax.axis_size(axis)
    pairs = [(i, i + step) for i in range(n) if 0 <= i + step < n]
    return lax.ppermute(x, axis, pairs)


def halo(x, width):
    rows, cols, chans = x.shape
    above = shift(x[rows - width :], "row", 1)
    below = shift(x[:width], "row", -1)
    to_right = jnp.concatenate(
        [above[:, cols - width :], x[:, cols - width :], below[:, cols - width :]], 0
    )
    to_left = jnp.concatenate([above[:, :width], x[:, :width], below[:, :width]], 0)
    left = shift(to_right, "col", 1)
    right = shift(to_left, "col", -1)
    flat = lambda v: v.reshape(-1, chans)
    return flat(above), flat(below), flat(left), flat(right)


def place_halo(wide, centre, above, below, left, right, width, rows, cols):
    wide[...] = jnp.zeros(wide.shape, wide.dtype)
    wide[width : width + rows, 0:cols, :] = centre.reshape(rows, cols, -1)
    wide[0:width, 0:cols, :] = above.reshape(width, cols, -1)
    wide[width + rows :, 0:cols, :] = below.reshape(width, cols, -1)
    for r in range(rows + 2 * width):
        wide[r, WIDE - width :, :] = left[r * width : (r + 1) * width]
        wide[r, cols : cols + width, :] = right[r * width : (r + 1) * width]


def normalize(x):
    center = x - jnp.mean(x, -1, keepdims=True)
    ratio = lax.rsqrt(jnp.mean(center * center, -1, keepdims=True) + EPS)
    return center * ratio, ratio


def normalize_back(x, grad):
    scaled, ratio = normalize(x)
    return (
        grad
        - jnp.mean(grad, -1, keepdims=True)
        - scaled * jnp.mean(grad * scaled, -1, keepdims=True)
    ) * ratio


A0 = 0.7978845608028654
A1 = A0 * 0.044715


def gelu_parts(x):
    sq = x * x
    t = jnp.tanh(x * (A0 + A1 * sq))
    half = 0.5 + 0.5 * t
    slope = half + (0.5 * x) * ((1.0 - t * t) * (A0 + (3.0 * A1) * sq))
    return x * half, slope


def dot(a, b):
    return jnp.dot(a, b, preferred_element_type=F32)


def dot_nt(a, b):
    return lax.dot_general(a, b, (((1,), (1,)), ((), ())), preferred_element_type=F32)


def dot_tn(a, b):
    return lax.dot_general(a, b, (((0,), (0,)), ((), ())), preferred_element_type=F32)


def roll(x, by):
    return pltpu.roll(x, by % x.shape[0], 0)


def forward_kernel(
    x_ref, above_ref, below_ref, left_ref, right_ref, go_ref, we_ref, wd_ref, wp_ref,
    act_out, slope_c_out, slope_e_out, mid_out, resid_out, send_out,
    wide, normed, pre, act, slope_c, acc,
):
    step = pl.program_id(0)
    rows, cols = 16, 32

    @pl.when(step == 0)
    def _():
        place_halo(
            wide,
            x_ref[...].astype(F32), above_ref[...].astype(F32), below_ref[...].astype(F32),
            left_ref[...].astype(F32), right_ref[...].astype(F32), 2, rows, cols,
        )
        normed[...] = normalize(wide[...].reshape(-1, wide.shape[-1]))[0].astype(BF)
        acc[...] = jnp.zeros(acc.shape, F32)

    pre[...] = dot(normed[...], we_ref[...]).reshape(pre.shape)

    def expand_row(r, _):
        g, s = gelu_parts(pre[r])
        act[r] = g.astype(BF).astype(F32)
        pre[r] = s
        return 0

    lax.fori_loop(0, rows + 4, expand_row, 0)
    slope_e_out[...] = pre[2 : 2 + rows, 0:cols, :].astype(BF)
    act_out[...] = act[1 : rows + 3].reshape(act_out.shape).astype(BF)
    taps = [wd_ref[k : k + 1, :].astype(F32) for k in range(9)]

    def conv_row(r, _):
        lines = [act[r], act[r + 1], act[r + 2]]
        sums = [sum(lines[i] * taps[3 * i + j] for i in range(3)) for j in range(3)]
        conv = sums[1] + roll(sums[0], 1) + roll(sums[2], -1)
        g, s = gelu_parts(conv)
        slope_c[r] = s
        pre[r] = g
        return 0

    lax.fori_loop(0, rows + 2, conv_row, 0)
    slope_c_out[...] = slope_c[...].reshape(slope_c_out.shape).astype(BF)
    mid = pre[1 : 1 + rows, 0:cols, :].reshape(rows * cols, -1).astype(BF)
    mid_out[...] = mid
    acc[...] += dot(mid, wp_ref[...])

    @pl.when(step == pl.num_programs(0) - 1)
    def _():
        resid = (x_ref[...].astype(F32) + acc[...]).astype(BF)
        resid_out[...] = resid
        width = resid.shape[1]
        send_out[:, 0:width] = normalize(resid.astype(F32))[0].astype(BF)
        send_out[:, width:] = go_ref[...]


def forward_block(x, strips, go, w_expand, w_depthwise, w_project):
    tokens, width = x.shape
    hid = w_expand.shape[1]
    rows, cols = 16, 32
    whole = lambda a: pl.BlockSpec(a.shape, lambda j: (0,) * a.ndim)
    return pl.pallas_call(
        forward_kernel,
        name="mbconv_forward",
        grid=(hid // CHUNK,),
        in_specs=[
            whole(x), *[whole(s) for s in strips], whole(go),
            pl.BlockSpec((width, CHUNK), lambda j: (0, j)),
            pl.BlockSpec((9, CHUNK), lambda j: (0, j)),
            pl.BlockSpec((CHUNK, width), lambda j: (j, 0)),
        ],
        out_specs=[
            pl.BlockSpec(((rows + 2) * WIDE, CHUNK), lambda j: (0, j)),
            pl.BlockSpec(((rows + 2) * WIDE, CHUNK), lambda j: (0, j)),
            pl.BlockSpec((rows, cols, CHUNK), lambda j: (0, 0, j)),
            pl.BlockSpec((tokens, CHUNK), lambda j: (0, j)),
            pl.BlockSpec((tokens, width), lambda j: (0, 0)),
            pl.BlockSpec((tokens, 2 * width), lambda j: (0, 0)),
        ],
        out_shape=[
            jax.ShapeDtypeStruct(((rows + 2) * WIDE, hid), BF),
            jax.ShapeDtypeStruct(((rows + 2) * WIDE, hid), BF),
            jax.ShapeDtypeStruct((rows, cols, hid), BF),
            jax.ShapeDtypeStruct((tokens, hid), BF),
            jax.ShapeDtypeStruct((tokens, width), BF),
            jax.ShapeDtypeStruct((tokens, 2 * width), BF),
        ],
        scratch_shapes=[
            pltpu.VMEM((rows + 4, WIDE, width), F32),
            pltpu.VMEM(((rows + 4) * WIDE, width), BF),
            pltpu.VMEM((rows + 4, WIDE, CHUNK), F32),
            pltpu.VMEM((rows + 4, WIDE, CHUNK), F32),
            pltpu.VMEM((rows + 2, WIDE, CHUNK), F32),
            pltpu.VMEM((tokens, width), F32),
        ],
        compiler_params=pltpu.CompilerParams(vmem_limit_bytes=48 * 2**20),
        cost_estimate=pl.CostEstimate(
            flops=2 * (800 + 512) * 512 * 2048, bytes_accessed=20 * 2**20, transcendentals=3 * 2**20
        ),
    )(x, *strips, go, w_expand, w_depthwise, w_project)


def attention_kernel(in_ref, wq_ref, wo_ref, send_out, gq_out, att_out, qkv, gatt, att, gq):
    width = wo_ref.shape[0]
    groups = 8
    members = in_ref.shape[0] // groups
    scale = HDIM ** (-0.5)
    quads = width // 128

    def put(ref, at, value):
        value = value.astype(BF).astype(F32)
        for quad in range(quads):
            ref[at + quad] = value[:, quad * 128 : (quad + 1) * 128]

    for part in range(3):
        lanes = slice(part * width, (part + 1) * width)
        put(qkv, part * quads, dot(in_ref[:, 0:width], wq_ref[:, lanes]))
    put(gatt, 0, dot_nt(in_ref[:, width:], wo_ref[...]))
    per = 128 // HDIM
    head = lax.broadcasted_iota(jnp.int32, (members, 128), 1) // HDIM

    def spread(v):
        return jnp.concatenate([jnp.where(head == h, v, 0.0) for h in range(per)], 0).astype(BF)

    def gather(v):
        out = jnp.where(head == 0, v[0:members], 0.0)
        for h in range(1, per):
            out = jnp.where(head == h, v[h * members : (h + 1) * members], out)
        return out

    def one_group(g, _):
        at = pl.ds(g, members, stride=groups)
        for quad in range(quads):
            q = qkv[quad, at, :]
            k = qkv[quads + quad, at, :].astype(BF)
            v = qkv[2 * quads + quad, at, :].astype(BF)
            do = gatt[quad, at, :]
            qs, dos = spread(q), spread(do)
            scores = dot_nt(k, qs) * scale
            dp = dot_nt(v, dos)
            p = jnp.exp(scores - jnp.max(scores, 0, keepdims=True))
            p = p / jnp.sum(p, 0, keepdims=True)
            pb = p.astype(BF)
            ds = (p * (dp - jnp.sum(p * dp, 0, keepdims=True)) * scale).astype(BF)
            att[quad, at, :] = gather(dot_tn(pb, v))
            gq[quad, at, :] = gather(dot_tn(ds, k))
            gq[quads + quad, at, :] = dot(ds, qs)
            gq[2 * quads + quad, at, :] = dot(pb, dos)
        return 0

    lax.fori_loop(0, groups, one_group, 0)
    attended = jnp.concatenate([att[i] for i in range(quads)], 1).astype(BF)
    att_out[...] = attended
    send_out[:, 0:width] = dot(attended, wo_ref[...]).astype(BF)
    gqb = jnp.concatenate([gq[i] for i in range(3 * quads)], 1).astype(BF)
    gq_out[...] = gqb
    send_out[:, width:] = dot_nt(gqb, wq_ref[...]).astype(BF)


def attention_block(arrived, w_qkv, w_out):
    tokens = arrived.shape[0]
    width = w_out.shape[0]
    return pl.pallas_call(
        attention_kernel,
        name="grid_attention",
        out_shape=[
            jax.ShapeDtypeStruct((tokens, 2 * width), BF),
            jax.ShapeDtypeStruct((tokens, 3 * width), BF),
            jax.ShapeDtypeStruct((tokens, width), BF),
        ],
        scratch_shapes=[
            pltpu.VMEM((3 * width // 128, tokens, 128), F32),
            pltpu.VMEM((width // 128, tokens, 128), F32),
            pltpu.VMEM((width // 128, tokens, 128), F32),
            pltpu.VMEM((3 * width // 128, tokens, 128), F32),
        ],
        compiler_params=pltpu.CompilerParams(vmem_limit_bytes=48 * 2**20),
        cost_estimate=pl.CostEstimate(
            flops=2 * 512 * 512 * 512 * 8, bytes_accessed=7 * 2**20, transcendentals=2**20
        ),
    )(arrived, w_qkv, w_out)


def residual_kernel(home_ref, resid_ref, go_ref, out_ref, gr_ref):
    width = resid_ref.shape[1]
    resid = resid_ref[...].astype(F32)
    out_ref[...] = (resid + home_ref[:, 0:width].astype(F32)).astype(BF)
    back = normalize_back(resid, home_ref[:, width:].astype(F32))
    gr_ref[...] = (go_ref[...].astype(F32) + back).astype(BF)


def residual_block(home, resid, go):
    return pl.pallas_call(
        residual_kernel,
        name="residual",
        out_shape=[jax.ShapeDtypeStruct(resid.shape, BF)] * 2,
        compiler_params=pltpu.CompilerParams(vmem_limit_bytes=48 * 2**20),
    )(home, resid, go)


def backward_kernel(
    x_ref, gr_ref, above_ref, below_ref, left_ref, right_ref, act_ref, slope_c_ref, slope_e_ref,
    we_ref, wd_ref, wp_ref,
    gx_out, ge_out, gd_out,
    wide, grad_wide, normed, gmid, act, gpre, acc,
):
    step = pl.program_id(0)
    rows, cols = 16, 32

    @pl.when(step == 0)
    def _():
        place_halo(
            wide,
            gr_ref[...].astype(F32), above_ref[...].astype(F32), below_ref[...].astype(F32),
            left_ref[...].astype(F32), right_ref[...].astype(F32), 1, rows, cols,
        )
        grad_wide[...] = wide[...].reshape(grad_wide.shape).astype(BF)
        normed[...] = normalize(x_ref[...].astype(F32))[0].astype(BF)
        acc[...] = jnp.zeros(acc.shape, F32)

    gm = dot_nt(grad_wide[...], wp_ref[...]) * slope_c_ref[...].astype(F32)
    gmid[...] = gm.astype(BF).astype(F32).reshape(gmid.shape)
    act[...] = act_ref[...].astype(F32).reshape(act.shape)
    taps = [wd_ref[k : k + 1, :].astype(F32) for k in range(9)]
    lanes = wd_ref.shape[1]
    inside = lax.broadcasted_iota(jnp.int32, (WIDE, lanes), 0) < cols

    def one_row(r, sums):
        lines = [gmid[r + 2], gmid[r + 1], gmid[r]]
        parts = [sum(lines[i] * taps[3 * i + j] for i in range(3)) for j in range(3)]
        grad_act = parts[1] + roll(parts[0], -1) + roll(parts[2], 1)
        gpre[r] = (grad_act[0:cols] * slope_e_ref[r].astype(F32)).astype(BF)
        own = jnp.where(inside, lines[1], 0.0)
        moved = [roll(own, -1), own, roll(own, 1)]
        new = []
        for i in range(3):
            line = act[r + i]
            for j in range(3):
                prod = (line * moved[j]).reshape(WIDE // 8, 8, lanes)
                new.append(sums[3 * i + j] + jnp.sum(prod, 0))
        return tuple(new)

    zero = jnp.zeros((8, lanes), F32)
    sums = lax.fori_loop(0, rows, one_row, (zero,) * 9)
    gd_out[...] = jnp.zeros(gd_out.shape, F32)
    for k in range(9):
        gd_out[k : k + 1, :] = jnp.sum(sums[k], 0, keepdims=True)
    gp = gpre[...].reshape(rows * cols, lanes)
    ge_out[...] = dot_tn(gp, normed[...]).astype(BF)
    acc[...] += dot_nt(gp, we_ref[...])

    @pl.when(step == pl.num_programs(0) - 1)
    def _():
        back = normalize_back(x_ref[...].astype(F32), acc[...])
        gx_out[...] = (gr_ref[...].astype(F32) + back).astype(BF)


def backward_block(x, gr, strips, act, slope_c, slope_e, w_expand, w_depthwise, w_project):
    tokens, width = x.shape
    hid = w_expand.shape[1]
    rows, cols = 16, 32
    whole = lambda a: pl.BlockSpec(a.shape, lambda j: (0,) * a.ndim)
    return pl.pallas_call(
        backward_kernel,
        name="mbconv_backward",
        grid=(hid // CHUNK,),
        in_specs=[
            whole(x), whole(gr), *[whole(s) for s in strips],
            pl.BlockSpec(((rows + 2) * WIDE, CHUNK), lambda j: (0, j)),
            pl.BlockSpec(((rows + 2) * WIDE, CHUNK), lambda j: (0, j)),
            pl.BlockSpec((rows, cols, CHUNK), lambda j: (0, 0, j)),
            pl.BlockSpec((width, CHUNK), lambda j: (0, j)),
            pl.BlockSpec((9, CHUNK), lambda j: (0, j)),
            pl.BlockSpec((CHUNK, width), lambda j: (j, 0)),
        ],
        out_specs=[
            pl.BlockSpec((tokens, width), lambda j: (0, 0)),
            pl.BlockSpec((CHUNK, width), lambda j: (j, 0)),
            pl.BlockSpec((16, CHUNK), lambda j: (0, j)),
        ],
        out_shape=[
            jax.ShapeDtypeStruct((tokens, width), BF),
            jax.ShapeDtypeStruct((hid, width), BF),
            jax.ShapeDtypeStruct((16, hid), F32),
        ],
        scratch_shapes=[
            pltpu.VMEM((rows + 2, WIDE, width), F32),
            pltpu.VMEM(((rows + 2) * WIDE, width), BF),
            pltpu.VMEM((tokens, width), BF),
            pltpu.VMEM((rows + 2, WIDE, CHUNK), F32),
            pltpu.VMEM((rows + 2, WIDE, CHUNK), F32),
            pltpu.VMEM((rows, cols, CHUNK), BF),
            pltpu.VMEM((tokens, width), F32),
        ],
        compiler_params=pltpu.CompilerParams(vmem_limit_bytes=48 * 2**20),
        cost_estimate=pl.CostEstimate(
            flops=2 * (720 + 1024) * 512 * 2048, bytes_accessed=20 * 2**20, transcendentals=2**20
        ),
    )(x, gr, *strips, act, slope_c, slope_e, w_expand, w_depthwise, w_project)


def sum_to_owners(parts):
    rows, chans = parts.shape[1:]
    mine = lax.axis_index("row") % 2
    by_core = parts.reshape(8, 2, 8, rows, chans)
    kept = lax.dynamic_index_in_dim(by_core, mine, 1, keepdims=False)
    sent = lax.dynamic_index_in_dim(by_core, 1 - mine, 1, keepdims=False)
    got = lax.ppermute(sent, AX, other_core())
    pair = (kept.astype(F32) + got.astype(F32)).astype(BF).reshape(64, rows, chans)
    return jnp.sum(across_chips(pair).astype(F32), 0)


def body(block_input, w_expand, w_depthwise, w_project, w_qkv, w_out, grad_out):
    _, rows, cols, width = block_input.shape
    hid = w_expand.shape[1]
    tokens = rows * cols
    image = block_input[0]
    x = image.reshape(tokens, width)
    go = grad_out[0].reshape(tokens, width)
    act, slope_c, slope_e, mid, resid, send = forward_block(
        x, halo(image, 2), go, w_expand, w_depthwise, w_project
    )
    arrived = across_chips(send.reshape(64, 8, 2 * width)).reshape(tokens, 2 * width)
    back, gqkv, attended = attention_block(arrived, w_qkv, w_out)
    home = across_chips(back.reshape(64, 8, 2 * width)).reshape(tokens, 2 * width)
    grad_qkv = dot_tn(gqkv, arrived[:, :width]).astype(BF)
    grad_outproj = dot_tn(arrived[:, width:], attended).astype(BF)
    out, gr = residual_block(home, resid, go)
    grad_project = dot_tn(mid, gr).astype(BF)
    first = sum_to_owners(
        jnp.concatenate(
            [
                grad_project.reshape(128, -1, width),
                grad_qkv.reshape(128, -1, width),
                grad_outproj.reshape(128, -1, width),
            ],
            1,
        )
    )
    gx, grad_expand, grad_depth = backward_block(
        x, gr, halo(gr.reshape(rows, cols, width), 1), act, slope_c, slope_e,
        w_expand, w_depthwise, w_project,
    )
    depth = grad_depth.reshape(16, 128, 16).transpose(1, 0, 2).reshape(128, 1, 256)
    depth = jnp.pad(depth, ((0, 0), (0, 0), (0, width - 256))).astype(BF)
    second = sum_to_owners(jnp.concatenate([grad_expand.reshape(128, -1, width), depth], 1))
    own = hid // 128
    return (
        out.reshape(1, rows, cols, width),
        gx.reshape(1, rows, cols, width),
        second[:own].T,
        second[own, :256].reshape(16, 16)[:9],
        first[:own].T,
        first[own : own + 12].T,
        first[own + 12 :].T,
    )


def solution(mesh):
    tokens = P(None, "row", "col", None)
    split = P(None, AX)
    return jax.shard_map(
        body,
        mesh=mesh,
        in_specs=(tokens, P(), P(), P(), P(), P(), tokens),
        out_specs=(tokens, tokens, split, split, split, split, split),
        check_vma=False,
    )
```

```python
import functools
import itertools

import jax
import jax.numpy as jnp
from jax import lax
from jax.experimental import pallas as pl
from jax.experimental.pallas import tpu as pltpu
from jax.sharding import PartitionSpec as P

HEADS = 16
HDIM = 32
EPS = 1e-05
BF = jnp.bfloat16
F32 = jnp.float32
AX = ("row", "col")
WIDE = 40
CHUNK = 256

SIZES = dict(y_lo=2, z=4, core=2, x=4, y_hi=2)
STRIDES = dict(y_lo=64, z=16, core=8, x=2, y_hi=1)
CHIPS = ("y_lo", "z", "x", "y_hi")


def device_groups(axes):
    rest = [a for a in SIZES if a not in axes]
    found = []
    for at in itertools.product(*[range(SIZES[a]) for a in rest]):
        base = sum(v * STRIDES[a] for v, a in zip(at, rest))
        found.append(
            [
                base + sum(v * STRIDES[a] for v, a in zip(m, axes))
                for m in itertools.product(*[range(SIZES[a]) for a in axes])
            ]
        )
    return found


def other_core():
    return [(d, d ^ STRIDES["core"]) for d in range(128)]


def across_chips(x):
    return lax.all_to_all(x, AX, 0, 0, tiled=True, axis_index_groups=device_groups(CHIPS))


def shift(x, axis, step):
    n = lax.axis_size(axis)
    pairs = [(i, i + step) for i in range(n) if 0 <= i + step < n]
    return lax.ppermute(x, axis, pairs)


def halo(x, width):
    rows, cols, chans = x.shape
    above = shift(x[rows - width :], "row", 1)
    below = shift(x[:width], "row", -1)
    to_right = jnp.concatenate(
        [above[:, cols - width :], x[:, cols - width :], below[:, cols - width :]], 0
    )
    to_left = jnp.concatenate([above[:, :width], x[:, :width], below[:, :width]], 0)
    left = shift(to_right, "col", 1)
    right = shift(to_left, "col", -1)
    gap = jnp.zeros((rows + 2 * width, 8 - 2 * width, chans), x.dtype)
    sides = jnp.concatenate([right, gap, left], 1)
    flat = [v.reshape(-1, chans) for v in (above, below, sides)]
    return jnp.concatenate(flat, 0)


def place(wide, centre, strips, width, rows, cols):
    lanes = centre.shape[-1]
    n = width * cols
    wide[width : width + rows, 0:cols, :] = centre.reshape(rows, cols, lanes)
    wide[0:width, 0:cols, :] = strips[0:n].reshape(width, cols, lanes)
    wide[width + rows :, 0:cols, :] = strips[n : 2 * n].reshape(width, cols, lanes)
    wide[:, cols:, :] = strips[2 * n :].reshape(rows + 2 * width, WIDE - cols, lanes)


def normalize(x):
    center = x - jnp.mean(x, -1, keepdims=True)
    ratio = lax.rsqrt(jnp.mean(center * center, -1, keepdims=True) + EPS)
    return center * ratio, ratio


def normalize_back(x, grad):
    scaled, ratio = normalize(x)
    return (
        grad
        - jnp.mean(grad, -1, keepdims=True)
        - scaled * jnp.mean(grad * scaled, -1, keepdims=True)
    ) * ratio


A0 = 0.7978845608028654
A1 = A0 * 0.044715


def gelu_parts(x):
    inner = A0 + A1 * (x * x)
    half = 0.5 + 0.5 * jnp.tanh(x * inner)
    value = x * half
    return value, half + (value - value * half) * (6.0 * inner - 4.0 * A0)


def dot(a, b):
    return jnp.dot(a, b, preferred_element_type=F32)


def dot_nt(a, b):
    return lax.dot_general(a, b, (((1,), (1,)), ((), ())), preferred_element_type=F32)


def dot_tn(a, b):
    return lax.dot_general(a, b, (((0,), (0,)), ((), ())), preferred_element_type=F32)


def roll(x, by):
    return pltpu.roll(x, by % x.shape[0], 0)


def expand_kernel(x_ref, we_ref, act_out, slope_out, normed):
    @pl.when(pl.program_id(0) == 0)
    def _():
        normed[...] = normalize(x_ref[...].astype(F32))[0].astype(BF)

    for tile in range(0, x_ref.shape[0], 128):
        value, slope = gelu_parts(dot(normed[tile : tile + 128, :], we_ref[...]))
        act_out[tile : tile + 128, :] = value.astype(BF)
        slope_out[tile : tile + 128, :] = slope.astype(BF)


def expand_block(x, w_expand):
    tokens, width = x.shape
    hid = w_expand.shape[1]
    lanes = 512
    return pl.pallas_call(
        expand_kernel,
        name="expand",
        grid=(hid // lanes,),
        in_specs=[
            pl.BlockSpec((tokens, width), lambda j: (0, 0)),
            pl.BlockSpec((width, lanes), lambda j: (0, j)),
        ],
        out_specs=[pl.BlockSpec((tokens, lanes), lambda j: (0, j))] * 2,
        out_shape=[jax.ShapeDtypeStruct((tokens, hid), BF)] * 2,
        scratch_shapes=[pltpu.VMEM((tokens, width), BF)],
        compiler_params=pltpu.CompilerParams(vmem_limit_bytes=48 * 2**20),
        cost_estimate=pl.CostEstimate(
            flops=16 * 512 * 512 * 2048, bytes_accessed=8 * 2**20, transcendentals=2**20
        ),
    )(x, w_expand)


def forward_kernel(
    x_ref, strips_ref, go_ref, act_ref, we_ref, wd_ref, wp_ref,
    act_out, slope_out, mid_out, resid_out, send_out,
    normed, act, acc,
):
    step = pl.program_id(0)
    rows, cols = 16, 32

    @pl.when(step == 0)
    def _():
        normed[...] = normalize(strips_ref[...].astype(F32))[0].astype(BF)
        acc[...] = jnp.zeros(acc.shape, F32)

    strips = jax.nn.gelu(dot(normed[...], we_ref[...])).astype(BF).astype(F32)
    place(act, act_ref[...].astype(F32), strips, 2, rows, cols)
    act_out[...] = act[1 : rows + 3].reshape(act_out.shape).astype(BF)
    for lo in range(0, CHUNK, 128):
        lanes = slice(lo, lo + 128)
        taps = [wd_ref[k : k + 1, lanes].astype(F32) for k in range(9)]
        lines = [act[0, :, lanes], act[1, :, lanes]]
        held = None
        for r in range(rows + 2):
            lines = lines[-2:] + [act[r + 2, :, lanes]]
            sums = [sum(lines[i] * taps[3 * i + j] for i in range(3)) for j in range(3)]
            value, slope = gelu_parts(sums[1] + roll(sums[0], 1) + roll(sums[2], -1))
            if 1 <= r <= rows:
                mid_out[(r - 1) * cols : r * cols, lanes] = value[0:cols].astype(BF)
            if r % 2:
                pair = jnp.concatenate([held, slope], 0).astype(BF)
                slope_out[(r - 1) * WIDE : (r + 1) * WIDE, lanes] = pair
            held = slope
    acc[...] += dot(mid_out[...], wp_ref[...])

    @pl.when(step == pl.num_programs(0) - 1)
    def _():
        resid = (x_ref[...].astype(F32) + acc[...]).astype(BF)
        resid_out[...] = resid
        width = resid.shape[1]
        send_out[:, 0:width] = normalize(resid.astype(F32))[0].astype(BF)
        send_out[:, width:] = go_ref[...]


def forward_block(x, strips, go, act, w_expand, w_depthwise, w_project):
    tokens, width = x.shape
    hid = w_expand.shape[1]
    rows, cols = 16, 32
    whole = lambda a: pl.BlockSpec(a.shape, lambda j: (0,) * a.ndim)
    return pl.pallas_call(
        forward_kernel,
        name="mbconv_forward",
        grid=(hid // CHUNK,),
        in_specs=[
            whole(x), whole(strips), whole(go),
            pl.BlockSpec((tokens, CHUNK), lambda j: (0, j)),
            pl.BlockSpec((width, CHUNK), lambda j: (0, j)),
            pl.BlockSpec((9, CHUNK), lambda j: (0, j)),
            pl.BlockSpec((CHUNK, width), lambda j: (j, 0)),
        ],
        out_specs=[
            pl.BlockSpec(((rows + 2) * WIDE, CHUNK), lambda j: (0, j)),
            pl.BlockSpec(((rows + 2) * WIDE, CHUNK), lambda j: (0, j)),
            pl.BlockSpec((tokens, CHUNK), lambda j: (0, j)),
            pl.BlockSpec((tokens, width), lambda j: (0, 0)),
            pl.BlockSpec((tokens, 2 * width), lambda j: (0, 0)),
        ],
        out_shape=[
            jax.ShapeDtypeStruct(((rows + 2) * WIDE, hid), BF),
            jax.ShapeDtypeStruct(((rows + 2) * WIDE, hid), BF),
            jax.ShapeDtypeStruct((tokens, hid), BF),
            jax.ShapeDtypeStruct((tokens, width), BF),
            jax.ShapeDtypeStruct((tokens, 2 * width), BF),
        ],
        scratch_shapes=[
            pltpu.VMEM(strips.shape, BF),
            pltpu.VMEM((rows + 4, WIDE, CHUNK), F32),
            pltpu.VMEM((tokens, width), F32),
        ],
        compiler_params=pltpu.CompilerParams(vmem_limit_bytes=48 * 2**20),
        cost_estimate=pl.CostEstimate(
            flops=2 * (800 + 512) * 512 * 2048, bytes_accessed=20 * 2**20, transcendentals=3 * 2**20
        ),
    )(x, strips, go, act, w_expand, w_depthwise, w_project)


def attention_kernel(in_ref, wq_ref, wo_ref, send_out, gq_out, att_out, qkv, gatt, att, gq):
    width = wo_ref.shape[0]
    groups = 8
    members = in_ref.shape[0] // groups
    scale = HDIM ** (-0.5)
    quads = width // 128

    def put(ref, at, value):
        value = value.astype(BF).astype(F32)
        for quad in range(quads):
            ref[at + quad] = value[:, quad * 128 : (quad + 1) * 128]

    for part in range(3):
        lanes = slice(part * width, (part + 1) * width)
        put(qkv, part * quads, dot(in_ref[:, 0:width], wq_ref[:, lanes]))
    put(gatt, 0, dot_nt(in_ref[:, width:], wo_ref[...]))
    per = 128 // HDIM
    head = lax.broadcasted_iota(jnp.int32, (members, 128), 1) // HDIM

    def spread(v):
        return jnp.concatenate([jnp.where(head == h, v, 0.0) for h in range(per)], 0).astype(BF)

    def gather(v):
        out = jnp.where(head == 0, v[0:members], 0.0)
        for h in range(1, per):
            out = jnp.where(head == h, v[h * members : (h + 1) * members], out)
        return out

    def one_group(g, _):
        at = pl.ds(g, members, stride=groups)
        for quad in range(quads):
            q = qkv[quad, at, :]
            k = qkv[quads + quad, at, :].astype(BF)
            v = qkv[2 * quads + quad, at, :].astype(BF)
            do = gatt[quad, at, :]
            qs, dos = spread(q), spread(do)
            scores = dot_nt(k, qs) * scale
            dp = dot_nt(v, dos)
            p = jnp.exp(scores - jnp.max(scores, 0, keepdims=True))
            p = p / jnp.sum(p, 0, keepdims=True)
            pb = p.astype(BF)
            ds = (p * (dp - jnp.sum(p * dp, 0, keepdims=True)) * scale).astype(BF)
            att[quad, at, :] = gather(dot_tn(pb, v))
            gq[quad, at, :] = gather(dot_tn(ds, k))
            gq[quads + quad, at, :] = dot(ds, qs)
            gq[2 * quads + quad, at, :] = dot(pb, dos)
        return 0

    lax.fori_loop(0, groups, one_group, 0)
    attended = jnp.concatenate([att[i] for i in range(quads)], 1).astype(BF)
    att_out[...] = attended
    send_out[:, 0:width] = dot(attended, wo_ref[...]).astype(BF)
    gqb = jnp.concatenate([gq[i] for i in range(3 * quads)], 1).astype(BF)
    gq_out[...] = gqb
    send_out[:, width:] = dot_nt(gqb, wq_ref[...]).astype(BF)


def attention_block(arrived, w_qkv, w_out):
    tokens = arrived.shape[0]
    width = w_out.shape[0]
    return pl.pallas_call(
        attention_kernel,
        name="grid_attention",
        out_shape=[
            jax.ShapeDtypeStruct((tokens, 2 * width), BF),
            jax.ShapeDtypeStruct((tokens, 3 * width), BF),
            jax.ShapeDtypeStruct((tokens, width), BF),
        ],
        scratch_shapes=[
            pltpu.VMEM((3 * width // 128, tokens, 128), F32),
            pltpu.VMEM((width // 128, tokens, 128), F32),
            pltpu.VMEM((width // 128, tokens, 128), F32),
            pltpu.VMEM((3 * width // 128, tokens, 128), F32),
        ],
        compiler_params=pltpu.CompilerParams(vmem_limit_bytes=48 * 2**20),
        cost_estimate=pl.CostEstimate(
            flops=2 * 512 * 512 * 512 * 8, bytes_accessed=7 * 2**20, transcendentals=2**20
        ),
    )(arrived, w_qkv, w_out)


def residual_kernel(home_ref, resid_ref, go_ref, out_ref, gr_ref):
    width = resid_ref.shape[1]
    resid = resid_ref[...].astype(F32)
    out_ref[...] = (resid + home_ref[:, 0:width].astype(F32)).astype(BF)
    back = normalize_back(resid, home_ref[:, width:].astype(F32))
    gr_ref[...] = (go_ref[...].astype(F32) + back).astype(BF)


def residual_block(home, resid, go):
    return pl.pallas_call(
        residual_kernel,
        name="residual",
        out_shape=[jax.ShapeDtypeStruct(resid.shape, BF)] * 2,
        compiler_params=pltpu.CompilerParams(vmem_limit_bytes=48 * 2**20),
    )(home, resid, go)


def split_by_core(core, full, mine_out, other_out):
    half = full.shape[0] // 2
    own = pl.multiple_of(core * half, half)
    mine_out[...] = full[pl.ds(own, half), :]
    other_out[...] = full[pl.ds(pl.multiple_of(half - own, half), half), :].astype(BF)


def backward_kernel(
    core_ref, x_ref, gr_ref, strips_ref, act_ref, slope_c_ref, slope_e_ref, we_ref, wd_ref, wp_ref,
    gx_out, mine_out, other_out,
    wide, grad_wide, normed, gmid, act, gpre, full, taps_t, acc,
):
    step = pl.program_id(0)
    rows, cols = 16, 32
    width = x_ref.shape[1]

    @pl.when(step == 0)
    def _():
        place(wide, gr_ref[...].astype(F32), strips_ref[...].astype(F32), 1, rows, cols)
        grad_wide[...] = wide[...].reshape(grad_wide.shape).astype(BF)
        normed[...] = normalize(x_ref[...].astype(F32))[0].astype(BF)
        acc[...] = jnp.zeros(acc.shape, F32)
        taps_t[...] = jnp.zeros(taps_t.shape, F32)

    gm = dot_nt(grad_wide[...], wp_ref[...]) * slope_c_ref[...].astype(F32)
    gmid[...] = gm.reshape(gmid.shape)
    act[...] = act_ref[...].astype(F32).reshape(act.shape)
    inside = lax.broadcasted_iota(jnp.int32, (WIDE, 128), 0) < cols
    for lo in range(0, CHUNK, 128):
        lanes = slice(lo, lo + 128)
        taps = [wd_ref[k : k + 1, lanes].astype(F32) for k in range(9)]
        sums = [None] * 9
        grads = [gmid[0, :, lanes], gmid[1, :, lanes]]
        acts = [act[0, :, lanes], act[1, :, lanes]]
        for r in range(rows):
            grads = grads[-2:] + [gmid[r + 2, :, lanes]]
            acts = acts[-2:] + [act[r + 2, :, lanes]]
            parts = [sum(grads[2 - i] * taps[3 * i + j] for i in range(3)) for j in range(3)]
            grad_act = parts[1] + roll(parts[0], -1) + roll(parts[2], 1)
            at = slice(r * cols, (r + 1) * cols)
            gpre[at, lanes] = (grad_act[0:cols] * slope_e_ref[at, lanes].astype(F32)).astype(BF)
            own = jnp.where(inside, grads[1], 0.0)
            moved = [roll(own, -1), own, roll(own, 1)]
            for k in range(9):
                prod = jnp.sum((acts[k // 3] * moved[k % 3]).reshape(WIDE // 8, 8, 128), 0)
                sums[k] = prod if r == 0 else sums[k] + prod
        for k in range(9):
            taps_t[k : k + 1, lanes] = jnp.sum(sums[k], 0, keepdims=True)
    full[:, 0:width] = dot_tn(gpre[...], normed[...])
    full[:, width:] = taps_t[...].T
    split_by_core(core_ref[0], full, mine_out, other_out)
    acc[...] += dot_nt(gpre[...], we_ref[...])

    @pl.when(step == pl.num_programs(0) - 1)
    def _():
        back = normalize_back(x_ref[...].astype(F32), acc[...])
        gx_out[...] = (gr_ref[...].astype(F32) + back).astype(BF)


def backward_block(core, x, gr, strips, act, slope_c, slope_e, w_expand, w_depthwise, w_project):
    tokens, width = x.shape
    hid = w_expand.shape[1]
    rows, cols = 16, 32
    whole = lambda a: pl.BlockSpec(a.shape, lambda j, c: (0,) * a.ndim)
    return pl.pallas_call(
        backward_kernel,
        name="mbconv_backward",
        grid_spec=pltpu.PrefetchScalarGridSpec(
            num_scalar_prefetch=1,
            grid=(hid // CHUNK,),
            in_specs=[
                whole(x), whole(gr), whole(strips),
                pl.BlockSpec(((rows + 2) * WIDE, CHUNK), lambda j, c: (0, j)),
                pl.BlockSpec(((rows + 2) * WIDE, CHUNK), lambda j, c: (0, j)),
                pl.BlockSpec((tokens, CHUNK), lambda j, c: (0, j)),
                pl.BlockSpec((width, CHUNK), lambda j, c: (0, j)),
                pl.BlockSpec((9, CHUNK), lambda j, c: (0, j)),
                pl.BlockSpec((CHUNK, width), lambda j, c: (j, 0)),
            ],
            out_specs=[
                pl.BlockSpec((tokens, width), lambda j, c: (0, 0)),
                pl.BlockSpec((CHUNK // 2, width + 128), lambda j, c: (j, 0)),
                pl.BlockSpec((CHUNK // 2, width + 128), lambda j, c: (j, 0)),
            ],
            scratch_shapes=[
                pltpu.VMEM((rows + 2, WIDE, width), F32),
                pltpu.VMEM(((rows + 2) * WIDE, width), BF),
                pltpu.VMEM((tokens, width), BF),
                pltpu.VMEM((rows + 2, WIDE, CHUNK), F32),
                pltpu.VMEM((rows + 2, WIDE, CHUNK), F32),
                pltpu.VMEM((tokens, CHUNK), BF),
                pltpu.VMEM((CHUNK, width + 128), F32),
                pltpu.VMEM((128, CHUNK), F32),
                pltpu.VMEM((tokens, width), F32),
            ],
        ),
        out_shape=[
            jax.ShapeDtypeStruct((tokens, width), BF),
            jax.ShapeDtypeStruct((hid // 2, width + 128), F32),
            jax.ShapeDtypeStruct((hid // 2, width + 128), BF),
        ],
        compiler_params=pltpu.CompilerParams(vmem_limit_bytes=48 * 2**20),
        cost_estimate=pl.CostEstimate(
            flops=16 * 512 * 512 * 2048, bytes_accessed=20 * 2**20, transcendentals=2**20
        ),
    )(core, x, gr, strips, act, slope_c, slope_e, w_expand, w_depthwise, w_project)


def project_kernel(core_ref, mid_ref, gr_ref, mine_out, other_out, full):
    full[...] = dot_tn(mid_ref[...], gr_ref[...])
    split_by_core(core_ref[0], full, mine_out, other_out)


def project_grads(core, mid, gr):
    tokens, hid = mid.shape
    width = gr.shape[1]
    return pl.pallas_call(
        project_kernel,
        name="grad_project",
        grid_spec=pltpu.PrefetchScalarGridSpec(
            num_scalar_prefetch=1,
            grid=(hid // CHUNK,),
            in_specs=[
                pl.BlockSpec((tokens, CHUNK), lambda j, c: (0, j)),
                pl.BlockSpec((tokens, width), lambda j, c: (0, 0)),
            ],
            out_specs=[pl.BlockSpec((CHUNK // 2, width), lambda j, c: (j, 0))] * 2,
            scratch_shapes=[pltpu.VMEM((CHUNK, width), F32)],
        ),
        out_shape=[
            jax.ShapeDtypeStruct((hid // 2, width), F32),
            jax.ShapeDtypeStruct((hid // 2, width), BF),
        ],
        compiler_params=pltpu.CompilerParams(vmem_limit_bytes=48 * 2**20),
        cost_estimate=pl.CostEstimate(
            flops=2 * 512 * 512 * 2048, bytes_accessed=7 * 2**20, transcendentals=0
        ),
    )(core, mid, gr)


def attention_grads_kernel(
    core_ref, arrived_ref, gqkv_ref, att_ref, mine_out, other_out, qkv, outp, half_q, half_o, full
):
    width = att_ref.shape[1]
    qkv[...] = dot_tn(gqkv_ref[...], arrived_ref[:, 0:width])
    outp[...] = dot_tn(arrived_ref[:, width:], att_ref[...])
    nq, no = qkv.shape[0] // 16, outp.shape[0] // 16
    for j in range(8):
        for own in (True, False):
            core = core_ref[0] if own else 1 - core_ref[0]
            half_q[...] = qkv[pl.ds(pl.multiple_of((2 * j + core) * nq, 8), nq), :]
            half_o[...] = outp[pl.ds(pl.multiple_of((2 * j + core) * no, 8), no), :]
            for k in range(8):
                full[16 * k : 16 * k + 12, :] = half_q[12 * k : 12 * k + 12, :]
                full[16 * k + 12 : 16 * k + 16, :] = half_o[4 * k : 4 * k + 4, :]
            at = slice(128 * j, 128 * j + 128)
            if own:
                mine_out[at, :] = full[...]
            else:
                other_out[at, :] = full[...].astype(BF)


def attention_grads(core, arrived, gqkv, attended):
    tokens, width = attended.shape
    vmem = pl.BlockSpec(memory_space=pltpu.VMEM)
    return pl.pallas_call(
        attention_grads_kernel,
        name="attention_grads",
        in_specs=[pl.BlockSpec(memory_space=pltpu.SMEM), vmem, vmem, vmem],
        out_specs=[vmem, vmem],
        out_shape=[
            jax.ShapeDtypeStruct((1024, width), F32),
            jax.ShapeDtypeStruct((1024, width), BF),
        ],
        scratch_shapes=[
            pltpu.VMEM((3 * width, width), F32),
            pltpu.VMEM((width, width), F32),
            pltpu.VMEM((96, width), F32),
            pltpu.VMEM((32, width), F32),
            pltpu.VMEM((128, width), F32),
        ],
        compiler_params=pltpu.CompilerParams(vmem_limit_bytes=48 * 2**20),
        cost_estimate=pl.CostEstimate(
            flops=8 * 512 * 512 * 512, bytes_accessed=8 * 2**20, transcendentals=0
        ),
    )(core, arrived, gqkv, attended)


def add_pair(mine, other):
    got = lax.ppermute(other, AX, other_core())
    return (mine + got.astype(F32)).astype(BF).reshape(64, 16, -1)


def body(block_input, w_expand, w_depthwise, w_project, w_qkv, w_out, grad_out):
    _, rows, cols, width = block_input.shape
    tokens = rows * cols
    core = (lax.axis_index("row") % 2).astype(jnp.int32).reshape(1)
    image = block_input[0]
    x = image.reshape(tokens, width)
    go = grad_out[0].reshape(tokens, width)
    centre, slope_e = expand_block(x, w_expand)
    act, slope_c, mid, resid, send = forward_block(
        x, halo(image, 2), go, centre, w_expand, w_depthwise, w_project
    )
    arrived = across_chips(send.reshape(64, 8, 2 * width)).reshape(tokens, 2 * width)
    back, gqkv, attended = attention_block(arrived, w_qkv, w_out)
    home = across_chips(back.reshape(64, 8, 2 * width)).reshape(tokens, 2 * width)
    attention_pair = add_pair(*attention_grads(core, arrived, gqkv, attended))
    out, gr = residual_block(home, resid, go)
    project_pair = add_pair(*project_grads(core, mid, gr))
    first = jnp.concatenate([project_pair, attention_pair], 1)
    strips = halo(gr.reshape(rows, cols, width), 1)
    strips, first = lax.optimization_barrier((strips, first))
    first = across_chips(first)
    gx, mine, other = backward_block(
        core, x, gr, strips, act, slope_c, slope_e, w_expand, w_depthwise, w_project
    )
    second = add_pair(mine, other)
    second, first = lax.optimization_barrier((second, first))
    second = jnp.sum(across_chips(second).astype(F32), 0)
    first = jnp.sum(first.astype(F32), 0)
    return (
        out.reshape(1, rows, cols, width),
        gx.reshape(1, rows, cols, width),
        second[:, :width].T,
        second[:, width : width + 9].T,
        first[:16].T,
        first[16:28].T,
        first[28:].T,
    )


def solution(mesh):
    tokens = P(None, "row", "col", None)
    split = P(None, AX)
    return jax.shard_map(
        body,
        mesh=mesh,
        in_specs=(tokens, P(), P(), P(), P(), P(), tokens),
        out_specs=(tokens, tokens, split, split, split, split, split),
        check_vma=False,
    )
```

```python
import functools
import itertools

import jax
import jax.numpy as jnp
from jax import lax
from jax.experimental import pallas as pl
from jax.experimental.pallas import tpu as pltpu
from jax.sharding import PartitionSpec as P

HEADS = 16
HDIM = 32
EPS = 1e-05
BF = jnp.bfloat16
F32 = jnp.float32
AX = ("row", "col")
WIDE = 40
CHUNK = 256
MIB = 2**20

SIZES = dict(y_lo=2, z=4, core=2, x=4, y_hi=2)
STRIDES = dict(y_lo=64, z=16, core=8, x=2, y_hi=1)
CHIPS = ("y_lo", "z", "x", "y_hi")


def device_groups(axes):
    rest = [a for a in SIZES if a not in axes]
    found = []
    for at in itertools.product(*[range(SIZES[a]) for a in rest]):
        base = sum(v * STRIDES[a] for v, a in zip(at, rest))
        found.append(
            [
                base + sum(v * STRIDES[a] for v, a in zip(m, axes))
                for m in itertools.product(*[range(SIZES[a]) for a in axes])
            ]
        )
    return found


def other_core():
    return [(d, d ^ STRIDES["core"]) for d in range(128)]


def across_chips(x):
    return lax.all_to_all(x, AX, 0, 0, tiled=True, axis_index_groups=device_groups(CHIPS))


def shift(x, axis, step):
    n = lax.axis_size(axis)
    pairs = [(i, i + step) for i in range(n) if 0 <= i + step < n]
    return lax.ppermute(x, axis, pairs)


def halo(x, width, ahead):
    rows, cols, chans = x.shape
    above = shift(x[rows - width :], "row", 1)
    below = shift(x[:width], "row", -1)
    above, below, _ = lax.optimization_barrier((above, below, ahead))
    to_right = jnp.concatenate(
        [above[:, cols - width :], x[:, cols - width :], below[:, cols - width :]], 0
    )
    to_left = jnp.concatenate([above[:, :width], x[:, :width], below[:, :width]], 0)
    left = shift(to_right, "col", 1)
    right = shift(to_left, "col", -1)
    gap = jnp.zeros((rows + 2 * width, 8 - 2 * width, chans), x.dtype)
    sides = jnp.concatenate([right, gap, left], 1)
    flat = [v.reshape(-1, chans) for v in (above, below, sides)]
    return jnp.concatenate(flat, 0)


def place(wide, centre, strips, width, rows, cols):
    lanes = strips.shape[-1]
    n = width * cols
    if centre is not None:
        wide[width : width + rows, 0:cols, :] = centre.reshape(rows, cols, lanes)
    wide[0:width, 0:cols, :] = strips[0:n].reshape(width, cols, lanes)
    wide[width + rows :, 0:cols, :] = strips[n : 2 * n].reshape(width, cols, lanes)
    wide[:, cols:, :] = strips[2 * n :].reshape(rows + 2 * width, WIDE - cols, lanes)


def normalize(x):
    center = x - jnp.mean(x, -1, keepdims=True)
    ratio = lax.rsqrt(jnp.mean(center * center, -1, keepdims=True) + EPS)
    return center * ratio, ratio


def normalize_back(x, grad):
    scaled, ratio = normalize(x)
    return (
        grad
        - jnp.mean(grad, -1, keepdims=True)
        - scaled * jnp.mean(grad * scaled, -1, keepdims=True)
    ) * ratio


A0 = 0.7978845608028654
A1 = A0 * 0.044715


def gelu_half(x):
    inner = A0 + A1 * (x * x)
    return inner, 0.5 + 0.5 * jnp.tanh(x * inner)


def gelu(x):
    return x * gelu_half(x)[1]


def gelu_slope(x):
    inner, half = gelu_half(x)
    value = x * half
    return half + (value - value * half) * (6.0 * inner - 4.0 * A0)


def dot(a, b):
    return jnp.dot(a, b, preferred_element_type=F32)


def dot_nt(a, b):
    return lax.dot_general(a, b, (((1,), (1,)), ((), ())), preferred_element_type=F32)


def dot_tn(a, b):
    return lax.dot_general(a, b, (((0,), (0,)), ((), ())), preferred_element_type=F32)


def in_hbm(*arrays):
    return [pltpu.with_memory_space_constraint(a, pltpu.HBM) for a in arrays]


def roll(x, by):
    return pltpu.roll(x, by % x.shape[0], 0)


def expand_kernel(x_ref, we_ref, act_out, normed):
    @pl.when(pl.program_id(0) == 0)
    def _():
        normed[...] = normalize(x_ref[...].astype(F32))[0].astype(BF)

    for tile in range(0, x_ref.shape[0], 128):
        at = slice(tile, tile + 128)
        act_out[at, :] = gelu(dot(normed[at, :], we_ref[...])).astype(BF)


def expand_block(x, w_expand, part, parts):
    tokens, width = x.shape
    lanes = 512
    steps = w_expand.shape[1] // lanes // parts
    return pl.pallas_call(
        expand_kernel,
        name="expand",
        grid=(steps,),
        in_specs=[
            pl.BlockSpec((tokens, width), lambda j: (0, 0)),
            pl.BlockSpec((width, lanes), lambda j: (0, j + part * steps)),
        ],
        out_specs=pl.BlockSpec((tokens, lanes), lambda j: (0, j)),
        out_shape=jax.ShapeDtypeStruct((tokens, steps * lanes), BF),
        scratch_shapes=[pltpu.VMEM((tokens, width), BF)],
        compiler_params=pltpu.CompilerParams(vmem_limit_bytes=8 * MIB),
        cost_estimate=pl.CostEstimate(
            flops=8 * 512 * 512 * 2048, bytes_accessed=3 * 2**20, transcendentals=2**19
        ),
    )(*in_hbm(x, w_expand))


def forward_kernel(
    x_ref, strips_ref, go_ref, act0_ref, act1_ref, we_ref, wd_ref, wp_ref,
    mid_out, resid_out, send_out,
    normed, act, acc,
):
    step = pl.program_id(0)
    rows, cols = 16, 32

    @pl.when(step == 0)
    def _():
        every = normalize(strips_ref[...].astype(F32))[0]
        sides = 4 * cols + 8
        near = [every[cols : 3 * cols], every[sides : sides + 8 * (rows + 2)]]
        normed[...] = jnp.concatenate(near, 0).astype(BF)
        acc[...] = jnp.zeros(acc.shape, F32)

    strips = gelu(dot(normed[...], we_ref[...])).astype(BF).astype(F32)
    centre = jnp.where(step < pl.num_programs(0) // 2, act0_ref[...], act1_ref[...])
    place(act, centre.astype(F32), strips, 1, rows, cols)
    for lo in range(0, CHUNK, 128):
        lanes = slice(lo, lo + 128)
        taps = [wd_ref[k : k + 1, lanes].astype(F32) for k in range(9)]
        lines = [act[0, :, lanes], act[1, :, lanes]]
        for r in range(rows):
            lines = lines[-2:] + [act[r + 2, :, lanes]]
            sums = [sum(lines[i] * taps[3 * i + j] for i in range(3)) for j in range(3)]
            conv = sums[1] + roll(sums[0], 1) + roll(sums[2], -1)
            mid_out[r * cols : (r + 1) * cols, lanes] = gelu(conv[0:cols]).astype(BF)
    acc[...] += dot(mid_out[...], wp_ref[...])

    @pl.when(step == pl.num_programs(0) - 1)
    def _():
        resid = (x_ref[...].astype(F32) + acc[...]).astype(BF)
        resid_out[...] = resid
        width = resid.shape[1]
        send_out[:, 0:width] = normalize(resid.astype(F32))[0].astype(BF)
        send_out[:, width:] = go_ref[...]


def forward_block(x, strips, go, act0, act1, w_expand, w_depthwise, w_project):
    tokens, width = x.shape
    hid = w_expand.shape[1]
    rows, cols = 16, 32
    steps = hid // CHUNK
    whole = lambda a: pl.BlockSpec(a.shape, lambda j: (0,) * a.ndim)
    return pl.pallas_call(
        forward_kernel,
        name="mbconv_forward",
        grid=(steps,),
        in_specs=[
            whole(x), whole(strips), whole(go),
            pl.BlockSpec((tokens, CHUNK), lambda j: (0, jnp.minimum(j, steps // 2 - 1))),
            pl.BlockSpec((tokens, CHUNK), lambda j: (0, jnp.maximum(j - steps // 2, 0))),
            pl.BlockSpec((width, CHUNK), lambda j: (0, j)),
            pl.BlockSpec((9, CHUNK), lambda j: (0, j)),
            pl.BlockSpec((CHUNK, width), lambda j: (j, 0)),
        ],
        out_specs=[
            pl.BlockSpec((tokens, CHUNK), lambda j: (0, j)),
            pl.BlockSpec((tokens, width), lambda j: (0, 0)),
            pl.BlockSpec((tokens, 2 * width), lambda j: (0, 0)),
        ],
        out_shape=[
            pltpu.HBM((tokens, hid), BF),
            pltpu.HBM((tokens, width), BF),
            pltpu.HBM((tokens, 2 * width), BF),
        ],
        scratch_shapes=[
            pltpu.VMEM((2 * cols + 8 * (rows + 2), width), BF),
            pltpu.VMEM((rows + 2, WIDE, CHUNK), F32),
            pltpu.VMEM((tokens, width), F32),
        ],
        compiler_params=pltpu.CompilerParams(vmem_limit_bytes=14 * MIB),
        cost_estimate=pl.CostEstimate(
            flops=2 * 700 * 512 * 2048, bytes_accessed=10 * 2**20, transcendentals=2**20
        ),
    )(*in_hbm(x), strips, *in_hbm(go), act0, act1, *in_hbm(w_expand, w_depthwise, w_project))


def slopes_kernel(
    x_ref, strips_ref, we_ref, wd_ref, act_out, slope_c_out, slope_e_out, normed, normed_s, act
):
    rows, cols = 16, 32

    @pl.when(pl.program_id(0) == 0)
    def _():
        normed[...] = normalize(x_ref[...].astype(F32))[0].astype(BF)
        normed_s[...] = normalize(strips_ref[...].astype(F32))[0].astype(BF)

    for tile in range(0, x_ref.shape[0], 128):
        at = slice(tile, tile + 128)
        pre = dot(normed[at, :], we_ref[...])
        slope_e_out[at, :] = gelu_slope(pre).astype(BF)
        act[2 + tile // cols : 2 + (tile + 128) // cols, 0:cols, :] = (
            gelu(pre).astype(BF).astype(F32).reshape(128 // cols, cols, CHUNK)
        )
    strips = gelu(dot(normed_s[...], we_ref[...])).astype(BF).astype(F32)
    place(act, None, strips, 2, rows, cols)
    act_out[...] = act[1 : rows + 3].reshape(act_out.shape).astype(BF)
    for lo in range(0, CHUNK, 128):
        lanes = slice(lo, lo + 128)
        taps = [wd_ref[k : k + 1, lanes].astype(F32) for k in range(9)]
        lines = [act[0, :, lanes], act[1, :, lanes]]
        held = None
        for r in range(rows + 2):
            lines = lines[-2:] + [act[r + 2, :, lanes]]
            sums = [sum(lines[i] * taps[3 * i + j] for i in range(3)) for j in range(3)]
            slope = gelu_slope(sums[1] + roll(sums[0], 1) + roll(sums[2], -1))
            if r % 2:
                pair = jnp.concatenate([held, slope], 0).astype(BF)
                slope_c_out[(r - 1) * WIDE : (r + 1) * WIDE, lanes] = pair
            held = slope


def slopes_block(x, strips, w_expand, w_depthwise):
    tokens, width = x.shape
    hid = w_expand.shape[1]
    rows, cols = 16, 32
    wide = (rows + 2) * WIDE
    whole = lambda a: pl.BlockSpec(a.shape, lambda j: (0,) * a.ndim)
    return pl.pallas_call(
        slopes_kernel,
        name="gelu_slopes",
        grid=(hid // CHUNK,),
        in_specs=[
            whole(x), whole(strips),
            pl.BlockSpec((width, CHUNK), lambda j: (0, j)),
            pl.BlockSpec((9, CHUNK), lambda j: (0, j)),
        ],
        out_specs=[
            pl.BlockSpec((wide, CHUNK), lambda j: (0, j)),
            pl.BlockSpec((wide, CHUNK), lambda j: (0, j)),
            pl.BlockSpec((tokens, CHUNK), lambda j: (0, j)),
        ],
        out_shape=[
            pltpu.HBM((wide, hid), BF),
            pltpu.HBM((wide, hid), BF),
            pltpu.HBM((tokens, hid), BF),
        ],
        scratch_shapes=[
            pltpu.VMEM((tokens, width), BF),
            pltpu.VMEM(strips.shape, BF),
            pltpu.VMEM((rows + 4, WIDE, CHUNK), F32),
        ],
        compiler_params=pltpu.CompilerParams(vmem_limit_bytes=16 * MIB),
        cost_estimate=pl.CostEstimate(
            flops=2 * 10**10, bytes_accessed=12 * 2**20, transcendentals=3 * 2**20
        ),
    )(*in_hbm(x), strips, *in_hbm(w_expand, w_depthwise))


def attention_kernel(in_ref, wq_ref, wo_ref, send_out, gq_out, att_out, qkv, gatt, att, gq):
    width = wo_ref.shape[0]
    groups = 8
    members = in_ref.shape[0] // groups
    scale = HDIM ** (-0.5)
    quads = width // 128

    def put(ref, at, value):
        value = value.astype(BF).astype(F32)
        for quad in range(quads):
            ref[at + quad] = value[:, quad * 128 : (quad + 1) * 128]

    for part in range(3):
        lanes = slice(part * width, (part + 1) * width)
        put(qkv, part * quads, dot(in_ref[:, 0:width], wq_ref[:, lanes]))
    put(gatt, 0, dot_nt(in_ref[:, width:], wo_ref[...]))
    per = 128 // HDIM
    head = lax.broadcasted_iota(jnp.int32, (members, 128), 1) // HDIM

    def spread(v):
        return jnp.concatenate([jnp.where(head == h, v, 0.0) for h in range(per)], 0).astype(BF)

    def gather(v):
        out = jnp.where(head == 0, v[0:members], 0.0)
        for h in range(1, per):
            out = jnp.where(head == h, v[h * members : (h + 1) * members], out)
        return out

    def one_group(g, _):
        at = pl.ds(g, members, stride=groups)
        for quad in range(quads):
            q = qkv[quad, at, :]
            k = qkv[quads + quad, at, :].astype(BF)
            v = qkv[2 * quads + quad, at, :].astype(BF)
            do = gatt[quad, at, :]
            qs, dos = spread(q), spread(do)
            scores = dot_nt(k, qs) * scale
            dp = dot_nt(v, dos)
            p = jnp.exp(scores - jnp.max(scores, 0, keepdims=True))
            p = p / jnp.sum(p, 0, keepdims=True)
            pb = p.astype(BF)
            ds = (p * (dp - jnp.sum(p * dp, 0, keepdims=True)) * scale).astype(BF)
            att[quad, at, :] = gather(dot_tn(pb, v))
            gq[quad, at, :] = gather(dot_tn(ds, k))
            gq[quads + quad, at, :] = dot(ds, qs)
            gq[2 * quads + quad, at, :] = dot(pb, dos)
        return 0

    lax.fori_loop(0, groups, one_group, 0)
    attended = jnp.concatenate([att[i] for i in range(quads)], 1).astype(BF)
    att_out[...] = attended
    send_out[:, 0:width] = dot(attended, wo_ref[...]).astype(BF)
    gqb = jnp.concatenate([gq[i] for i in range(3 * quads)], 1).astype(BF)
    gq_out[...] = gqb
    send_out[:, width:] = dot_nt(gqb, wq_ref[...]).astype(BF)


def attention_block(arrived, w_qkv, w_out):
    tokens = arrived.shape[0]
    width = w_out.shape[0]
    return pl.pallas_call(
        attention_kernel,
        name="grid_attention",
        out_shape=[
            pltpu.HBM((tokens, 2 * width), BF),
            pltpu.HBM((tokens, 3 * width), BF),
            pltpu.HBM((tokens, width), BF),
        ],
        scratch_shapes=[
            pltpu.VMEM((3 * width // 128, tokens, 128), F32),
            pltpu.VMEM((width // 128, tokens, 128), F32),
            pltpu.VMEM((width // 128, tokens, 128), F32),
            pltpu.VMEM((3 * width // 128, tokens, 128), F32),
        ],
        compiler_params=pltpu.CompilerParams(vmem_limit_bytes=22 * MIB),
        cost_estimate=pl.CostEstimate(
            flops=2 * 512 * 512 * 512 * 8, bytes_accessed=7 * 2**20, transcendentals=2**20
        ),
    )(arrived, *in_hbm(w_qkv, w_out))


def residual_kernel(home_ref, resid_ref, go_ref, out_ref, gr_ref):
    width = resid_ref.shape[1]
    resid = resid_ref[...].astype(F32)
    out_ref[...] = (resid + home_ref[:, 0:width].astype(F32)).astype(BF)
    back = normalize_back(resid, home_ref[:, width:].astype(F32))
    gr_ref[...] = (go_ref[...].astype(F32) + back).astype(BF)


def residual_block(home, resid, go):
    return pl.pallas_call(
        residual_kernel,
        name="residual",
        out_shape=[jax.ShapeDtypeStruct(resid.shape, BF)] * 2,
        compiler_params=pltpu.CompilerParams(vmem_limit_bytes=8 * MIB),
    )(home, *in_hbm(resid, go))


def split_by_core(core, full, mine_out, other_out):
    half = 128
    for j in range(full.shape[0] // (2 * half)):
        at = slice(j * half, (j + 1) * half)
        own = pl.multiple_of((2 * j + core) * half, half)
        other = pl.multiple_of((2 * j + 1 - core) * half, half)
        mine_out[at, :] = full[pl.ds(own, half), :]
        other_out[at, :] = full[pl.ds(other, half), :].astype(BF)


def backward_kernel(
    core_ref, x_ref, gr_ref, strips_ref, act_ref, slope_c_ref, slope_e_ref, wd_ref, wp_ref,
    gpre, mine_out, other_out,
    wide, grad_wide, normed, gmid, act, full, taps_t,
):
    step = pl.program_id(0)
    rows, cols = 16, 32
    width = x_ref.shape[1]

    @pl.when(step == 0)
    def _():
        place(wide, gr_ref[...].astype(F32), strips_ref[...].astype(F32), 1, rows, cols)
        grad_wide[...] = wide[...].reshape(grad_wide.shape).astype(BF)
        normed[...] = normalize(x_ref[...].astype(F32))[0].astype(BF)
        taps_t[...] = jnp.zeros(taps_t.shape, F32)

    gm = dot_nt(grad_wide[...], wp_ref[...]) * slope_c_ref[...].astype(F32)
    gmid[...] = gm.reshape(gmid.shape)
    act[...] = act_ref[...].astype(F32).reshape(act.shape)
    inside = lax.broadcasted_iota(jnp.int32, (WIDE, 128), 0) < cols
    for lo in range(0, CHUNK, 128):
        lanes = slice(lo, lo + 128)
        taps = [wd_ref[k : k + 1, lanes].astype(F32) for k in range(9)]
        sums = [None] * 9
        grads = [gmid[0, :, lanes], gmid[1, :, lanes]]
        acts = [act[0, :, lanes], act[1, :, lanes]]
        for r in range(rows):
            grads = grads[-2:] + [gmid[r + 2, :, lanes]]
            acts = acts[-2:] + [act[r + 2, :, lanes]]
            parts = [sum(grads[2 - i] * taps[3 * i + j] for i in range(3)) for j in range(3)]
            grad_act = parts[1] + roll(parts[0], -1) + roll(parts[2], 1)
            at = slice(r * cols, (r + 1) * cols)
            gpre[at, lanes] = (grad_act[0:cols] * slope_e_ref[at, lanes].astype(F32)).astype(BF)
            own = jnp.where(inside, grads[1], 0.0)
            moved = [roll(own, -1), own, roll(own, 1)]
            for k in range(9):
                prod = jnp.sum((acts[k // 3] * moved[k % 3]).reshape(WIDE // 8, 8, 128), 0)
                sums[k] = prod if r == 0 else sums[k] + prod
        for k in range(9):
            taps_t[k : k + 1, lanes] = jnp.sum(sums[k], 0, keepdims=True)
    full[:, 0:width] = dot_tn(gpre[...], normed[...])
    full[:, width:] = taps_t[...].T
    split_by_core(core_ref[0], full, mine_out, other_out)


def backward_block(core, x, gr, strips, act, slope_c, slope_e, w_depthwise, w_project):
    tokens, width = x.shape
    hid = w_project.shape[0]
    rows, cols = 16, 32
    whole = lambda a: pl.BlockSpec(a.shape, lambda j, c: (0,) * a.ndim)
    return pl.pallas_call(
        backward_kernel,
        name="mbconv_backward",
        grid_spec=pltpu.PrefetchScalarGridSpec(
            num_scalar_prefetch=1,
            grid=(hid // CHUNK,),
            in_specs=[
                whole(x), whole(gr), whole(strips),
                pl.BlockSpec(((rows + 2) * WIDE, CHUNK), lambda j, c: (0, j)),
                pl.BlockSpec(((rows + 2) * WIDE, CHUNK), lambda j, c: (0, j)),
                pl.BlockSpec((tokens, CHUNK), lambda j, c: (0, j)),
                pl.BlockSpec((9, CHUNK), lambda j, c: (0, j)),
                pl.BlockSpec((CHUNK, width), lambda j, c: (j, 0)),
            ],
            out_specs=[
                pl.BlockSpec((tokens, CHUNK), lambda j, c: (0, j)),
                pl.BlockSpec((CHUNK // 2, width + 128), lambda j, c: (j, 0)),
                pl.BlockSpec((CHUNK // 2, width + 128), lambda j, c: (j, 0)),
            ],
            scratch_shapes=[
                pltpu.VMEM((rows + 2, WIDE, width), F32),
                pltpu.VMEM(((rows + 2) * WIDE, width), BF),
                pltpu.VMEM((tokens, width), BF),
                pltpu.VMEM((rows + 2, WIDE, CHUNK), F32),
                pltpu.VMEM((rows + 2, WIDE, CHUNK), F32),
                pltpu.VMEM((CHUNK, width + 128), F32),
                pltpu.VMEM((128, CHUNK), F32),
            ],
        ),
        out_shape=[
            pltpu.HBM((tokens, hid), BF),
            jax.ShapeDtypeStruct((hid // 2, width + 128), F32),
            jax.ShapeDtypeStruct((hid // 2, width + 128), BF),
        ],
        compiler_params=pltpu.CompilerParams(vmem_limit_bytes=18 * MIB),
        cost_estimate=pl.CostEstimate(
            flops=16 * 512 * 512 * 2048, bytes_accessed=20 * 2**20, transcendentals=2**20
        ),
    )(core, *in_hbm(x), gr, strips, *in_hbm(act, slope_c, slope_e, w_depthwise, w_project))


def input_kernel(gpre_ref, we_ref, x_ref, gr_ref, gx_out):
    back = normalize_back(x_ref[...].astype(F32), dot_nt(gpre_ref[...], we_ref[...]))
    gx_out[...] = (gr_ref[...].astype(F32) + back).astype(BF)


def input_grads(gpre, w_expand, x, gr):
    tokens, width = x.shape
    hid = w_expand.shape[1]
    tile = 128
    return pl.pallas_call(
        input_kernel,
        name="grad_input",
        grid=(tokens // tile,),
        in_specs=[
            pl.BlockSpec((tile, hid), lambda i: (i, 0)),
            pl.BlockSpec((width, hid), lambda i: (0, 0)),
            pl.BlockSpec((tile, width), lambda i: (i, 0)),
            pl.BlockSpec((tile, width), lambda i: (i, 0)),
        ],
        out_specs=pl.BlockSpec((tile, width), lambda i: (i, 0)),
        out_shape=jax.ShapeDtypeStruct((tokens, width), BF),
        compiler_params=pltpu.CompilerParams(vmem_limit_bytes=12 * MIB),
        cost_estimate=pl.CostEstimate(
            flops=4 * 512 * 512 * 2048, bytes_accessed=6 * 2**20, transcendentals=0
        ),
    )(*in_hbm(gpre, w_expand, x, gr))


def finish_kernel(parts_ref, expand_out, depth_out):
    total = jnp.sum(parts_ref[...].astype(F32), 0)
    own, lanes = total.shape
    width = expand_out.shape[0]
    square = jnp.concatenate([total, jnp.zeros((128 - own, lanes), F32)], 0)
    expand_out[...] = square[:, 0:width].T[:, 0:own]
    depth_out[...] = square[:, width:].T[0:9, 0:own]


def finish(parts):
    _, own, lanes = parts.shape
    return pl.pallas_call(
        finish_kernel,
        name="last_sum",
        out_shape=[
            jax.ShapeDtypeStruct((lanes - 128, own), F32),
            jax.ShapeDtypeStruct((9, own), F32),
        ],
        compiler_params=pltpu.CompilerParams(vmem_limit_bytes=10 * MIB),
    )(parts)


def project_kernel(core_ref, mid_ref, gr_ref, mine_out, other_out, full):
    full[...] = dot_tn(mid_ref[...], gr_ref[...])
    split_by_core(core_ref[0], full, mine_out, other_out)


def project_grads(core, mid, gr):
    tokens, hid = mid.shape
    width = gr.shape[1]
    lanes = 512
    return pl.pallas_call(
        project_kernel,
        name="grad_project",
        grid_spec=pltpu.PrefetchScalarGridSpec(
            num_scalar_prefetch=1,
            grid=(hid // lanes,),
            in_specs=[
                pl.BlockSpec((tokens, lanes), lambda j, c: (0, j)),
                pl.BlockSpec((tokens, width), lambda j, c: (0, 0)),
            ],
            out_specs=[pl.BlockSpec((lanes // 2, width), lambda j, c: (j, 0))] * 2,
            scratch_shapes=[pltpu.VMEM((lanes, width), F32)],
        ),
        out_shape=[
            jax.ShapeDtypeStruct((hid // 2, width), F32),
            jax.ShapeDtypeStruct((hid // 2, width), BF),
        ],
        compiler_params=pltpu.CompilerParams(vmem_limit_bytes=8 * MIB),
        cost_estimate=pl.CostEstimate(
            flops=2 * 512 * 512 * 2048, bytes_accessed=7 * 2**20, transcendentals=0
        ),
    )(core, *in_hbm(mid), gr)


def attention_grads_kernel(
    core_ref, arrived_ref, gqkv_ref, att_ref, mine_out, other_out, qkv, outp, half_q, half_o, full
):
    width = att_ref.shape[1]
    qkv[...] = dot_tn(gqkv_ref[...], arrived_ref[:, 0:width])
    outp[...] = dot_tn(arrived_ref[:, width:], att_ref[...])
    nq, no = qkv.shape[0] // 16, outp.shape[0] // 16
    for j in range(8):
        for own in (True, False):
            core = core_ref[0] if own else 1 - core_ref[0]
            half_q[...] = qkv[pl.ds(pl.multiple_of((2 * j + core) * nq, 8), nq), :]
            half_o[...] = outp[pl.ds(pl.multiple_of((2 * j + core) * no, 8), no), :]
            for k in range(8):
                full[16 * k : 16 * k + 12, :] = half_q[12 * k : 12 * k + 12, :]
                full[16 * k + 12 : 16 * k + 16, :] = half_o[4 * k : 4 * k + 4, :]
            at = slice(128 * j, 128 * j + 128)
            if own:
                mine_out[at, :] = full[...]
            else:
                other_out[at, :] = full[...].astype(BF)


def attention_grads(core, arrived, gqkv, attended):
    tokens, width = attended.shape
    vmem = pl.BlockSpec(memory_space=pltpu.VMEM)
    return pl.pallas_call(
        attention_grads_kernel,
        name="attention_grads",
        in_specs=[pl.BlockSpec(memory_space=pltpu.SMEM), vmem, vmem, vmem],
        out_specs=[vmem, vmem],
        out_shape=[
            jax.ShapeDtypeStruct((1024, width), F32),
            jax.ShapeDtypeStruct((1024, width), BF),
        ],
        scratch_shapes=[
            pltpu.VMEM((3 * width, width), F32),
            pltpu.VMEM((width, width), F32),
            pltpu.VMEM((96, width), F32),
            pltpu.VMEM((32, width), F32),
            pltpu.VMEM((128, width), F32),
        ],
        compiler_params=pltpu.CompilerParams(vmem_limit_bytes=14 * MIB),
        cost_estimate=pl.CostEstimate(
            flops=8 * 512 * 512 * 512, bytes_accessed=8 * 2**20, transcendentals=0
        ),
    )(core, *in_hbm(arrived, gqkv, attended))


def add_pair(mine, other):
    got = lax.ppermute(other, AX, other_core())
    return (mine + got.astype(F32)).astype(BF).reshape(64, 16, -1)


def body(block_input, w_expand, w_depthwise, w_project, w_qkv, w_out, grad_out):
    _, rows, cols, width = block_input.shape
    tokens = rows * cols
    core = (lax.axis_index("row") % 2).astype(jnp.int32).reshape(1)
    image = block_input[0]
    x = image.reshape(tokens, width)
    go = grad_out[0].reshape(tokens, width)
    act0 = expand_block(x, w_expand, 0, 2)
    act1 = expand_block(x, w_expand, 1, 2)
    strips, (act0, act1) = halo(image, 2, act0), (act0, act1)
    mid, resid, send = forward_block(
        x, strips, go, act0, act1, w_expand, w_depthwise, w_project
    )
    arrived = across_chips(send.reshape(64, 8, 2 * width)).reshape(tokens, 2 * width)
    slopes = slopes_block(x, strips, w_expand, w_depthwise)
    arrived, (act, slope_c, slope_e) = lax.optimization_barrier((arrived, slopes))
    back, gqkv, attended = attention_block(arrived, w_qkv, w_out)
    home = across_chips(back.reshape(64, 8, 2 * width)).reshape(tokens, 2 * width)
    attention_pair = add_pair(*attention_grads(core, arrived, gqkv, attended))
    out, gr = residual_block(home, resid, go)
    mine, other = project_grads(core, mid, gr)
    strips = halo(gr.reshape(rows, cols, width), 1, mine)
    first = jnp.concatenate([add_pair(mine, other), attention_pair], 1)
    strips, first = lax.optimization_barrier((strips, first))
    first = across_chips(first)
    gpre, mine, other = backward_block(
        core, x, gr, strips, act, slope_c, slope_e, w_depthwise, w_project
    )
    gx = input_grads(gpre, w_expand, x, gr)
    second = add_pair(mine, other)
    second, first = lax.optimization_barrier((second, first))
    grad_expand, grad_depth = finish(across_chips(second))
    first = jnp.sum(first.astype(F32), 0)
    return (
        out.reshape(1, rows, cols, width),
        gx.reshape(1, rows, cols, width),
        grad_expand,
        grad_depth,
        first[:16].T,
        first[16:28].T,
        first[28:].T,
    )


def solution(mesh):
    tokens = P(None, "row", "col", None)
    split = P(None, AX)
    return jax.shard_map(
        body,
        mesh=mesh,
        in_specs=(tokens, P(), P(), P(), P(), P(), tokens),
        out_specs=(tokens, tokens, split, split, split, split, split),
        check_vma=False,
    )
```

```python
import functools
import itertools

import jax
import jax.numpy as jnp
from jax import lax
from jax.experimental import pallas as pl
from jax.experimental.pallas import tpu as pltpu
from jax.sharding import PartitionSpec as P

HEADS = 16
HDIM = 32
EPS = 1e-05
BF = jnp.bfloat16
F32 = jnp.float32
AX = ("row", "col")
WIDE = 40
CHUNK = 256
MIB = 2**20

SIZES = dict(y_lo=2, z=4, core=2, x=4, y_hi=2)
STRIDES = dict(y_lo=64, z=16, core=8, x=2, y_hi=1)
CHIPS = ("y_lo", "z", "x", "y_hi")


def device_groups(axes):
    rest = [a for a in SIZES if a not in axes]
    found = []
    for at in itertools.product(*[range(SIZES[a]) for a in rest]):
        base = sum(v * STRIDES[a] for v, a in zip(at, rest))
        found.append(
            [
                base + sum(v * STRIDES[a] for v, a in zip(m, axes))
                for m in itertools.product(*[range(SIZES[a]) for a in axes])
            ]
        )
    return found


def other_core():
    return [(d, d ^ STRIDES["core"]) for d in range(128)]


def across_chips(x):
    return lax.all_to_all(x, AX, 0, 0, tiled=True, axis_index_groups=device_groups(CHIPS))


def shift(x, axis, step):
    n = lax.axis_size(axis)
    pairs = [(i, i + step) for i in range(n) if 0 <= i + step < n]
    return lax.ppermute(x, axis, pairs)


def halo(x, width, ahead):
    rows, cols, chans = x.shape
    above = shift(x[rows - width :], "row", 1)
    below = shift(x[:width], "row", -1)
    above, below, _ = lax.optimization_barrier((above, below, ahead))
    to_right = jnp.concatenate(
        [above[:, cols - width :], x[:, cols - width :], below[:, cols - width :]], 0
    )
    to_left = jnp.concatenate([above[:, :width], x[:, :width], below[:, :width]], 0)
    left = shift(to_right, "col", 1)
    right = shift(to_left, "col", -1)
    gap = jnp.zeros((rows + 2 * width, 8 - 2 * width, chans), x.dtype)
    sides = jnp.concatenate([right, gap, left], 1)
    flat = [v.reshape(-1, chans) for v in (above, below, sides)]
    return jnp.concatenate(flat, 0)


def place(wide, centre, strips, width, rows, cols):
    lanes = strips.shape[-1]
    n = width * cols
    if centre is not None:
        wide[width : width + rows, 0:cols, :] = centre.reshape(rows, cols, lanes)
    wide[0:width, 0:cols, :] = strips[0:n].reshape(width, cols, lanes)
    wide[width + rows :, 0:cols, :] = strips[n : 2 * n].reshape(width, cols, lanes)
    wide[:, cols:, :] = strips[2 * n :].reshape(rows + 2 * width, WIDE - cols, lanes)


def normalize(x):
    center = x - jnp.mean(x, -1, keepdims=True)
    ratio = lax.rsqrt(jnp.mean(center * center, -1, keepdims=True) + EPS)
    return center * ratio, ratio


def normalize_back(x, grad):
    scaled, ratio = normalize(x)
    return (
        grad
        - jnp.mean(grad, -1, keepdims=True)
        - scaled * jnp.mean(grad * scaled, -1, keepdims=True)
    ) * ratio


A0 = 0.7978845608028654
A1 = A0 * 0.044715


def gelu_half(x):
    inner = A0 + A1 * (x * x)
    return inner, 0.5 + 0.5 * jnp.tanh(x * inner)


def gelu(x):
    return x * gelu_half(x)[1]


def gelu_slope(x):
    inner, half = gelu_half(x)
    value = x * half
    return half + (value - value * half) * (6.0 * inner - 4.0 * A0)


def dot(a, b):
    return jnp.dot(a, b, preferred_element_type=F32)


def dot_nt(a, b):
    return lax.dot_general(a, b, (((1,), (1,)), ((), ())), preferred_element_type=F32)


def dot_tn(a, b):
    return lax.dot_general(a, b, (((0,), (0,)), ((), ())), preferred_element_type=F32)


def in_hbm(*arrays):
    return [pltpu.with_memory_space_constraint(a, pltpu.HBM) for a in arrays]


def roll(x, by):
    return pltpu.roll(x, by % x.shape[0], 0)


def expand_kernel(x_ref, we_ref, *refs):
    act_out, normed = refs[-2:]

    @pl.when(pl.program_id(0) == 0)
    def _():
        normed[...] = normalize(x_ref[...].astype(F32))[0].astype(BF)

    for tile in range(0, x_ref.shape[0], 128):
        at = slice(tile, tile + 128)
        act_out[at, :] = gelu(dot(normed[at, :], we_ref[...])).astype(BF)


def expand_block(x, w_expand, part, parts, held=None):
    tokens, width = x.shape
    hid = w_expand.shape[1]
    lanes = 512
    steps = hid // lanes // parts
    held = [] if held is None else [held]
    return pl.pallas_call(
        expand_kernel,
        name="expand",
        grid=(steps,),
        in_specs=[
            pl.BlockSpec((tokens, width), lambda j: (0, 0)),
            pl.BlockSpec((width, lanes), lambda j: (0, j + part * steps)),
            *[pl.BlockSpec(memory_space=pl.ANY) for _ in held],
        ],
        out_specs=pl.BlockSpec((tokens, lanes), lambda j: (0, j + part * steps)),
        out_shape=jax.ShapeDtypeStruct((tokens, hid), BF),
        scratch_shapes=[pltpu.VMEM((tokens, width), BF)],
        input_output_aliases={2: 0} if held else {},
        compiler_params=pltpu.CompilerParams(vmem_limit_bytes=8 * MIB),
        cost_estimate=pl.CostEstimate(
            flops=8 * 512 * 512 * 2048, bytes_accessed=3 * 2**20, transcendentals=2**19
        ),
    )(*in_hbm(x, w_expand), *held)


FORWARD = 512


def forward_kernel(
    x_hbm, strips_ref, go_hbm, act_ref, we_ref, wd_ref, wp_ref,
    mid_out, resid_out, send_out,
    normed, edge, acc, x_ref, go_ref, sems,
):
    step = pl.program_id(0)
    rows, cols = 16, 32
    width = x_ref.shape[1]
    load_x = pltpu.make_async_copy(x_hbm, x_ref, sems.at[0])
    load_go = pltpu.make_async_copy(go_hbm, go_ref, sems.at[1])

    @pl.when(step == 0)
    def _():
        load_x.start()
        load_go.start()
        every = normalize(strips_ref[...].astype(F32))[0]
        sides = 4 * cols + 8
        near = [every[cols : 3 * cols], every[sides : sides + 8 * (rows + 2)]]
        normed[...] = jnp.concatenate(near, 0).astype(BF)

    edge[...] = gelu(dot(normed[...], we_ref[...]))
    for lo in range(0, FORWARD, 128):
        lanes = slice(lo, lo + 128)
        taps = [wd_ref[k : k + 1, lanes].astype(F32) for k in range(9)]

        def line(r):
            if r == 0:
                centre = edge[0:cols, lanes]
            elif r == rows + 1:
                centre = edge[cols : 2 * cols, lanes]
            else:
                centre = act_ref[(r - 1) * cols : r * cols, lanes].astype(F32)
            side = edge[2 * cols + 8 * r : 2 * cols + 8 * (r + 1), lanes]
            whole = jnp.concatenate([centre, side], 0)
            return roll(whole, 1)[0:cols], centre, roll(whole, -1)[0:cols]

        lines = [line(0), line(1)]
        for r in range(rows):
            lines = lines[-2:] + [line(r + 2)]
            conv = sum(lines[k // 3][k % 3] * taps[k] for k in range(9))
            mid_out[r * cols : (r + 1) * cols, lanes] = gelu(conv).astype(BF)
        if lo % 256:
            at = slice(lo - 128, lo + 128)
            part = dot(mid_out[:, at], wp_ref[at, :])
            product = part if lo == 128 else product + part

    @pl.when(step == 0)
    def _():
        acc[...] = product

    @pl.when(step > 0)
    def _():
        acc[...] += product

    @pl.when(step == pl.num_programs(0) - 1)
    def _():
        load_x.wait()
        resid = (x_ref[...].astype(F32) + acc[...]).astype(BF)
        resid_out[...] = resid
        send_out[:, 0:width] = normalize(resid.astype(F32))[0].astype(BF)
        load_go.wait()
        send_out[:, width:] = go_ref[...]


def forward_block(x, strips, go, act, w_expand, w_depthwise, w_project):
    tokens, width = x.shape
    hid = w_expand.shape[1]
    rows, cols = 16, 32
    near = 2 * cols + 8 * (rows + 2)
    anywhere = pl.BlockSpec(memory_space=pl.ANY)
    whole = lambda a: pl.BlockSpec(a.shape, lambda j: (0,) * a.ndim)
    return pl.pallas_call(
        forward_kernel,
        name="mbconv_forward",
        grid=(hid // FORWARD,),
        in_specs=[
            anywhere, whole(strips), anywhere,
            pl.BlockSpec((tokens, FORWARD), lambda j: (0, j)),
            pl.BlockSpec((width, FORWARD), lambda j: (0, j)),
            pl.BlockSpec((9, FORWARD), lambda j: (0, j)),
            pl.BlockSpec((FORWARD, width), lambda j: (j, 0)),
        ],
        out_specs=[
            pl.BlockSpec((tokens, FORWARD), lambda j: (0, j)),
            pl.BlockSpec((tokens, width), lambda j: (0, 0)),
            pl.BlockSpec((tokens, 2 * width), lambda j: (0, 0)),
        ],
        out_shape=[
            pltpu.HBM((tokens, hid), BF),
            pltpu.HBM((tokens, width), BF),
            pltpu.HBM((tokens, 2 * width), BF),
        ],
        scratch_shapes=[
            pltpu.VMEM((near, width), BF),
            pltpu.VMEM((near, FORWARD), F32),
            pltpu.VMEM((tokens, width), F32),
            pltpu.VMEM((tokens, width), BF),
            pltpu.VMEM((tokens, width), BF),
            pltpu.SemaphoreType.DMA((2,)),
        ],
        compiler_params=pltpu.CompilerParams(vmem_limit_bytes=18 * MIB),
        cost_estimate=pl.CostEstimate(
            flops=2 * 700 * 512 * 2048, bytes_accessed=10 * 2**20, transcendentals=2**20
        ),
    )(*in_hbm(x), strips, *in_hbm(go), act, *in_hbm(w_expand, w_depthwise, w_project))


def slopes_kernel(
    x_ref, strips_ref, we_ref, wd_ref, act_out, slope_c_out, slope_e_out, normed, normed_s, act
):
    rows, cols = 16, 32

    @pl.when(pl.program_id(0) == 0)
    def _():
        normed[...] = normalize(x_ref[...].astype(F32))[0].astype(BF)
        normed_s[...] = normalize(strips_ref[...].astype(F32))[0].astype(BF)

    for tile in range(0, x_ref.shape[0], 128):
        at = slice(tile, tile + 128)
        pre = dot(normed[at, :], we_ref[...])
        slope_e_out[at, :] = gelu_slope(pre).astype(BF)
        act[2 + tile // cols : 2 + (tile + 128) // cols, 0:cols, :] = (
            gelu(pre).astype(BF).astype(F32).reshape(128 // cols, cols, CHUNK)
        )
    strips = gelu(dot(normed_s[...], we_ref[...])).astype(BF).astype(F32)
    place(act, None, strips, 2, rows, cols)
    act_out[...] = act[1 : rows + 3].reshape(act_out.shape).astype(BF)
    for lo in range(0, CHUNK, 128):
        lanes = slice(lo, lo + 128)
        taps = [wd_ref[k : k + 1, lanes].astype(F32) for k in range(9)]
        lines = [act[0, :, lanes], act[1, :, lanes]]
        held = None
        for r in range(rows + 2):
            lines = lines[-2:] + [act[r + 2, :, lanes]]
            sums = [sum(lines[i] * taps[3 * i + j] for i in range(3)) for j in range(3)]
            slope = gelu_slope(sums[1] + roll(sums[0], 1) + roll(sums[2], -1))
            if r % 2:
                pair = jnp.concatenate([held, slope], 0).astype(BF)
                slope_c_out[(r - 1) * WIDE : (r + 1) * WIDE, lanes] = pair
            held = slope


def slopes_block(x, strips, w_expand, w_depthwise):
    tokens, width = x.shape
    hid = w_expand.shape[1]
    rows, cols = 16, 32
    wide = (rows + 2) * WIDE
    whole = lambda a: pl.BlockSpec(a.shape, lambda j: (0,) * a.ndim)
    return pl.pallas_call(
        slopes_kernel,
        name="gelu_slopes",
        grid=(hid // CHUNK,),
        in_specs=[
            whole(x), whole(strips),
            pl.BlockSpec((width, CHUNK), lambda j: (0, j)),
            pl.BlockSpec((9, CHUNK), lambda j: (0, j)),
        ],
        out_specs=[
            pl.BlockSpec((wide, CHUNK), lambda j: (0, j)),
            pl.BlockSpec((wide, CHUNK), lambda j: (0, j)),
            pl.BlockSpec((tokens, CHUNK), lambda j: (0, j)),
        ],
        out_shape=[
            pltpu.HBM((wide, hid), BF),
            pltpu.HBM((wide, hid), BF),
            pltpu.HBM((tokens, hid), BF),
        ],
        scratch_shapes=[
            pltpu.VMEM((tokens, width), BF),
            pltpu.VMEM(strips.shape, BF),
            pltpu.VMEM((rows + 4, WIDE, CHUNK), F32),
        ],
        compiler_params=pltpu.CompilerParams(vmem_limit_bytes=16 * MIB),
        cost_estimate=pl.CostEstimate(
            flops=2 * 10**10, bytes_accessed=12 * 2**20, transcendentals=3 * 2**20
        ),
    )(*in_hbm(x), strips, *in_hbm(w_expand, w_depthwise))


def attention_kernel(
    in_ref, wq_hbm, wo_hbm, send_hbm, gq_hbm, att_hbm,
    wq, wo, qkv, gatt, att, gq, send, gqb, attended, sems,
):
    tokens, width = attended.shape
    groups = 8
    members = tokens // groups
    quads = width // 128
    scale = HDIM ** (-0.5)
    load_wo = pltpu.make_async_copy(wo_hbm, wo, sems.at[0])
    load_wq = pltpu.make_async_copy(wq_hbm, wq, sems.at[1])
    load_wo.start()
    load_wq.start()

    def put(ref, at, value):
        value = value.astype(BF).astype(F32)
        for quad in range(quads):
            ref[at + quad] = value[:, quad * 128 : (quad + 1) * 128]

    load_wo.wait()
    put(gatt, 0, dot_nt(in_ref[:, width:], wo[...]))
    load_wq.wait()
    for part in range(3):
        lanes = slice(part * width, (part + 1) * width)
        put(qkv, part * quads, dot(in_ref[:, 0:width], wq[:, lanes]))
    per = 128 // HDIM
    head = lax.broadcasted_iota(jnp.int32, (members, 128), 1) // HDIM

    def spread(v):
        return jnp.concatenate([jnp.where(head == h, v, 0.0) for h in range(per)], 0).astype(BF)

    def gather(v):
        out = jnp.where(head == 0, v[0:members], 0.0)
        for h in range(1, per):
            out = jnp.where(head == h, v[h * members : (h + 1) * members], out)
        return out

    def one_group(g, _):
        at = pl.ds(g, members, stride=groups)
        every = range(quads)
        q = [spread(qkv[i, at, :]) for i in every]
        k = [qkv[quads + i, at, :].astype(BF) for i in every]
        v = [qkv[2 * quads + i, at, :].astype(BF) for i in every]
        do = [spread(gatt[i, at, :]) for i in every]
        scores = [dot_nt(k[i], q[i]) * scale for i in every]
        dp = [dot_nt(v[i], do[i]) for i in every]
        p = [jnp.exp(s - jnp.max(s, 0, keepdims=True)) for s in scores]
        p = [e * (1.0 / jnp.sum(e, 0, keepdims=True)) for e in p]
        pb = [e.astype(BF) for e in p]
        ds = [
            (p[i] * (dp[i] - jnp.sum(p[i] * dp[i], 0, keepdims=True)) * scale).astype(BF)
            for i in every
        ]
        for i in every:
            att[i, at, :] = gather(dot_tn(pb[i], v[i]))
            gq[i, at, :] = gather(dot_tn(ds[i], k[i]))
            gq[quads + i, at, :] = dot(ds[i], q[i])
            gq[2 * quads + i, at, :] = dot(pb[i], do[i])
        return 0

    lax.fori_loop(0, groups, one_group, 0)
    attended[...] = jnp.concatenate([att[i] for i in range(quads)], 1).astype(BF)
    store_att = pltpu.make_async_copy(attended, att_hbm, sems.at[2])
    store_att.start()
    gqb[...] = jnp.concatenate([gq[i] for i in range(3 * quads)], 1).astype(BF)
    store_gq = pltpu.make_async_copy(gqb, gq_hbm, sems.at[3])
    store_gq.start()
    stores = []
    for half in range(2):
        at = pl.ds(half * tokens // 2, tokens // 2)
        rows = slice(half * tokens // 2, (half + 1) * tokens // 2)
        send[rows, 0:width] = dot(attended[rows, :], wo[...]).astype(BF)
        send[rows, width:] = dot_nt(gqb[rows, :], wq[...]).astype(BF)
        store = pltpu.make_async_copy(send.at[at], send_hbm.at[at], sems.at[4 + half])
        store.start()
        stores.append(store)
    for store in [store_att, store_gq, *stores]:
        store.wait()


def attention_block(arrived, w_qkv, w_out):
    tokens = arrived.shape[0]
    width = w_out.shape[0]
    anywhere = pl.BlockSpec(memory_space=pl.ANY)
    return pl.pallas_call(
        attention_kernel,
        name="grid_attention",
        in_specs=[pl.BlockSpec(memory_space=pltpu.VMEM), anywhere, anywhere],
        out_specs=[anywhere] * 3,
        out_shape=[
            pltpu.HBM((tokens, 2 * width), BF),
            pltpu.HBM((tokens, 3 * width), BF),
            pltpu.HBM((tokens, width), BF),
        ],
        scratch_shapes=[
            pltpu.VMEM((width, 3 * width), BF),
            pltpu.VMEM((width, width), BF),
            pltpu.VMEM((3 * width // 128, tokens, 128), F32),
            pltpu.VMEM((width // 128, tokens, 128), F32),
            pltpu.VMEM((width // 128, tokens, 128), F32),
            pltpu.VMEM((3 * width // 128, tokens, 128), F32),
            pltpu.VMEM((tokens, 2 * width), BF),
            pltpu.VMEM((tokens, 3 * width), BF),
            pltpu.VMEM((tokens, width), BF),
            pltpu.SemaphoreType.DMA((6,)),
        ],
        compiler_params=pltpu.CompilerParams(vmem_limit_bytes=24 * MIB),
        cost_estimate=pl.CostEstimate(
            flops=2 * 512 * 512 * 512 * 8, bytes_accessed=7 * 2**20, transcendentals=2**20
        ),
    )(arrived, *in_hbm(w_qkv, w_out))


def residual_kernel(home_ref, resid_ref, go_ref, out_ref, gr_ref):
    width = resid_ref.shape[1]
    resid = resid_ref[...].astype(F32)
    out_ref[...] = (resid + home_ref[:, 0:width].astype(F32)).astype(BF)
    back = normalize_back(resid, home_ref[:, width:].astype(F32))
    gr_ref[...] = (go_ref[...].astype(F32) + back).astype(BF)


def residual_block(home, resid, go):
    return pl.pallas_call(
        residual_kernel,
        name="residual",
        out_shape=[jax.ShapeDtypeStruct(resid.shape, BF)] * 2,
        compiler_params=pltpu.CompilerParams(vmem_limit_bytes=8 * MIB),
    )(home, *in_hbm(resid, go))


def split_by_core(core, full, mine_out, other_out):
    half = 128
    for j in range(full.shape[0] // (2 * half)):
        at = slice(j * half, (j + 1) * half)
        own = pl.multiple_of((2 * j + core) * half, half)
        other = pl.multiple_of((2 * j + 1 - core) * half, half)
        mine_out[at, :] = full[pl.ds(own, half), :]
        other_out[at, :] = full[pl.ds(other, half), :].astype(BF)


def backward_kernel(
    core_ref, x_ref, gr_ref, strips_ref, act_ref, slope_c_ref, slope_e_ref, wd_ref, wp_ref,
    gpre, mine_out, other_out,
    wide, grad_wide, normed, gmid, act, full, taps_t,
):
    step = pl.program_id(0)
    rows, cols = 16, 32
    width = x_ref.shape[1]

    @pl.when(step == 0)
    def _():
        place(wide, gr_ref[...].astype(F32), strips_ref[...].astype(F32), 1, rows, cols)
        grad_wide[...] = wide[...].reshape(grad_wide.shape).astype(BF)
        normed[...] = normalize(x_ref[...].astype(F32))[0].astype(BF)
        taps_t[...] = jnp.zeros(taps_t.shape, F32)

    gm = dot_nt(grad_wide[...], wp_ref[...]) * slope_c_ref[...].astype(F32)
    gmid[...] = gm.reshape(gmid.shape)
    act[...] = act_ref[...].astype(F32).reshape(act.shape)
    inside = lax.broadcasted_iota(jnp.int32, (WIDE, 128), 0) < cols
    for lo in range(0, CHUNK, 128):
        lanes = slice(lo, lo + 128)
        taps = [wd_ref[k : k + 1, lanes].astype(F32) for k in range(9)]
        sums = [None] * 9
        grads = [gmid[0, :, lanes], gmid[1, :, lanes]]
        acts = [act[0, :, lanes], act[1, :, lanes]]
        for r in range(rows):
            grads = grads[-2:] + [gmid[r + 2, :, lanes]]
            acts = acts[-2:] + [act[r + 2, :, lanes]]
            parts = [sum(grads[2 - i] * taps[3 * i + j] for i in range(3)) for j in range(3)]
            grad_act = parts[1] + roll(parts[0], -1) + roll(parts[2], 1)
            at = slice(r * cols, (r + 1) * cols)
            gpre[at, lanes] = (grad_act[0:cols] * slope_e_ref[at, lanes].astype(F32)).astype(BF)
            own = jnp.where(inside, grads[1], 0.0)
            moved = [roll(own, -1), own, roll(own, 1)]
            for k in range(9):
                prod = jnp.sum((acts[k // 3] * moved[k % 3]).reshape(WIDE // 8, 8, 128), 0)
                sums[k] = prod if r == 0 else sums[k] + prod
        for k in range(9):
            taps_t[k : k + 1, lanes] = jnp.sum(sums[k], 0, keepdims=True)
    full[:, 0:width] = dot_tn(gpre[...], normed[...])
    full[:, width:] = taps_t[...].T
    split_by_core(core_ref[0], full, mine_out, other_out)


def backward_block(core, x, gr, strips, act, slope_c, slope_e, w_depthwise, w_project):
    tokens, width = x.shape
    hid = w_project.shape[0]
    rows, cols = 16, 32
    whole = lambda a: pl.BlockSpec(a.shape, lambda j, c: (0,) * a.ndim)
    return pl.pallas_call(
        backward_kernel,
        name="mbconv_backward",
        grid_spec=pltpu.PrefetchScalarGridSpec(
            num_scalar_prefetch=1,
            grid=(hid // CHUNK,),
            in_specs=[
                whole(x), whole(gr), whole(strips),
                pl.BlockSpec(((rows + 2) * WIDE, CHUNK), lambda j, c: (0, j)),
                pl.BlockSpec(((rows + 2) * WIDE, CHUNK), lambda j, c: (0, j)),
                pl.BlockSpec((tokens, CHUNK), lambda j, c: (0, j)),
                pl.BlockSpec((9, CHUNK), lambda j, c: (0, j)),
                pl.BlockSpec((CHUNK, width), lambda j, c: (j, 0)),
            ],
            out_specs=[
                pl.BlockSpec((tokens, CHUNK), lambda j, c: (0, j)),
                pl.BlockSpec((CHUNK // 2, width + 128), lambda j, c: (j, 0)),
                pl.BlockSpec((CHUNK // 2, width + 128), lambda j, c: (j, 0)),
            ],
            scratch_shapes=[
                pltpu.VMEM((rows + 2, WIDE, width), F32),
                pltpu.VMEM(((rows + 2) * WIDE, width), BF),
                pltpu.VMEM((tokens, width), BF),
                pltpu.VMEM((rows + 2, WIDE, CHUNK), F32),
                pltpu.VMEM((rows + 2, WIDE, CHUNK), F32),
                pltpu.VMEM((CHUNK, width + 128), F32),
                pltpu.VMEM((128, CHUNK), F32),
            ],
        ),
        out_shape=[
            pltpu.HBM((tokens, hid), BF),
            jax.ShapeDtypeStruct((hid // 2, width + 128), F32),
            jax.ShapeDtypeStruct((hid // 2, width + 128), BF),
        ],
        compiler_params=pltpu.CompilerParams(vmem_limit_bytes=18 * MIB),
        cost_estimate=pl.CostEstimate(
            flops=16 * 512 * 512 * 2048, bytes_accessed=20 * 2**20, transcendentals=2**20
        ),
    )(core, *in_hbm(x), gr, strips, *in_hbm(act, slope_c, slope_e, w_depthwise, w_project))


def input_kernel(gpre_ref, we_ref, x_ref, gr_ref, gx_out):
    back = normalize_back(x_ref[...].astype(F32), dot_nt(gpre_ref[...], we_ref[...]))
    gx_out[...] = (gr_ref[...].astype(F32) + back).astype(BF)


def input_grads(gpre, w_expand, x, gr):
    tokens, width = x.shape
    hid = w_expand.shape[1]
    tile = 128
    return pl.pallas_call(
        input_kernel,
        name="grad_input",
        grid=(tokens // tile,),
        in_specs=[
            pl.BlockSpec((tile, hid), lambda i: (i, 0)),
            pl.BlockSpec((width, hid), lambda i: (0, 0)),
            pl.BlockSpec((tile, width), lambda i: (i, 0)),
            pl.BlockSpec((tile, width), lambda i: (i, 0)),
        ],
        out_specs=pl.BlockSpec((tile, width), lambda i: (i, 0)),
        out_shape=jax.ShapeDtypeStruct((tokens, width), BF),
        compiler_params=pltpu.CompilerParams(vmem_limit_bytes=12 * MIB),
        cost_estimate=pl.CostEstimate(
            flops=4 * 512 * 512 * 2048, bytes_accessed=6 * 2**20, transcendentals=0
        ),
    )(*in_hbm(gpre, w_expand, x, gr))


def finish_kernel(parts_ref, expand_out, depth_out):
    total = jnp.sum(parts_ref[...].astype(F32), 0)
    own, width = expand_out.shape
    expand_out[...] = total[:, 0:width]
    square = jnp.concatenate([total[:, width:], jnp.zeros((128 - own, 128), F32)], 0)
    depth_out[...] = square.T[0:9, 0:own]


def finish(parts):
    _, own, lanes = parts.shape
    return pl.pallas_call(
        finish_kernel,
        name="last_sum",
        out_shape=[
            pltpu.HBM((own, lanes - 128), F32),
            pltpu.HBM((9, own), F32),
        ],
        compiler_params=pltpu.CompilerParams(vmem_limit_bytes=10 * MIB),
    )(parts)


def project_kernel(core_ref, mid_ref, gr_ref, mine_out, other_out, full):
    full[...] = dot_tn(mid_ref[...], gr_ref[...])
    split_by_core(core_ref[0], full, mine_out, other_out)


def project_grads(core, mid, gr):
    tokens, hid = mid.shape
    width = gr.shape[1]
    lanes = 512
    return pl.pallas_call(
        project_kernel,
        name="grad_project",
        grid_spec=pltpu.PrefetchScalarGridSpec(
            num_scalar_prefetch=1,
            grid=(hid // lanes,),
            in_specs=[
                pl.BlockSpec((tokens, lanes), lambda j, c: (0, j)),
                pl.BlockSpec((tokens, width), lambda j, c: (0, 0)),
            ],
            out_specs=[pl.BlockSpec((lanes // 2, width), lambda j, c: (j, 0))] * 2,
            scratch_shapes=[pltpu.VMEM((lanes, width), F32)],
        ),
        out_shape=[
            jax.ShapeDtypeStruct((hid // 2, width), F32),
            jax.ShapeDtypeStruct((hid // 2, width), BF),
        ],
        compiler_params=pltpu.CompilerParams(vmem_limit_bytes=8 * MIB),
        cost_estimate=pl.CostEstimate(
            flops=2 * 512 * 512 * 2048, bytes_accessed=7 * 2**20, transcendentals=0
        ),
    )(core, *in_hbm(mid), gr)


def attention_grads_kernel(
    core_ref, arrived_ref, gqkv_ref, att_ref, mine_out, other_out, qkv, outp, half_q, half_o, full
):
    width = att_ref.shape[1]
    qkv[...] = dot_tn(gqkv_ref[...], arrived_ref[:, 0:width])
    outp[...] = dot_tn(arrived_ref[:, width:], att_ref[...])
    nq, no = qkv.shape[0] // 16, outp.shape[0] // 16
    for j in range(8):
        for own in (True, False):
            core = core_ref[0] if own else 1 - core_ref[0]
            half_q[...] = qkv[pl.ds(pl.multiple_of((2 * j + core) * nq, 8), nq), :]
            half_o[...] = outp[pl.ds(pl.multiple_of((2 * j + core) * no, 8), no), :]
            for k in range(8):
                full[16 * k : 16 * k + 12, :] = half_q[12 * k : 12 * k + 12, :]
                full[16 * k + 12 : 16 * k + 16, :] = half_o[4 * k : 4 * k + 4, :]
            at = slice(128 * j, 128 * j + 128)
            if own:
                mine_out[at, :] = full[...]
            else:
                other_out[at, :] = full[...].astype(BF)


def attention_grads(core, arrived, gqkv, attended):
    tokens, width = attended.shape
    vmem = pl.BlockSpec(memory_space=pltpu.VMEM)
    return pl.pallas_call(
        attention_grads_kernel,
        name="attention_grads",
        in_specs=[pl.BlockSpec(memory_space=pltpu.SMEM), vmem, vmem, vmem],
        out_specs=[vmem, vmem],
        out_shape=[
            jax.ShapeDtypeStruct((1024, width), F32),
            jax.ShapeDtypeStruct((1024, width), BF),
        ],
        scratch_shapes=[
            pltpu.VMEM((3 * width, width), F32),
            pltpu.VMEM((width, width), F32),
            pltpu.VMEM((96, width), F32),
            pltpu.VMEM((32, width), F32),
            pltpu.VMEM((128, width), F32),
        ],
        compiler_params=pltpu.CompilerParams(vmem_limit_bytes=14 * MIB),
        cost_estimate=pl.CostEstimate(
            flops=8 * 512 * 512 * 512, bytes_accessed=8 * 2**20, transcendentals=0
        ),
    )(core, *in_hbm(arrived, gqkv, attended))


def add_pair(mine, other):
    got = lax.ppermute(other, AX, other_core())
    return (mine + got.astype(F32)).astype(BF).reshape(64, 16, -1)


def body(block_input, w_expand, w_depthwise, w_project, w_qkv, w_out, grad_out):
    _, rows, cols, width = block_input.shape
    tokens = rows * cols
    core = (lax.axis_index("row") % 2).astype(jnp.int32).reshape(1)
    image = block_input[0]
    x = image.reshape(tokens, width)
    go = grad_out[0].reshape(tokens, width)
    act0 = expand_block(x, w_expand, 0, 2)
    centre = expand_block(x, w_expand, 1, 2, act0)
    strips = halo(image, 2, act0)
    mid, resid, send = forward_block(x, strips, go, centre, w_expand, w_depthwise, w_project)
    arrived = across_chips(send.reshape(64, 8, 2 * width)).reshape(tokens, 2 * width)
    slopes = slopes_block(x, strips, w_expand, w_depthwise)
    arrived, (act, slope_c, slope_e) = lax.optimization_barrier((arrived, slopes))
    back, gqkv, attended = attention_block(arrived, w_qkv, w_out)
    home = across_chips(back.reshape(64, 8, 2 * width)).reshape(tokens, 2 * width)
    attention_pair = add_pair(*attention_grads(core, arrived, gqkv, attended))
    out, gr = residual_block(home, resid, go)
    mine, other = project_grads(core, mid, gr)
    strips = halo(gr.reshape(rows, cols, width), 1, mine)
    first = jnp.concatenate([add_pair(mine, other), attention_pair], 1)
    strips, first = lax.optimization_barrier((strips, first))
    first = across_chips(first)
    gpre, mine, other = backward_block(
        core, x, gr, strips, act, slope_c, slope_e, w_depthwise, w_project
    )
    gx = input_grads(gpre, w_expand, x, gr)
    second = add_pair(mine, other)
    second, first = lax.optimization_barrier((second, first))
    grad_expand, grad_depth = finish(across_chips(second))
    first = jnp.sum(first.astype(F32), 0)
    return (
        out.reshape(1, rows, cols, width),
        gx.reshape(1, rows, cols, width),
        grad_expand.T,
        grad_depth,
        first[:16].T,
        first[16:28].T,
        first[28:].T,
    )


def solution(mesh):
    tokens = P(None, "row", "col", None)
    split = P(None, AX)
    return jax.shard_map(
        body,
        mesh=mesh,
        in_specs=(tokens, P(), P(), P(), P(), P(), tokens),
        out_specs=(tokens, tokens, split, split, split, split, split),
        check_vma=False,
    )
```

```python
import functools
import itertools

import jax
import jax.numpy as jnp
from jax import lax
from jax.experimental import pallas as pl
from jax.experimental.pallas import tpu as pltpu
from jax.sharding import PartitionSpec as P

HEADS = 16
HDIM = 32
EPS = 1e-05
BF = jnp.bfloat16
F32 = jnp.float32
AX = ("row", "col")
WIDE = 40
CHUNK = 256
MIB = 2**20

SIZES = dict(y_lo=2, z=4, core=2, x=4, y_hi=2)
STRIDES = dict(y_lo=64, z=16, core=8, x=2, y_hi=1)
CHIPS = ("y_lo", "z", "x", "y_hi")


def device_groups(axes):
    rest = [a for a in SIZES if a not in axes]
    found = []
    for at in itertools.product(*[range(SIZES[a]) for a in rest]):
        base = sum(v * STRIDES[a] for v, a in zip(at, rest))
        found.append(
            [
                base + sum(v * STRIDES[a] for v, a in zip(m, axes))
                for m in itertools.product(*[range(SIZES[a]) for a in axes])
            ]
        )
    return found


def other_core():
    return [(d, d ^ STRIDES["core"]) for d in range(128)]


def across_chips(x):
    return lax.all_to_all(x, AX, 0, 0, tiled=True, axis_index_groups=device_groups(CHIPS))


def shift(x, axis, step):
    n = lax.axis_size(axis)
    pairs = [(i, i + step) for i in range(n) if 0 <= i + step < n]
    return lax.ppermute(x, axis, pairs)


def halo(x, width, ahead, beside):
    rows, cols, chans = x.shape
    above = shift(x[rows - width :], "row", 1)
    below = shift(x[:width], "row", -1)
    above, below, _ = lax.optimization_barrier((above, below, ahead))
    flat = lambda v: v.reshape(-1, chans)

    def column(at, other):
        parts = [above[:, at], x[:, at], below[:, at]]
        return jnp.concatenate([flat(p) for p in parts] + [beside[:, other]], 0)

    left = shift(column(slice(cols - width, cols), cols - 1), "col", 1)
    right = shift(column(slice(0, width), 0), "col", -1)
    n = (rows + 2 * width) * width

    def sides(right, left, width):
        right, left = [v.reshape(-1, width, chans) for v in (right, left)]
        gap = jnp.zeros((right.shape[0], 8 - 2 * width, chans), x.dtype)
        return flat(jnp.concatenate([right, gap, left], 1))

    strips = [flat(above), flat(below), sides(right[:n], left[:n], width)]
    return jnp.concatenate(strips, 0), sides(right[n:], left[n:], 1)


def place(wide, centre, strips, width, rows, cols):
    lanes = strips.shape[-1]
    n = width * cols
    if centre is not None:
        wide[width : width + rows, 0:cols, :] = centre.reshape(rows, cols, lanes)
    wide[0:width, 0:cols, :] = strips[0:n].reshape(width, cols, lanes)
    wide[width + rows :, 0:cols, :] = strips[n : 2 * n].reshape(width, cols, lanes)
    wide[:, cols:, :] = strips[2 * n :].reshape(rows + 2 * width, WIDE - cols, lanes)


def normalize(x):
    center = x - jnp.mean(x, -1, keepdims=True)
    ratio = lax.rsqrt(jnp.mean(center * center, -1, keepdims=True) + EPS)
    return center * ratio, ratio


def normalize_back(x, grad):
    scaled, ratio = normalize(x)
    return (
        grad
        - jnp.mean(grad, -1, keepdims=True)
        - scaled * jnp.mean(grad * scaled, -1, keepdims=True)
    ) * ratio


A0 = 0.7978845608028654
A1 = A0 * 0.044715


def gelu_half(x):
    inner = A0 + A1 * (x * x)
    return inner, 0.5 + 0.5 * jnp.tanh(x * inner)


def gelu(x):
    return x * gelu_half(x)[1]


def gelu_slope(x):
    inner, half = gelu_half(x)
    value = x * half
    return half + (value - value * half) * (6.0 * inner - 4.0 * A0)


def dot(a, b):
    return jnp.dot(a, b, preferred_element_type=F32)


def dot_nt(a, b):
    return lax.dot_general(a, b, (((1,), (1,)), ((), ())), preferred_element_type=F32)


def dot_tn(a, b):
    return lax.dot_general(a, b, (((0,), (0,)), ((), ())), preferred_element_type=F32)


def in_hbm(*arrays):
    return [pltpu.with_memory_space_constraint(a, pltpu.HBM) for a in arrays]


def roll(x, by):
    return pltpu.roll(x, by % x.shape[0], 0)


def expand_kernel(apply, x_ref, we_ref, *refs):
    act_out, normed = refs[-2:]

    @pl.when(pl.program_id(0) == 0)
    def _():
        normed[...] = normalize(x_ref[...].astype(F32))[0].astype(BF)

    for tile in range(0, x_ref.shape[0], 128):
        at = slice(tile, tile + 128)
        act_out[at, :] = apply(dot(normed[at, :], we_ref[...])).astype(BF)


def expand_block(x, w_expand, apply, part, parts, held=None):
    tokens, width = x.shape
    hid = w_expand.shape[1]
    lanes = 512
    steps = hid // lanes // parts
    held = [] if held is None else [held]
    return pl.pallas_call(
        functools.partial(expand_kernel, apply),
        name=apply.__name__ + "_expand",
        grid=(steps,),
        in_specs=[
            pl.BlockSpec((tokens, width), lambda j: (0, 0)),
            pl.BlockSpec((width, lanes), lambda j: (0, j + part * steps)),
            *[pl.BlockSpec(memory_space=pl.ANY) for _ in held],
        ],
        out_specs=pl.BlockSpec((tokens, lanes), lambda j: (0, j + part * steps)),
        out_shape=pltpu.HBM((tokens, hid), BF),
        scratch_shapes=[pltpu.VMEM((tokens, width), BF)],
        input_output_aliases={2: 0} if held else {},
        compiler_params=pltpu.CompilerParams(vmem_limit_bytes=8 * MIB),
        cost_estimate=pl.CostEstimate(
            flops=8 * 512 * 512 * 2048, bytes_accessed=3 * 2**20, transcendentals=2**19
        ),
    )(*in_hbm(x, w_expand), *held)


FORWARD = 512


def forward_kernel(
    x_hbm, strips_ref, go_hbm, act_ref, we_ref, wd_ref, wp_ref,
    mid_out, resid_out, send_out,
    normed, edge, acc, x_ref, go_ref, sems,
):
    step = pl.program_id(0)
    rows, cols = 16, 32
    width = x_ref.shape[1]
    load_x = pltpu.make_async_copy(x_hbm, x_ref, sems.at[0])
    load_go = pltpu.make_async_copy(go_hbm, go_ref, sems.at[1])

    @pl.when(step == 0)
    def _():
        load_x.start()
        load_go.start()
        every = normalize(strips_ref[...].astype(F32))[0]
        sides = 4 * cols + 8
        near = [every[cols : 3 * cols], every[sides : sides + 8 * (rows + 2)]]
        normed[...] = jnp.concatenate(near, 0).astype(BF)

    edge[...] = gelu(dot(normed[...], we_ref[...]))
    for lo in range(0, FORWARD, 128):
        lanes = slice(lo, lo + 128)
        taps = [wd_ref[k : k + 1, lanes].astype(F32) for k in range(9)]

        def line(r):
            if r == 0:
                centre = edge[0:cols, lanes]
            elif r == rows + 1:
                centre = edge[cols : 2 * cols, lanes]
            else:
                centre = act_ref[(r - 1) * cols : r * cols, lanes].astype(F32)
            side = edge[2 * cols + 8 * r : 2 * cols + 8 * (r + 1), lanes]
            whole = jnp.concatenate([centre, side], 0)
            return roll(whole, 1)[0:cols], centre, roll(whole, -1)[0:cols]

        lines = [line(0), line(1)]
        for r in range(rows):
            lines = lines[-2:] + [line(r + 2)]
            conv = sum(lines[k // 3][k % 3] * taps[k] for k in range(9))
            mid_out[r * cols : (r + 1) * cols, lanes] = gelu(conv).astype(BF)
        if lo % 256:
            at = slice(lo - 128, lo + 128)
            part = dot(mid_out[:, at], wp_ref[at, :])
            product = part if lo == 128 else product + part

    @pl.when(step == 0)
    def _():
        acc[...] = product

    @pl.when(step > 0)
    def _():
        acc[...] += product

    @pl.when(step == pl.num_programs(0) - 1)
    def _():
        load_x.wait()
        resid = (x_ref[...].astype(F32) + acc[...]).astype(BF)
        resid_out[...] = resid
        send_out[:, 0:width] = normalize(resid.astype(F32))[0].astype(BF)
        load_go.wait()
        send_out[:, width:] = go_ref[...]


def forward_block(x, strips, go, act, w_expand, w_depthwise, w_project):
    tokens, width = x.shape
    hid = w_expand.shape[1]
    rows, cols = 16, 32
    near = 2 * cols + 8 * (rows + 2)
    anywhere = pl.BlockSpec(memory_space=pl.ANY)
    whole = lambda a: pl.BlockSpec(a.shape, lambda j: (0,) * a.ndim)
    return pl.pallas_call(
        forward_kernel,
        name="mbconv_forward",
        grid=(hid // FORWARD,),
        in_specs=[
            anywhere, whole(strips), anywhere,
            pl.BlockSpec((tokens, FORWARD), lambda j: (0, j)),
            pl.BlockSpec((width, FORWARD), lambda j: (0, j)),
            pl.BlockSpec((9, FORWARD), lambda j: (0, j)),
            pl.BlockSpec((FORWARD, width), lambda j: (j, 0)),
        ],
        out_specs=[
            pl.BlockSpec((tokens, FORWARD), lambda j: (0, j)),
            pl.BlockSpec((tokens, width), lambda j: (0, 0)),
            pl.BlockSpec((tokens, 2 * width), lambda j: (0, 0)),
        ],
        out_shape=[
            pltpu.HBM((tokens, hid), BF),
            pltpu.HBM((tokens, width), BF),
            pltpu.HBM((tokens, 2 * width), BF),
        ],
        scratch_shapes=[
            pltpu.VMEM((near, width), BF),
            pltpu.VMEM((near, FORWARD), F32),
            pltpu.VMEM((tokens, width), F32),
            pltpu.VMEM((tokens, width), BF),
            pltpu.VMEM((tokens, width), BF),
            pltpu.SemaphoreType.DMA((2,)),
        ],
        compiler_params=pltpu.CompilerParams(vmem_limit_bytes=18 * MIB),
        cost_estimate=pl.CostEstimate(
            flops=2 * 700 * 512 * 2048, bytes_accessed=10 * 2**20, transcendentals=2**20
        ),
    )(*in_hbm(x), strips, *in_hbm(go, act, w_expand, w_depthwise, w_project))


SLOPES = 512


def slopes_kernel(
    strips_ref, centre_ref, we_ref, wd_ref, wp_ref,
    act_out, slope_out, resid_out,
    normed, edge, beside, acc,
):
    rows, cols = 16, 32

    @pl.when(pl.program_id(0) == 0)
    def _():
        acc[...] = jnp.zeros(acc.shape, F32)
        normed[...] = normalize(strips_ref[...].astype(F32))[0].astype(BF)

    edge[...] = gelu(dot(normed[...], we_ref[...]))
    for lo in range(0, SLOPES, 128):
        lanes = slice(lo, lo + 128)
        taps = [wd_ref[k : k + 1, lanes].astype(F32) for k in range(9)]

        def line(r):
            if r < 2:
                centre = edge[r * cols : (r + 1) * cols, lanes]
            elif r < rows + 2:
                centre = centre_ref[(r - 2) * cols : (r - 1) * cols, lanes].astype(F32)
            else:
                centre = edge[(r - rows) * cols : (r - rows + 1) * cols, lanes]
            side = edge[4 * cols + 8 * r : 4 * cols + 8 * (r + 1), lanes]
            return jnp.concatenate([centre, side], 0)

        lines = [line(0), line(1)]
        held = None
        for r in range(rows + 2):
            lines = lines[-2:] + [line(r + 2)]
            sums = [sum(lines[i] * taps[3 * i + j] for i in range(3)) for j in range(3)]
            conv = sums[1] + roll(sums[0], 1) + roll(sums[2], -1)
            slope = gelu_slope(conv)
            if 1 <= r <= rows:
                beside[8 * (r - 1) : 8 * r, lanes] = gelu(conv[cols:])
            if r % 2:
                at = slice((r - 1) * WIDE, (r + 1) * WIDE)
                act_out[at, lanes] = jnp.concatenate(lines[:2], 0).astype(BF)
                slope_out[at, lanes] = jnp.concatenate([held, slope], 0).astype(BF)
            held = slope
    acc[...] += dot(beside[...].astype(BF), wp_ref[...])

    @pl.when(pl.program_id(0) == pl.num_programs(0) - 1)
    def _():
        at = 2 * (2 * cols) + 2 * 8
        resid_out[...] = (strips_ref[at : at + 8 * rows, :].astype(F32) + acc[...]).astype(BF)


def slopes_block(strips, centre, w_expand, w_depthwise, w_project):
    tokens, hid = centre.shape
    width = strips.shape[1]
    rows = 16
    wide = (rows + 2) * WIDE
    return pl.pallas_call(
        slopes_kernel,
        name="gelu_slopes",
        grid=(hid // SLOPES,),
        in_specs=[
            pl.BlockSpec(strips.shape, lambda j: (0, 0)),
            pl.BlockSpec((tokens, SLOPES), lambda j: (0, j)),
            pl.BlockSpec((width, SLOPES), lambda j: (0, j)),
            pl.BlockSpec((9, SLOPES), lambda j: (0, j)),
            pl.BlockSpec((SLOPES, width), lambda j: (j, 0)),
        ],
        out_specs=[
            pl.BlockSpec((wide, SLOPES), lambda j: (0, j)),
            pl.BlockSpec((wide, SLOPES), lambda j: (0, j)),
            pl.BlockSpec((8 * rows, width), lambda j: (0, 0)),
        ],
        out_shape=[
            pltpu.HBM((wide, hid), BF),
            pltpu.HBM((wide, hid), BF),
            pltpu.HBM((8 * rows, width), BF),
        ],
        scratch_shapes=[
            pltpu.VMEM(strips.shape, BF),
            pltpu.VMEM((strips.shape[0], SLOPES), F32),
            pltpu.VMEM((8 * rows, SLOPES), F32),
            pltpu.VMEM((8 * rows, width), F32),
        ],
        compiler_params=pltpu.CompilerParams(vmem_limit_bytes=18 * MIB),
        cost_estimate=pl.CostEstimate(
            flops=2 * 10**10, bytes_accessed=12 * 2**20, transcendentals=3 * 2**20
        ),
    )(strips, *in_hbm(centre, w_expand, w_depthwise, w_project))


def attention_kernel(
    col_ref, in_ref, wq_hbm, wo_hbm, send_hbm, gq_hbm, att_hbm,
    wq, wo, qkv, gatt, att, gq, send, gqb, attended, edge, sems,
):
    tokens, width = attended.shape
    groups = 8
    members = tokens // groups
    quads = width // 128
    scale = HDIM ** (-0.5)
    load_wo = pltpu.make_async_copy(wo_hbm, wo, sems.at[0])
    load_wq = pltpu.make_async_copy(wq_hbm, wq, sems.at[1])
    load_wo.start()
    load_wq.start()

    def put(ref, at, value):
        value = value.astype(BF).astype(F32)
        for quad in range(quads):
            ref[at + quad] = value[:, quad * 128 : (quad + 1) * 128]

    load_wo.wait()
    put(gatt, 0, dot_nt(in_ref[:, width:], wo[...]))
    load_wq.wait()
    for part in range(3):
        lanes = slice(part * width, (part + 1) * width)
        put(qkv, part * quads, dot(in_ref[:, 0:width], wq[:, lanes]))
    per = 128 // HDIM
    head = lax.broadcasted_iota(jnp.int32, (members, 128), 1) // HDIM

    def spread(v):
        return jnp.concatenate([jnp.where(head == h, v, 0.0) for h in range(per)], 0).astype(BF)

    def gather(v):
        out = jnp.where(head == 0, v[0:members], 0.0)
        for h in range(1, per):
            out = jnp.where(head == h, v[h * members : (h + 1) * members], out)
        return out

    def one_group(g, _):
        at = pl.ds(g, members, stride=groups)
        every = range(quads)
        q = [spread(qkv[i, at, :]) for i in every]
        k = [qkv[quads + i, at, :].astype(BF) for i in every]
        v = [qkv[2 * quads + i, at, :].astype(BF) for i in every]
        do = [spread(gatt[i, at, :]) for i in every]
        scores = [dot_nt(k[i], q[i]) * scale for i in every]
        dp = [dot_nt(v[i], do[i]) for i in every]
        p = [jnp.exp(s - jnp.max(s, 0, keepdims=True)) for s in scores]
        p = [e * (1.0 / jnp.sum(e, 0, keepdims=True)) for e in p]
        pb = [e.astype(BF) for e in p]
        ds = [
            (p[i] * (dp[i] - jnp.sum(p[i] * dp[i], 0, keepdims=True)) * scale).astype(BF)
            for i in every
        ]
        for i in every:
            att[i, at, :] = gather(dot_tn(pb[i], v[i]))
            gq[i, at, :] = gather(dot_tn(ds[i], k[i]))
            gq[quads + i, at, :] = dot(ds[i], q[i])
            gq[2 * quads + i, at, :] = dot(pb[i], do[i])
        return 0

    lax.fori_loop(0, groups, one_group, 0)
    attended[...] = jnp.concatenate([att[i] for i in range(quads)], 1).astype(BF)
    store_att = pltpu.make_async_copy(attended, att_hbm, sems.at[2])
    store_att.start()
    gqb[...] = jnp.concatenate([gq[i] for i in range(3 * quads)], 1).astype(BF)
    store_gq = pltpu.make_async_copy(gqb, gq_hbm, sems.at[3])
    store_gq.start()
    grad = dot_nt(gqb[...], wq[...])
    send[:, width : 2 * width] = grad.astype(BF)
    put(gatt, 0, grad)
    place = lax.broadcasted_iota(jnp.int32, (members, 128), 0) % 8
    last = col_ref[0] % 4 == 3
    for i in range(quads):
        first_col = gatt[i, pl.ds(0, members, stride=groups), :]
        last_col = gatt[i, pl.ds(groups - 1, members, stride=groups), :]
        to_left = jnp.where(place == 7, 0.0, roll(first_col, -1))
        to_right = jnp.where(place == 0, 0.0, roll(last_col, 1))
        found = jnp.where(last, to_right, to_left)
        edge[pl.ds(2 * i, members, stride=groups), :] = found
        edge[pl.ds(2 * i + 1, members, stride=groups), :] = pltpu.roll(found, 64, 1)
    send[:, 2 * width :] = edge[...].astype(BF)
    send[:, 0:width] = dot(attended[...], wo[...]).astype(BF)
    store_send = pltpu.make_async_copy(send, send_hbm, sems.at[4])
    store_send.start()
    for store in [store_att, store_gq, store_send]:
        store.wait()


def attention_block(col, arrived, w_qkv, w_out):
    tokens = arrived.shape[0]
    width = w_out.shape[0]
    anywhere = pl.BlockSpec(memory_space=pl.ANY)
    return pl.pallas_call(
        attention_kernel,
        name="grid_attention",
        in_specs=[
            pl.BlockSpec(memory_space=pltpu.SMEM), pl.BlockSpec(memory_space=pltpu.VMEM), anywhere, anywhere
        ],
        out_specs=[anywhere] * 3,
        out_shape=[
            pltpu.HBM((tokens, 2 * width + 128), BF),
            pltpu.HBM((tokens, 3 * width), BF),
            pltpu.HBM((tokens, width), BF),
        ],
        scratch_shapes=[
            pltpu.VMEM((width, 3 * width), BF),
            pltpu.VMEM((width, width), BF),
            pltpu.VMEM((3 * width // 128, tokens, 128), F32),
            pltpu.VMEM((width // 128, tokens, 128), F32),
            pltpu.VMEM((width // 128, tokens, 128), F32),
            pltpu.VMEM((3 * width // 128, tokens, 128), F32),
            pltpu.VMEM((tokens, 2 * width + 128), BF),
            pltpu.VMEM((tokens, 3 * width), BF),
            pltpu.VMEM((tokens, width), BF),
            pltpu.VMEM((tokens, 128), F32),
            pltpu.SemaphoreType.DMA((5,)),
        ],
        compiler_params=pltpu.CompilerParams(vmem_limit_bytes=24 * MIB),
        cost_estimate=pl.CostEstimate(
            flops=2 * 512 * 512 * 512 * 8, bytes_accessed=7 * 2**20, transcendentals=2**20
        ),
    )(col, arrived, *in_hbm(w_qkv, w_out))


def residual_kernel(
    home_ref, resid_ref, go_ref, resid_s_ref, go_s_ref, out_ref, gr_ref, side_out, first_out, last_out,
    packed, side,
):
    tokens, width = resid_ref.shape
    rows, cols = 16, 32
    resid = resid_ref[...].astype(F32)
    out_ref[...] = (resid + home_ref[:, 0:width].astype(F32)).astype(BF)
    back = normalize_back(resid, home_ref[:, width : 2 * width].astype(F32))
    gr = (go_ref[...].astype(F32) + back).astype(BF)
    gr_ref[...] = gr
    packed[...] = home_ref[:, 2 * width :].astype(F32)
    side[...] = jnp.zeros(side.shape, F32)
    low = lax.broadcasted_iota(jnp.int32, (rows, 128), 1) < 64
    for i in range(width // 128):
        for at, start in ((0, 0), (7, cols - 8)):
            even = packed[pl.ds(start + 2 * i, rows, stride=cols), :]
            odd = packed[pl.ds(start + 2 * i + 1, rows, stride=cols), :]
            side[i, pl.ds(at, rows, stride=8), :] = jnp.where(low, even, pltpu.roll(odd, 64, 1))
    grad = jnp.concatenate([side[i] for i in range(width // 128)], 1)
    back = normalize_back(resid_s_ref[...].astype(F32), grad)
    gr_s = (go_s_ref[...].astype(F32) + back).astype(BF).astype(F32)
    side_out[...] = gr_s.astype(BF)
    none = jnp.zeros((8, width), F32)
    own = gr.astype(F32)
    first_out[...] = jnp.concatenate([own[0:cols], gr_s[0:8], none], 0).astype(BF)
    last_out[...] = jnp.concatenate([own[tokens - cols :], gr_s[8 * rows - 8 :], none], 0).astype(BF)


def residual_block(home, resid, go, resid_s, go_s):
    tokens, width = resid.shape
    beside = resid_s.shape[0]
    shapes = [(tokens, width), (tokens, width), (beside, width), (48, width), (48, width)]
    return pl.pallas_call(
        residual_kernel,
        name="residual",
        out_shape=[jax.ShapeDtypeStruct(shape, BF) for shape in shapes],
        scratch_shapes=[
            pltpu.VMEM((tokens, 128), F32),
            pltpu.VMEM((width // 128, beside, 128), F32),
        ],
        compiler_params=pltpu.CompilerParams(vmem_limit_bytes=12 * MIB),
    )(home, *in_hbm(resid, go, resid_s), go_s)


def split_by_core(core, full, mine_out, other_out):
    half = 128
    for j in range(full.shape[0] // (2 * half)):
        at = slice(j * half, (j + 1) * half)
        own = pl.multiple_of((2 * j + core) * half, half)
        other = pl.multiple_of((2 * j + 1 - core) * half, half)
        mine_out[at, :] = full[pl.ds(own, half), :]
        other_out[at, :] = full[pl.ds(other, half), :].astype(BF)


def backward_kernel(
    core_ref, x_ref, gr_ref, above_ref, below_ref, side_ref, act_ref, slope_c_ref, slope_e_ref,
    wd_ref, wp_ref,
    gpre, mine_out, other_out,
    wide, grad_wide, normed, gmid, act, full, taps_t,
):
    step = pl.program_id(0)
    rows, cols = 16, 32
    width = x_ref.shape[1]

    @pl.when(step == 0)
    def _():
        wide[0] = above_ref[0:WIDE, :].astype(F32)
        wide[rows + 1] = below_ref[0:WIDE, :].astype(F32)
        wide[1 : 1 + rows, 0:cols, :] = gr_ref[...].astype(F32).reshape(rows, cols, width)
        wide[1 : 1 + rows, cols:, :] = side_ref[...].astype(F32).reshape(rows, 8, width)
        grad_wide[...] = wide[...].reshape(grad_wide.shape).astype(BF)
        normed[...] = normalize(x_ref[...].astype(F32))[0].astype(BF)
        taps_t[...] = jnp.zeros(taps_t.shape, F32)

    gm = dot_nt(grad_wide[...], wp_ref[...]) * slope_c_ref[...].astype(F32)
    gmid[...] = gm.reshape(gmid.shape)
    act[...] = act_ref[...].astype(F32).reshape(act.shape)
    inside = lax.broadcasted_iota(jnp.int32, (WIDE, 128), 0) < cols
    for lo in range(0, CHUNK, 128):
        lanes = slice(lo, lo + 128)
        taps = [wd_ref[k : k + 1, lanes].astype(F32) for k in range(9)]
        sums = [None] * 9
        grads = [gmid[0, :, lanes], gmid[1, :, lanes]]
        acts = [act[0, :, lanes], act[1, :, lanes]]
        for r in range(rows):
            grads = grads[-2:] + [gmid[r + 2, :, lanes]]
            acts = acts[-2:] + [act[r + 2, :, lanes]]
            parts = [sum(grads[2 - i] * taps[3 * i + j] for i in range(3)) for j in range(3)]
            grad_act = parts[1] + roll(parts[0], -1) + roll(parts[2], 1)
            at = slice(r * cols, (r + 1) * cols)
            gpre[at, lanes] = (grad_act[0:cols] * slope_e_ref[at, lanes].astype(F32)).astype(BF)
            own = jnp.where(inside, grads[1], 0.0)
            moved = [roll(own, -1), own, roll(own, 1)]
            for k in range(9):
                prod = jnp.sum((acts[k // 3] * moved[k % 3]).reshape(WIDE // 8, 8, 128), 0)
                sums[k] = prod if r == 0 else sums[k] + prod
        for k in range(9):
            taps_t[k : k + 1, lanes] = jnp.sum(sums[k], 0, keepdims=True)
    full[:, 0:width] = dot_tn(gpre[...], normed[...])
    full[:, width:] = taps_t[...].T
    split_by_core(core_ref[0], full, mine_out, other_out)


def backward_block(core, x, gr, near, act, slope_c, slope_e, w_depthwise, w_project):
    tokens, width = x.shape
    hid = w_project.shape[0]
    rows, cols = 16, 32
    whole = lambda a: pl.BlockSpec(a.shape, lambda j, c: (0,) * a.ndim)
    return pl.pallas_call(
        backward_kernel,
        name="mbconv_backward",
        grid_spec=pltpu.PrefetchScalarGridSpec(
            num_scalar_prefetch=1,
            grid=(hid // CHUNK,),
            in_specs=[
                whole(x), whole(gr), *[whole(a) for a in near],
                pl.BlockSpec(((rows + 2) * WIDE, CHUNK), lambda j, c: (0, j)),
                pl.BlockSpec(((rows + 2) * WIDE, CHUNK), lambda j, c: (0, j)),
                pl.BlockSpec((tokens, CHUNK), lambda j, c: (0, j)),
                pl.BlockSpec((9, CHUNK), lambda j, c: (0, j)),
                pl.BlockSpec((CHUNK, width), lambda j, c: (j, 0)),
            ],
            out_specs=[
                pl.BlockSpec((tokens, CHUNK), lambda j, c: (0, j)),
                pl.BlockSpec((CHUNK // 2, width + 128), lambda j, c: (j, 0)),
                pl.BlockSpec((CHUNK // 2, width + 128), lambda j, c: (j, 0)),
            ],
            scratch_shapes=[
                pltpu.VMEM((rows + 2, WIDE, width), F32),
                pltpu.VMEM(((rows + 2) * WIDE, width), BF),
                pltpu.VMEM((tokens, width), BF),
                pltpu.VMEM((rows + 2, WIDE, CHUNK), F32),
                pltpu.VMEM((rows + 2, WIDE, CHUNK), F32),
                pltpu.VMEM((CHUNK, width + 128), F32),
                pltpu.VMEM((128, CHUNK), F32),
            ],
        ),
        out_shape=[
            pltpu.HBM((tokens, hid), BF),
            jax.ShapeDtypeStruct((hid // 2, width + 128), F32),
            jax.ShapeDtypeStruct((hid // 2, width + 128), BF),
        ],
        compiler_params=pltpu.CompilerParams(vmem_limit_bytes=18 * MIB),
        cost_estimate=pl.CostEstimate(
            flops=16 * 512 * 512 * 2048, bytes_accessed=20 * 2**20, transcendentals=2**20
        ),
    )(core, *in_hbm(x), gr, *near, *in_hbm(act, slope_c, slope_e, w_depthwise, w_project))


def input_kernel(gpre_ref, we_ref, x_ref, gr_ref, gx_out):
    back = normalize_back(x_ref[...].astype(F32), dot_nt(gpre_ref[...], we_ref[...]))
    gx_out[...] = (gr_ref[...].astype(F32) + back).astype(BF)


def input_grads(gpre, w_expand, x, gr):
    tokens, width = x.shape
    hid = w_expand.shape[1]
    tile = 128
    return pl.pallas_call(
        input_kernel,
        name="grad_input",
        grid=(tokens // tile,),
        in_specs=[
            pl.BlockSpec((tile, hid), lambda i: (i, 0)),
            pl.BlockSpec((width, hid), lambda i: (0, 0)),
            pl.BlockSpec((tile, width), lambda i: (i, 0)),
            pl.BlockSpec((tile, width), lambda i: (i, 0)),
        ],
        out_specs=pl.BlockSpec((tile, width), lambda i: (i, 0)),
        out_shape=jax.ShapeDtypeStruct((tokens, width), BF),
        compiler_params=pltpu.CompilerParams(vmem_limit_bytes=12 * MIB),
        cost_estimate=pl.CostEstimate(
            flops=4 * 512 * 512 * 2048, bytes_accessed=6 * 2**20, transcendentals=0
        ),
    )(*in_hbm(gpre, w_expand, x, gr))


def finish_kernel(parts_ref, expand_out, depth_out):
    total = jnp.sum(parts_ref[...].astype(F32), 0)
    own, width = expand_out.shape
    expand_out[...] = total[:, 0:width]
    square = jnp.concatenate([total[:, width:], jnp.zeros((128 - own, 128), F32)], 0)
    depth_out[...] = square.T[0:9, 0:own]


def finish(parts):
    _, own, lanes = parts.shape
    return pl.pallas_call(
        finish_kernel,
        name="last_sum",
        out_shape=[
            pltpu.HBM((own, lanes - 128), F32),
            pltpu.HBM((9, own), F32),
        ],
        compiler_params=pltpu.CompilerParams(vmem_limit_bytes=10 * MIB),
    )(parts)


def project_kernel(core_ref, mid_ref, gr_ref, mine_out, other_out, full):
    full[...] = dot_tn(mid_ref[...], gr_ref[...])
    split_by_core(core_ref[0], full, mine_out, other_out)


def project_grads(core, mid, gr):
    tokens, hid = mid.shape
    width = gr.shape[1]
    lanes = 512
    return pl.pallas_call(
        project_kernel,
        name="grad_project",
        grid_spec=pltpu.PrefetchScalarGridSpec(
            num_scalar_prefetch=1,
            grid=(hid // lanes,),
            in_specs=[
                pl.BlockSpec((tokens, lanes), lambda j, c: (0, j)),
                pl.BlockSpec((tokens, width), lambda j, c: (0, 0)),
            ],
            out_specs=[pl.BlockSpec((lanes // 2, width), lambda j, c: (j, 0))] * 2,
            scratch_shapes=[pltpu.VMEM((lanes, width), F32)],
        ),
        out_shape=[
            jax.ShapeDtypeStruct((hid // 2, width), F32),
            jax.ShapeDtypeStruct((hid // 2, width), BF),
        ],
        compiler_params=pltpu.CompilerParams(vmem_limit_bytes=8 * MIB),
        cost_estimate=pl.CostEstimate(
            flops=2 * 512 * 512 * 2048, bytes_accessed=7 * 2**20, transcendentals=0
        ),
    )(core, *in_hbm(mid), gr)


def attention_grads_kernel(
    core_ref, arrived_ref, gqkv_ref, att_ref, mine_out, other_out, qkv, outp, half_q, half_o, full
):
    width = att_ref.shape[1]
    qkv[...] = dot_tn(gqkv_ref[...], arrived_ref[:, 0:width])
    outp[...] = dot_tn(arrived_ref[:, width:], att_ref[...])
    nq, no = qkv.shape[0] // 16, outp.shape[0] // 16
    for j in range(8):
        for own in (True, False):
            core = core_ref[0] if own else 1 - core_ref[0]
            half_q[...] = qkv[pl.ds(pl.multiple_of((2 * j + core) * nq, 8), nq), :]
            half_o[...] = outp[pl.ds(pl.multiple_of((2 * j + core) * no, 8), no), :]
            for k in range(8):
                full[16 * k : 16 * k + 12, :] = half_q[12 * k : 12 * k + 12, :]
                full[16 * k + 12 : 16 * k + 16, :] = half_o[4 * k : 4 * k + 4, :]
            at = slice(128 * j, 128 * j + 128)
            if own:
                mine_out[at, :] = full[...]
            else:
                other_out[at, :] = full[...].astype(BF)


def attention_grads(core, arrived, gqkv, attended):
    tokens, width = attended.shape
    vmem = pl.BlockSpec(memory_space=pltpu.VMEM)
    return pl.pallas_call(
        attention_grads_kernel,
        name="attention_grads",
        in_specs=[pl.BlockSpec(memory_space=pltpu.SMEM), vmem, vmem, vmem],
        out_specs=[vmem, vmem],
        out_shape=[
            jax.ShapeDtypeStruct((1024, width), F32),
            jax.ShapeDtypeStruct((1024, width), BF),
        ],
        scratch_shapes=[
            pltpu.VMEM((3 * width, width), F32),
            pltpu.VMEM((width, width), F32),
            pltpu.VMEM((96, width), F32),
            pltpu.VMEM((32, width), F32),
            pltpu.VMEM((128, width), F32),
        ],
        compiler_params=pltpu.CompilerParams(vmem_limit_bytes=14 * MIB),
        cost_estimate=pl.CostEstimate(
            flops=8 * 512 * 512 * 512, bytes_accessed=8 * 2**20, transcendentals=0
        ),
    )(core, *in_hbm(arrived, gqkv, attended))


def add_pair(mine, other):
    got = lax.ppermute(other, AX, other_core())
    return (mine + got.astype(F32)).astype(BF).reshape(64, 16, -1)


def body(block_input, w_expand, w_depthwise, w_project, w_qkv, w_out, grad_out):
    _, rows, cols, width = block_input.shape
    tokens = rows * cols
    core = (lax.axis_index("row") % 2).astype(jnp.int32).reshape(1)
    col = lax.axis_index("col").astype(jnp.int32).reshape(1)
    image = block_input[0]
    x = image.reshape(tokens, width)
    go = grad_out[0].reshape(tokens, width)
    act0 = expand_block(x, w_expand, gelu, 0, 2)
    centre = expand_block(x, w_expand, gelu, 1, 2, act0)
    strips, go_side = halo(image, 2, act0, grad_out[0])
    mid, resid, send = forward_block(x, strips, go, centre, w_expand, w_depthwise, w_project)
    arrived = across_chips(send.reshape(64, 8, 2 * width)).reshape(tokens, 2 * width)
    slopes = slopes_block(strips, centre, w_expand, w_depthwise, w_project)
    arrived, (act, slope_c, resid_side) = lax.optimization_barrier((arrived, slopes))
    back, gqkv, attended = attention_block(col, arrived, w_qkv, w_out)
    home = across_chips(back.reshape(64, 8, -1)).reshape(tokens, -1)
    slope_e = expand_block(x, w_expand, gelu_slope, 0, 1)
    home, slope_e = lax.optimization_barrier((home, slope_e))
    attention_pair = add_pair(*attention_grads(core, arrived, gqkv, attended))
    out, gr, side, first_row, last_row = residual_block(home, resid, go, resid_side, go_side)
    above, below = shift(last_row, "row", 1), shift(first_row, "row", -1)
    project_pair = add_pair(*project_grads(core, mid, gr))
    first = jnp.concatenate([project_pair, attention_pair], 1)
    above, below, first = lax.optimization_barrier((above, below, first))
    first = across_chips(first)
    gpre, mine, other = backward_block(
        core, x, gr, (above, below, side), act, slope_c, slope_e, w_depthwise, w_project
    )
    gx = input_grads(gpre, w_expand, x, gr)
    second = add_pair(mine, other)
    second, first = lax.optimization_barrier((second, first))
    grad_expand, grad_depth = finish(across_chips(second))
    first = jnp.sum(first.astype(F32), 0)
    return (
        out.reshape(1, rows, cols, width),
        gx.reshape(1, rows, cols, width),
        grad_expand.T,
        grad_depth,
        first[:16].T,
        first[16:28].T,
        first[28:].T,
    )


def solution(mesh):
    tokens = P(None, "row", "col", None)
    split = P(None, AX)
    return jax.shard_map(
        body,
        mesh=mesh,
        in_specs=(tokens, P(), P(), P(), P(), P(), tokens),
        out_specs=(tokens, tokens, split, split, split, split, split),
        check_vma=False,
    )
```

```python
import functools
import itertools

import jax
import jax.numpy as jnp
from jax import lax
from jax.experimental import pallas as pl
from jax.experimental.pallas import tpu as pltpu
from jax.sharding import PartitionSpec as P

HEADS = 16
HDIM = 32
EPS = 1e-05
BF = jnp.bfloat16
F32 = jnp.float32
AX = ("row", "col")
WIDE = 40
CHUNK = 256
MIB = 2**20

SIZES = dict(y_lo=2, z=4, core=2, x=4, y_hi=2)
STRIDES = dict(y_lo=64, z=16, core=8, x=2, y_hi=1)
CHIPS = ("y_lo", "z", "x", "y_hi")


def device_groups(axes):
    rest = [a for a in SIZES if a not in axes]
    found = []
    for at in itertools.product(*[range(SIZES[a]) for a in rest]):
        base = sum(v * STRIDES[a] for v, a in zip(at, rest))
        found.append(
            [
                base + sum(v * STRIDES[a] for v, a in zip(m, axes))
                for m in itertools.product(*[range(SIZES[a]) for a in axes])
            ]
        )
    return found


def other_core():
    return [(d, d ^ STRIDES["core"]) for d in range(128)]


def across_chips(x):
    return lax.all_to_all(x, AX, 0, 0, tiled=True, axis_index_groups=device_groups(CHIPS))


def shift(x, axis, step):
    n = lax.axis_size(axis)
    pairs = [(i, i + step) for i in range(n) if 0 <= i + step < n]
    return lax.ppermute(x, axis, pairs)


def halo(x, width, ahead, beside):
    rows, cols, chans = x.shape
    above = shift(x[rows - width :], "row", 1)
    below = shift(x[:width], "row", -1)
    above, below, _ = lax.optimization_barrier((above, below, ahead))
    flat = lambda v: v.reshape(-1, chans)

    def column(at):
        parts = [above[:, at], x[:, at], below[:, at], beside[:, at]]
        return jnp.concatenate([flat(p) for p in parts], 0)

    left = shift(column(slice(cols - width, cols)), "col", 1)
    right = shift(column(slice(0, width)), "col", -1)
    n = (rows + 2 * width) * width

    def sides(right, left):
        right, left = [v.reshape(-1, width, chans) for v in (right, left)]
        gap = jnp.zeros((right.shape[0], 8 - 2 * width, chans), x.dtype)
        return flat(jnp.concatenate([right, gap, left], 1))

    strips = [flat(above), flat(below), sides(right[:n], left[:n])]
    return jnp.concatenate(strips, 0), sides(right[n:], left[n:])


def place(wide, centre, strips, width, rows, cols):
    lanes = strips.shape[-1]
    n = width * cols
    if centre is not None:
        wide[width : width + rows, 0:cols, :] = centre.reshape(rows, cols, lanes)
    wide[0:width, 0:cols, :] = strips[0:n].reshape(width, cols, lanes)
    wide[width + rows :, 0:cols, :] = strips[n : 2 * n].reshape(width, cols, lanes)
    wide[:, cols:, :] = strips[2 * n :].reshape(rows + 2 * width, WIDE - cols, lanes)


def normalize(x):
    center = x - jnp.mean(x, -1, keepdims=True)
    ratio = lax.rsqrt(jnp.mean(center * center, -1, keepdims=True) + EPS)
    return center * ratio, ratio


def normalize_back(x, grad):
    scaled, ratio = normalize(x)
    return (
        grad
        - jnp.mean(grad, -1, keepdims=True)
        - scaled * jnp.mean(grad * scaled, -1, keepdims=True)
    ) * ratio


A0 = 0.7978845608028654
A1 = A0 * 0.044715


def gelu_half(x):
    inner = A0 + A1 * (x * x)
    return inner, 0.5 + 0.5 * jnp.tanh(x * inner)


def gelu(x):
    return x * gelu_half(x)[1]


def gelu_slope(x):
    inner, half = gelu_half(x)
    value = x * half
    return half + (value - value * half) * (6.0 * inner - 4.0 * A0)


def dot(a, b):
    return jnp.dot(a, b, preferred_element_type=F32)


def dot_nt(a, b):
    return lax.dot_general(a, b, (((1,), (1,)), ((), ())), preferred_element_type=F32)


def dot_tn(a, b):
    return lax.dot_general(a, b, (((0,), (0,)), ((), ())), preferred_element_type=F32)


def in_hbm(*arrays):
    return [pltpu.with_memory_space_constraint(a, pltpu.HBM) for a in arrays]


def roll(x, by):
    return pltpu.roll(x, by % x.shape[0], 0)


def expand_kernel(apply, x_ref, we_ref, *refs):
    act_out, normed = refs[-2:]

    @pl.when(pl.program_id(0) == 0)
    def _():
        normed[...] = normalize(x_ref[...].astype(F32))[0].astype(BF)

    for tile in range(0, x_ref.shape[0], 128):
        at = slice(tile, tile + 128)
        act_out[at, :] = apply(dot(normed[at, :], we_ref[...])).astype(BF)


def expand_block(x, w_expand, apply, part, parts, held=None):
    tokens, width = x.shape
    hid = w_expand.shape[1]
    lanes = 512
    steps = hid // lanes // parts
    held = [] if held is None else [held]
    return pl.pallas_call(
        functools.partial(expand_kernel, apply),
        name=apply.__name__ + "_expand",
        grid=(steps,),
        in_specs=[
            pl.BlockSpec((tokens, width), lambda j: (0, 0)),
            pl.BlockSpec((width, lanes), lambda j: (0, j + part * steps)),
            *[pl.BlockSpec(memory_space=pl.ANY) for _ in held],
        ],
        out_specs=pl.BlockSpec((tokens, lanes), lambda j: (0, j + part * steps)),
        out_shape=pltpu.HBM((tokens, hid), BF),
        scratch_shapes=[pltpu.VMEM((tokens, width), BF)],
        input_output_aliases={2: 0} if held else {},
        compiler_params=pltpu.CompilerParams(vmem_limit_bytes=8 * MIB),
        cost_estimate=pl.CostEstimate(
            flops=8 * 512 * 512 * 2048, bytes_accessed=3 * 2**20, transcendentals=2**19
        ),
    )(*in_hbm(x, w_expand), *held)


FORWARD = 512


def forward_kernel(
    x_hbm, strips_ref, go_hbm, act_ref, we_ref, wd_ref, wp_ref,
    mid_out, resid_out, send_out,
    normed, edge, acc, x_ref, go_ref, sems,
):
    step = pl.program_id(0)
    rows, cols = 16, 32
    width = x_ref.shape[1]
    load_x = pltpu.make_async_copy(x_hbm, x_ref, sems.at[0])
    load_go = pltpu.make_async_copy(go_hbm, go_ref, sems.at[1])

    @pl.when(step == 0)
    def _():
        load_x.start()
        load_go.start()
        every = normalize(strips_ref[...].astype(F32))[0]
        sides = 4 * cols + 8
        near = [every[cols : 3 * cols], every[sides : sides + 8 * (rows + 2)]]
        normed[...] = jnp.concatenate(near, 0).astype(BF)

    edge[...] = gelu(dot(normed[...], we_ref[...]))
    for lo in range(0, FORWARD, 128):
        lanes = slice(lo, lo + 128)
        taps = [wd_ref[k : k + 1, lanes].astype(F32) for k in range(9)]

        def line(r):
            if r == 0:
                centre = edge[0:cols, lanes]
            elif r == rows + 1:
                centre = edge[cols : 2 * cols, lanes]
            else:
                centre = act_ref[(r - 1) * cols : r * cols, lanes].astype(F32)
            side = edge[2 * cols + 8 * r : 2 * cols + 8 * (r + 1), lanes]
            whole = jnp.concatenate([centre, side], 0)
            return roll(whole, 1)[0:cols], centre, roll(whole, -1)[0:cols]

        lines = [line(0), line(1)]
        for r in range(rows):
            lines = lines[-2:] + [line(r + 2)]
            conv = sum(lines[k // 3][k % 3] * taps[k] for k in range(9))
            mid_out[r * cols : (r + 1) * cols, lanes] = gelu(conv).astype(BF)
        if lo % 256:
            at = slice(lo - 128, lo + 128)
            part = dot(mid_out[:, at], wp_ref[at, :])
            product = part if lo == 128 else product + part

    @pl.when(step == 0)
    def _():
        acc[...] = product

    @pl.when(step > 0)
    def _():
        acc[...] += product

    @pl.when(step == pl.num_programs(0) - 1)
    def _():
        load_x.wait()
        resid = (x_ref[...].astype(F32) + acc[...]).astype(BF)
        resid_out[...] = resid
        send_out[:, 0:width] = normalize(resid.astype(F32))[0].astype(BF)
        load_go.wait()
        send_out[:, width:] = go_ref[...]


def forward_block(x, strips, go, act, w_expand, w_depthwise, w_project):
    tokens, width = x.shape
    hid = w_expand.shape[1]
    rows, cols = 16, 32
    near = 2 * cols + 8 * (rows + 2)
    anywhere = pl.BlockSpec(memory_space=pl.ANY)
    whole = lambda a: pl.BlockSpec(a.shape, lambda j: (0,) * a.ndim)
    return pl.pallas_call(
        forward_kernel,
        name="mbconv_forward",
        grid=(hid // FORWARD,),
        in_specs=[
            anywhere, whole(strips), anywhere,
            pl.BlockSpec((tokens, FORWARD), lambda j: (0, j)),
            pl.BlockSpec((width, FORWARD), lambda j: (0, j)),
            pl.BlockSpec((9, FORWARD), lambda j: (0, j)),
            pl.BlockSpec((FORWARD, width), lambda j: (j, 0)),
        ],
        out_specs=[
            pl.BlockSpec((tokens, FORWARD), lambda j: (0, j)),
            pl.BlockSpec((tokens, width), lambda j: (0, 0)),
            pl.BlockSpec((tokens, 2 * width), lambda j: (0, 0)),
        ],
        out_shape=[
            pltpu.HBM((tokens, hid), BF),
            pltpu.HBM((tokens, width), BF),
            pltpu.HBM((tokens, 2 * width), BF),
        ],
        scratch_shapes=[
            pltpu.VMEM((near, width), BF),
            pltpu.VMEM((near, FORWARD), F32),
            pltpu.VMEM((tokens, width), F32),
            pltpu.VMEM((tokens, width), BF),
            pltpu.VMEM((tokens, width), BF),
            pltpu.SemaphoreType.DMA((2,)),
        ],
        compiler_params=pltpu.CompilerParams(vmem_limit_bytes=18 * MIB),
        cost_estimate=pl.CostEstimate(
            flops=2 * 700 * 512 * 2048, bytes_accessed=10 * 2**20, transcendentals=2**20
        ),
    )(*in_hbm(x), strips, *in_hbm(go, act, w_expand, w_depthwise, w_project))


SLOPES = 512


def slopes_kernel(
    strips_ref, centre_ref, we_ref, wd_ref, wp_ref,
    act_out, slope_out, resid_out,
    normed, edge, beside, acc,
):
    rows, cols = 16, 32

    @pl.when(pl.program_id(0) == 0)
    def _():
        acc[...] = jnp.zeros(acc.shape, F32)
        normed[...] = normalize(strips_ref[...].astype(F32))[0].astype(BF)

    edge[...] = gelu(dot(normed[...], we_ref[...]))
    for lo in range(0, SLOPES, 128):
        lanes = slice(lo, lo + 128)
        taps = [wd_ref[k : k + 1, lanes].astype(F32) for k in range(9)]

        def line(r):
            if r < 2:
                centre = edge[r * cols : (r + 1) * cols, lanes]
            elif r < rows + 2:
                centre = centre_ref[(r - 2) * cols : (r - 1) * cols, lanes].astype(F32)
            else:
                centre = edge[(r - rows) * cols : (r - rows + 1) * cols, lanes]
            side = edge[4 * cols + 8 * r : 4 * cols + 8 * (r + 1), lanes]
            return jnp.concatenate([centre, side], 0)

        lines = [line(0), line(1)]
        held = None
        for r in range(rows + 2):
            lines = lines[-2:] + [line(r + 2)]
            sums = [sum(lines[i] * taps[3 * i + j] for i in range(3)) for j in range(3)]
            conv = sums[1] + roll(sums[0], 1) + roll(sums[2], -1)
            slope = gelu_slope(conv)
            if 1 <= r <= rows:
                beside[8 * (r - 1) : 8 * r, lanes] = gelu(conv[cols:])
            if r % 2:
                at = slice((r - 1) * WIDE, (r + 1) * WIDE)
                act_out[at, lanes] = jnp.concatenate(lines[:2], 0).astype(BF)
                slope_out[at, lanes] = jnp.concatenate([held, slope], 0).astype(BF)
            held = slope
    acc[...] += dot(beside[...].astype(BF), wp_ref[...])

    @pl.when(pl.program_id(0) == pl.num_programs(0) - 1)
    def _():
        at = 2 * (2 * cols) + 2 * 8
        resid_out[...] = (strips_ref[at : at + 8 * rows, :].astype(F32) + acc[...]).astype(BF)


def slopes_block(strips, centre, w_expand, w_depthwise, w_project):
    tokens, hid = centre.shape
    width = strips.shape[1]
    rows = 16
    wide = (rows + 2) * WIDE
    return pl.pallas_call(
        slopes_kernel,
        name="gelu_slopes",
        grid=(hid // SLOPES,),
        in_specs=[
            pl.BlockSpec(strips.shape, lambda j: (0, 0)),
            pl.BlockSpec((tokens, SLOPES), lambda j: (0, j)),
            pl.BlockSpec((width, SLOPES), lambda j: (0, j)),
            pl.BlockSpec((9, SLOPES), lambda j: (0, j)),
            pl.BlockSpec((SLOPES, width), lambda j: (j, 0)),
        ],
        out_specs=[
            pl.BlockSpec((wide, SLOPES), lambda j: (0, j)),
            pl.BlockSpec((wide, SLOPES), lambda j: (0, j)),
            pl.BlockSpec((8 * rows, width), lambda j: (0, 0)),
        ],
        out_shape=[
            pltpu.HBM((wide, hid), BF),
            pltpu.HBM((wide, hid), BF),
            pltpu.HBM((8 * rows, width), BF),
        ],
        scratch_shapes=[
            pltpu.VMEM(strips.shape, BF),
            pltpu.VMEM((strips.shape[0], SLOPES), F32),
            pltpu.VMEM((8 * rows, SLOPES), F32),
            pltpu.VMEM((8 * rows, width), F32),
        ],
        compiler_params=pltpu.CompilerParams(vmem_limit_bytes=18 * MIB),
        cost_estimate=pl.CostEstimate(
            flops=2 * 10**10, bytes_accessed=12 * 2**20, transcendentals=3 * 2**20
        ),
    )(strips, *in_hbm(centre, w_expand, w_depthwise, w_project))


def attention_kernel(
    col_ref, in_ref, wq_hbm, wo_hbm, send_hbm, gq_hbm, att_hbm,
    wq, wo, qkv, gatt, att, gq, send, gqb, attended, edge, sems,
):
    tokens, width = attended.shape
    groups = 8
    members = tokens // groups
    quads = width // 128
    scale = HDIM ** (-0.5)
    load_wo = pltpu.make_async_copy(wo_hbm, wo, sems.at[0])
    load_wq = pltpu.make_async_copy(wq_hbm, wq, sems.at[1])
    load_wo.start()
    load_wq.start()

    def put(ref, at, value):
        value = value.astype(BF).astype(F32)
        for quad in range(quads):
            ref[at + quad] = value[:, quad * 128 : (quad + 1) * 128]

    load_wo.wait()
    put(gatt, 0, dot_nt(in_ref[:, width:], wo[...]))
    load_wq.wait()
    for part in range(3):
        lanes = slice(part * width, (part + 1) * width)
        put(qkv, part * quads, dot(in_ref[:, 0:width], wq[:, lanes]))
    per = 128 // HDIM
    head = lax.broadcasted_iota(jnp.int32, (members, 128), 1) // HDIM

    def spread(v):
        return jnp.concatenate([jnp.where(head == h, v, 0.0) for h in range(per)], 0).astype(BF)

    def gather(v):
        out = jnp.where(head == 0, v[0:members], 0.0)
        for h in range(1, per):
            out = jnp.where(head == h, v[h * members : (h + 1) * members], out)
        return out

    def one_group(g, _):
        at = pl.ds(g, members, stride=groups)
        every = range(quads)
        q = [spread(qkv[i, at, :]) for i in every]
        k = [qkv[quads + i, at, :].astype(BF) for i in every]
        v = [qkv[2 * quads + i, at, :].astype(BF) for i in every]
        do = [spread(gatt[i, at, :]) for i in every]
        scores = [dot_nt(k[i], q[i]) * scale for i in every]
        dp = [dot_nt(v[i], do[i]) for i in every]
        p = [jnp.exp(s - jnp.max(s, 0, keepdims=True)) for s in scores]
        p = [e * (1.0 / jnp.sum(e, 0, keepdims=True)) for e in p]
        pb = [e.astype(BF) for e in p]
        ds = [
            (p[i] * (dp[i] - jnp.sum(p[i] * dp[i], 0, keepdims=True)) * scale).astype(BF)
            for i in every
        ]
        for i in every:
            att[i, at, :] = gather(dot_tn(pb[i], v[i]))
            gq[i, at, :] = gather(dot_tn(ds[i], k[i]))
            gq[quads + i, at, :] = dot(ds[i], q[i])
            gq[2 * quads + i, at, :] = dot(pb[i], do[i])
        return 0

    lax.fori_loop(0, groups, one_group, 0)
    attended[...] = jnp.concatenate([att[i] for i in range(quads)], 1).astype(BF)
    store_att = pltpu.make_async_copy(attended, att_hbm, sems.at[2])
    store_att.start()
    gqb[...] = jnp.concatenate([gq[i] for i in range(3 * quads)], 1).astype(BF)
    store_gq = pltpu.make_async_copy(gqb, gq_hbm, sems.at[3])
    store_gq.start()
    grad = dot_nt(gqb[...], wq[...])
    send[:, width : 2 * width] = grad.astype(BF)
    put(gatt, 0, grad)
    place = lax.broadcasted_iota(jnp.int32, (members, 128), 0) % 8
    last = col_ref[0] % 4 == 3
    for i in range(quads):
        first_col = gatt[i, pl.ds(0, members, stride=groups), :]
        last_col = gatt[i, pl.ds(groups - 1, members, stride=groups), :]
        to_left = jnp.where(place == 7, 0.0, roll(first_col, -1))
        to_right = jnp.where(place == 0, 0.0, roll(last_col, 1))
        found = jnp.where(last, to_right, to_left)
        edge[pl.ds(2 * i, members, stride=groups), :] = found
        edge[pl.ds(2 * i + 1, members, stride=groups), :] = pltpu.roll(found, 64, 1)
    send[:, 2 * width :] = edge[...].astype(BF)
    send[:, 0:width] = dot(attended[...], wo[...]).astype(BF)
    store_send = pltpu.make_async_copy(send, send_hbm, sems.at[4])
    store_send.start()
    for store in [store_att, store_gq, store_send]:
        store.wait()


def attention_block(col, arrived, w_qkv, w_out):
    tokens = arrived.shape[0]
    width = w_out.shape[0]
    anywhere = pl.BlockSpec(memory_space=pl.ANY)
    return pl.pallas_call(
        attention_kernel,
        name="grid_attention",
        in_specs=[
            pl.BlockSpec(memory_space=pltpu.SMEM), pl.BlockSpec(memory_space=pltpu.VMEM), anywhere, anywhere
        ],
        out_specs=[anywhere] * 3,
        out_shape=[
            pltpu.HBM((tokens, 2 * width + 128), BF),
            pltpu.HBM((tokens, 3 * width), BF),
            pltpu.HBM((tokens, width), BF),
        ],
        scratch_shapes=[
            pltpu.VMEM((width, 3 * width), BF),
            pltpu.VMEM((width, width), BF),
            pltpu.VMEM((3 * width // 128, tokens, 128), F32),
            pltpu.VMEM((width // 128, tokens, 128), F32),
            pltpu.VMEM((width // 128, tokens, 128), F32),
            pltpu.VMEM((3 * width // 128, tokens, 128), F32),
            pltpu.VMEM((tokens, 2 * width + 128), BF),
            pltpu.VMEM((tokens, 3 * width), BF),
            pltpu.VMEM((tokens, width), BF),
            pltpu.VMEM((tokens, 128), F32),
            pltpu.SemaphoreType.DMA((5,)),
        ],
        compiler_params=pltpu.CompilerParams(vmem_limit_bytes=24 * MIB),
        cost_estimate=pl.CostEstimate(
            flops=2 * 512 * 512 * 512 * 8, bytes_accessed=7 * 2**20, transcendentals=2**20
        ),
    )(col, arrived, *in_hbm(w_qkv, w_out))


def residual_kernel(
    home_ref, resid_ref, go_ref, resid_s_ref, go_s_ref, out_ref, gr_ref, side_out, first_out, last_out,
    packed, side,
):
    tokens, width = resid_ref.shape
    rows, cols = 16, 32
    resid = resid_ref[...].astype(F32)
    out_ref[...] = (resid + home_ref[:, 0:width].astype(F32)).astype(BF)
    back = normalize_back(resid, home_ref[:, width : 2 * width].astype(F32))
    gr = (go_ref[...].astype(F32) + back).astype(BF)
    gr_ref[...] = gr
    packed[...] = home_ref[:, 2 * width :].astype(F32)
    side[...] = jnp.zeros(side.shape, F32)
    low = lax.broadcasted_iota(jnp.int32, (rows, 128), 1) < 64
    for i in range(width // 128):
        for at, start in ((0, 0), (7, cols - 8)):
            even = packed[pl.ds(start + 2 * i, rows, stride=cols), :]
            odd = packed[pl.ds(start + 2 * i + 1, rows, stride=cols), :]
            side[i, pl.ds(at, rows, stride=8), :] = jnp.where(low, even, pltpu.roll(odd, 64, 1))
    grad = jnp.concatenate([side[i] for i in range(width // 128)], 1)
    back = normalize_back(resid_s_ref[...].astype(F32), grad)
    gr_s = (go_s_ref[...].astype(F32) + back).astype(BF).astype(F32)
    side_out[...] = gr_s.astype(BF)
    none = jnp.zeros((8, width), F32)
    own = gr.astype(F32)
    first_out[...] = jnp.concatenate([own[0:cols], gr_s[0:8], none], 0).astype(BF)
    last_out[...] = jnp.concatenate([own[tokens - cols :], gr_s[8 * rows - 8 :], none], 0).astype(BF)


def residual_block(home, resid, go, resid_s, go_s):
    tokens, width = resid.shape
    beside = resid_s.shape[0]
    shapes = [(tokens, width), (tokens, width), (beside, width), (48, width), (48, width)]
    return pl.pallas_call(
        residual_kernel,
        name="residual",
        out_shape=[jax.ShapeDtypeStruct(shape, BF) for shape in shapes],
        scratch_shapes=[
            pltpu.VMEM((tokens, 128), F32),
            pltpu.VMEM((width // 128, beside, 128), F32),
        ],
        compiler_params=pltpu.CompilerParams(vmem_limit_bytes=12 * MIB),
    )(home, *in_hbm(resid, go, resid_s), go_s)


def split_by_core(core, full, mine_out, other_out):
    half = 128
    for j in range(full.shape[0] // (2 * half)):
        at = slice(j * half, (j + 1) * half)
        own = pl.multiple_of((2 * j + core) * half, half)
        other = pl.multiple_of((2 * j + 1 - core) * half, half)
        mine_out[at, :] = full[pl.ds(own, half), :]
        other_out[at, :] = full[pl.ds(other, half), :].astype(BF)


def pack(rows, width):
    blocks = rows.reshape(8, 2, 8, -1)
    low, high = [blocks[:, i].reshape(64, -1) for i in range(2)]
    more = low[:, width:] + pltpu.roll(high[:, width:], 64, 1)
    return jnp.concatenate([low[:, :width], high[:, :width], more], 1)


def backward_kernel(
    core_ref, x_ref, gr_ref, above_ref, below_ref, side_ref, act_ref, slope_c_ref, slope_e_ref,
    wd_ref, wp_ref,
    gpre, mine_out, other_out,
    wide, grad_wide, normed, gmid, act, full, taps_t,
):
    step = pl.program_id(0)
    rows, cols = 16, 32
    width = x_ref.shape[1]

    @pl.when(step == 0)
    def _():
        wide[0] = above_ref[0:WIDE, :].astype(F32)
        wide[rows + 1] = below_ref[0:WIDE, :].astype(F32)
        wide[1 : 1 + rows, 0:cols, :] = gr_ref[...].astype(F32).reshape(rows, cols, width)
        wide[1 : 1 + rows, cols:, :] = side_ref[...].astype(F32).reshape(rows, 8, width)
        grad_wide[...] = wide[...].reshape(grad_wide.shape).astype(BF)
        normed[...] = normalize(x_ref[...].astype(F32))[0].astype(BF)
        taps_t[...] = jnp.zeros(taps_t.shape, F32)

    gm = dot_nt(grad_wide[...], wp_ref[...]) * slope_c_ref[...].astype(F32)
    gmid[...] = gm.reshape(gmid.shape)
    act[...] = act_ref[...].astype(F32).reshape(act.shape)
    inside = lax.broadcasted_iota(jnp.int32, (WIDE, 128), 0) < cols
    for lo in range(0, CHUNK, 128):
        lanes = slice(lo, lo + 128)
        taps = [wd_ref[k : k + 1, lanes].astype(F32) for k in range(9)]
        sums = [None] * 9
        grads = [gmid[0, :, lanes], gmid[1, :, lanes]]
        acts = [act[0, :, lanes], act[1, :, lanes]]
        for r in range(rows):
            grads = grads[-2:] + [gmid[r + 2, :, lanes]]
            acts = acts[-2:] + [act[r + 2, :, lanes]]
            parts = [sum(grads[2 - i] * taps[3 * i + j] for i in range(3)) for j in range(3)]
            grad_act = parts[1] + roll(parts[0], -1) + roll(parts[2], 1)
            at = slice(r * cols, (r + 1) * cols)
            gpre[at, lanes] = (grad_act[0:cols] * slope_e_ref[at, lanes].astype(F32)).astype(BF)
            own = jnp.where(inside, grads[1], 0.0)
            moved = [roll(own, -1), own, roll(own, 1)]
            for k in range(9):
                prod = jnp.sum((acts[k // 3] * moved[k % 3]).reshape(WIDE // 8, 8, 128), 0)
                sums[k] = prod if r == 0 else sums[k] + prod
        for k in range(9):
            taps_t[k : k + 1, lanes] = jnp.sum(sums[k], 0, keepdims=True)
    full[:, 0:width] = dot_tn(gpre[...], normed[...])
    full[:, width:] = taps_t[...].T
    own = pl.multiple_of(core_ref[0] * (CHUNK // 2), CHUNK // 2)
    other = pl.multiple_of(CHUNK // 2 - own, CHUNK // 2)
    mine_out[...] = pack(full[pl.ds(own, CHUNK // 2), :], width)
    other_out[...] = pack(full[pl.ds(other, CHUNK // 2), :], width).astype(BF)


def backward_block(core, x, gr, near, act, slope_c, slope_e, w_depthwise, w_project):
    tokens, width = x.shape
    hid = w_project.shape[0]
    rows, cols = 16, 32
    whole = lambda a: pl.BlockSpec(a.shape, lambda j, c: (0,) * a.ndim)
    return pl.pallas_call(
        backward_kernel,
        name="mbconv_backward",
        grid_spec=pltpu.PrefetchScalarGridSpec(
            num_scalar_prefetch=1,
            grid=(hid // CHUNK,),
            in_specs=[
                whole(x), whole(gr), *[whole(a) for a in near],
                pl.BlockSpec(((rows + 2) * WIDE, CHUNK), lambda j, c: (0, j)),
                pl.BlockSpec(((rows + 2) * WIDE, CHUNK), lambda j, c: (0, j)),
                pl.BlockSpec((tokens, CHUNK), lambda j, c: (0, j)),
                pl.BlockSpec((9, CHUNK), lambda j, c: (0, j)),
                pl.BlockSpec((CHUNK, width), lambda j, c: (j, 0)),
            ],
            out_specs=[
                pl.BlockSpec((tokens, CHUNK), lambda j, c: (0, j)),
                pl.BlockSpec((CHUNK // 4, 2 * width + 128), lambda j, c: (j, 0)),
                pl.BlockSpec((CHUNK // 4, 2 * width + 128), lambda j, c: (j, 0)),
            ],
            scratch_shapes=[
                pltpu.VMEM((rows + 2, WIDE, width), F32),
                pltpu.VMEM(((rows + 2) * WIDE, width), BF),
                pltpu.VMEM((tokens, width), BF),
                pltpu.VMEM((rows + 2, WIDE, CHUNK), F32),
                pltpu.VMEM((rows + 2, WIDE, CHUNK), F32),
                pltpu.VMEM((CHUNK, width + 128), F32),
                pltpu.VMEM((128, CHUNK), F32),
            ],
        ),
        out_shape=[
            pltpu.HBM((tokens, hid), BF),
            jax.ShapeDtypeStruct((hid // 4, 2 * width + 128), F32),
            jax.ShapeDtypeStruct((hid // 4, 2 * width + 128), BF),
        ],
        compiler_params=pltpu.CompilerParams(vmem_limit_bytes=18 * MIB),
        cost_estimate=pl.CostEstimate(
            flops=16 * 512 * 512 * 2048, bytes_accessed=20 * 2**20, transcendentals=2**20
        ),
    )(core, *in_hbm(x), gr, *near, *in_hbm(act, slope_c, slope_e, w_depthwise, w_project))


def input_kernel(gpre_ref, we_ref, x_ref, gr_ref, gx_out):
    back = normalize_back(x_ref[...].astype(F32), dot_nt(gpre_ref[...], we_ref[...]))
    gx_out[...] = (gr_ref[...].astype(F32) + back).astype(BF)


def input_grads(gpre, w_expand, x, gr):
    tokens, width = x.shape
    hid = w_expand.shape[1]
    tile = 128
    return pl.pallas_call(
        input_kernel,
        name="grad_input",
        grid=(tokens // tile,),
        in_specs=[
            pl.BlockSpec((tile, hid), lambda i: (i, 0)),
            pl.BlockSpec((width, hid), lambda i: (0, 0)),
            pl.BlockSpec((tile, width), lambda i: (i, 0)),
            pl.BlockSpec((tile, width), lambda i: (i, 0)),
        ],
        out_specs=pl.BlockSpec((tile, width), lambda i: (i, 0)),
        out_shape=jax.ShapeDtypeStruct((tokens, width), BF),
        compiler_params=pltpu.CompilerParams(vmem_limit_bytes=12 * MIB),
        cost_estimate=pl.CostEstimate(
            flops=4 * 512 * 512 * 2048, bytes_accessed=6 * 2**20, transcendentals=0
        ),
    )(*in_hbm(gpre, w_expand, x, gr))


def finish_kernel(parts_ref, expand_out, depth_out):
    total = jnp.sum(parts_ref[...].astype(F32), 0)
    own, width = expand_out.shape
    expand_out[0 : own // 2, :] = total[:, 0:width]
    expand_out[own // 2 :, :] = total[:, width : 2 * width]
    more = total[:, 2 * width :]
    rows = [more, pltpu.roll(more, 64, 1), jnp.zeros((128 - own, 128), F32)]
    depth_out[...] = jnp.concatenate(rows, 0).T[0:9, 0:own]


def finish(parts):
    own, width = 2 * parts.shape[1], (parts.shape[2] - 128) // 2
    return pl.pallas_call(
        finish_kernel,
        name="last_sum",
        out_shape=[
            pltpu.HBM((own, width), F32),
            pltpu.HBM((9, own), F32),
        ],
        compiler_params=pltpu.CompilerParams(vmem_limit_bytes=10 * MIB),
    )(parts)


def project_kernel(core_ref, mid_ref, gr_ref, mine_out, other_out, full):
    full[...] = dot_tn(mid_ref[...], gr_ref[...])
    split_by_core(core_ref[0], full, mine_out, other_out)


def project_grads(core, mid, gr):
    tokens, hid = mid.shape
    width = gr.shape[1]
    lanes = 512
    return pl.pallas_call(
        project_kernel,
        name="grad_project",
        grid_spec=pltpu.PrefetchScalarGridSpec(
            num_scalar_prefetch=1,
            grid=(hid // lanes,),
            in_specs=[
                pl.BlockSpec((tokens, lanes), lambda j, c: (0, j)),
                pl.BlockSpec((tokens, width), lambda j, c: (0, 0)),
            ],
            out_specs=[pl.BlockSpec((lanes // 2, width), lambda j, c: (j, 0))] * 2,
            scratch_shapes=[pltpu.VMEM((lanes, width), F32)],
        ),
        out_shape=[
            jax.ShapeDtypeStruct((hid // 2, width), F32),
            jax.ShapeDtypeStruct((hid // 2, width), BF),
        ],
        compiler_params=pltpu.CompilerParams(vmem_limit_bytes=8 * MIB),
        cost_estimate=pl.CostEstimate(
            flops=2 * 512 * 512 * 2048, bytes_accessed=7 * 2**20, transcendentals=0
        ),
    )(core, *in_hbm(mid), gr)


def attention_grads_kernel(
    core_ref, arrived_ref, gqkv_ref, att_ref, mine_out, other_out, qkv, outp, half_q, half_o, full
):
    width = att_ref.shape[1]
    qkv[...] = dot_tn(gqkv_ref[...], arrived_ref[:, 0:width])
    outp[...] = dot_tn(arrived_ref[:, width:], att_ref[...])
    nq, no = qkv.shape[0] // 16, outp.shape[0] // 16
    for j in range(8):
        for own in (True, False):
            core = core_ref[0] if own else 1 - core_ref[0]
            half_q[...] = qkv[pl.ds(pl.multiple_of((2 * j + core) * nq, 8), nq), :]
            half_o[...] = outp[pl.ds(pl.multiple_of((2 * j + core) * no, 8), no), :]
            for k in range(8):
                full[16 * k : 16 * k + 12, :] = half_q[12 * k : 12 * k + 12, :]
                full[16 * k + 12 : 16 * k + 16, :] = half_o[4 * k : 4 * k + 4, :]
            at = slice(128 * j, 128 * j + 128)
            if own:
                mine_out[at, :] = full[...]
            else:
                other_out[at, :] = full[...].astype(BF)


def attention_grads(core, arrived, gqkv, attended):
    tokens, width = attended.shape
    vmem = pl.BlockSpec(memory_space=pltpu.VMEM)
    return pl.pallas_call(
        attention_grads_kernel,
        name="attention_grads",
        in_specs=[pl.BlockSpec(memory_space=pltpu.SMEM), vmem, vmem, vmem],
        out_specs=[vmem, vmem],
        out_shape=[
            jax.ShapeDtypeStruct((1024, width), F32),
            jax.ShapeDtypeStruct((1024, width), BF),
        ],
        scratch_shapes=[
            pltpu.VMEM((3 * width, width), F32),
            pltpu.VMEM((width, width), F32),
            pltpu.VMEM((96, width), F32),
            pltpu.VMEM((32, width), F32),
            pltpu.VMEM((128, width), F32),
        ],
        compiler_params=pltpu.CompilerParams(vmem_limit_bytes=14 * MIB),
        cost_estimate=pl.CostEstimate(
            flops=8 * 512 * 512 * 512, bytes_accessed=8 * 2**20, transcendentals=0
        ),
    )(core, *in_hbm(arrived, gqkv, attended))


def add_pair(mine, other):
    got = lax.ppermute(other, AX, other_core())
    return (mine + got.astype(F32)).astype(BF).reshape(64, mine.shape[0] // 64, -1)


def body(block_input, w_expand, w_depthwise, w_project, w_qkv, w_out, grad_out):
    _, rows, cols, width = block_input.shape
    tokens = rows * cols
    core = (lax.axis_index("row") % 2).astype(jnp.int32).reshape(1)
    col = lax.axis_index("col").astype(jnp.int32).reshape(1)
    image = block_input[0]
    x = image.reshape(tokens, width)
    go = grad_out[0].reshape(tokens, width)
    act0 = expand_block(x, w_expand, gelu, 0, 2)
    centre = expand_block(x, w_expand, gelu, 1, 2, act0)
    strips, go_side = halo(image, 2, act0, grad_out[0])
    mid, resid, send = forward_block(x, strips, go, centre, w_expand, w_depthwise, w_project)
    arrived = across_chips(send.reshape(64, 8, 2 * width)).reshape(tokens, 2 * width)
    slopes = slopes_block(strips, centre, w_expand, w_depthwise, w_project)
    arrived, (act, slope_c, resid_side) = lax.optimization_barrier((arrived, slopes))
    back, gqkv, attended = attention_block(col, arrived, w_qkv, w_out)
    home = across_chips(back.reshape(64, 8, -1)).reshape(tokens, -1)
    slope_e = expand_block(x, w_expand, gelu_slope, 0, 1)
    home, slope_e = lax.optimization_barrier((home, slope_e))
    attention_pair = add_pair(*attention_grads(core, arrived, gqkv, attended))
    out, gr, side, first_row, last_row = residual_block(home, resid, go, resid_side, go_side)
    above, below = shift(last_row, "row", 1), shift(first_row, "row", -1)
    project_pair = add_pair(*project_grads(core, mid, gr))
    first = jnp.concatenate([project_pair, attention_pair], 1)
    above, below, first = lax.optimization_barrier((above, below, first))
    first = across_chips(first)
    gpre, mine, other = backward_block(
        core, x, gr, (above, below, side), act, slope_c, slope_e, w_depthwise, w_project
    )
    gx = input_grads(gpre, w_expand, x, gr)
    second = add_pair(mine, other)
    second, first = lax.optimization_barrier((second, first))
    grad_expand, grad_depth = finish(across_chips(second))
    first = jnp.sum(first.astype(F32), 0)
    return (
        out.reshape(1, rows, cols, width),
        gx.reshape(1, rows, cols, width),
        grad_expand.T,
        grad_depth,
        first[:16].T,
        first[16:28].T,
        first[28:].T,
    )


def solution(mesh):
    tokens = P(None, "row", "col", None)
    split = P(None, AX)
    return jax.shard_map(
        body,
        mesh=mesh,
        in_specs=(tokens, P(), P(), P(), P(), P(), tokens),
        out_specs=(tokens, tokens, split, split, split, split, split),
        check_vma=False,
    )
```

```python
import functools
import itertools

import jax
import jax.numpy as jnp
from jax import lax
from jax.experimental import pallas as pl
from jax.experimental.pallas import tpu as pltpu
from jax.sharding import PartitionSpec as P

HEADS = 16
HDIM = 32
EPS = 1e-05
BF = jnp.bfloat16
F32 = jnp.float32
AX = ("row", "col")
WIDE = 40
CHUNK = 256
MIB = 2**20

SIZES = dict(y_lo=2, z=4, core=2, x=4, y_hi=2)
STRIDES = dict(y_lo=64, z=16, core=8, x=2, y_hi=1)
CHIPS = ("y_lo", "z", "x", "y_hi")


def device_groups(axes):
    rest = [a for a in SIZES if a not in axes]
    found = []
    for at in itertools.product(*[range(SIZES[a]) for a in rest]):
        base = sum(v * STRIDES[a] for v, a in zip(at, rest))
        found.append(
            [
                base + sum(v * STRIDES[a] for v, a in zip(m, axes))
                for m in itertools.product(*[range(SIZES[a]) for a in axes])
            ]
        )
    return found


def other_core():
    return [(d, d ^ STRIDES["core"]) for d in range(128)]


def across_chips(x):
    return lax.all_to_all(x, AX, 0, 0, tiled=True, axis_index_groups=device_groups(CHIPS))


def shift(x, axis, step):
    n = lax.axis_size(axis)
    pairs = [(i, i + step) for i in range(n) if 0 <= i + step < n]
    return lax.ppermute(x, axis, pairs)


def halo(x, width, ahead, beside):
    rows, cols, chans = x.shape
    above = shift(x[rows - width :], "row", 1)
    below = shift(x[:width], "row", -1)
    above, below, _ = lax.optimization_barrier((above, below, ahead))
    flat = lambda v: v.reshape(-1, chans)

    def column(at):
        parts = [above[:, at], x[:, at], below[:, at], beside[:, at]]
        return jnp.concatenate([flat(p) for p in parts], 0)

    left = shift(column(slice(cols - width, cols)), "col", 1)
    right = shift(column(slice(0, width)), "col", -1)
    n = (rows + 2 * width) * width

    def sides(right, left):
        right, left = [v.reshape(-1, width, chans) for v in (right, left)]
        gap = jnp.zeros((right.shape[0], 8 - 2 * width, chans), x.dtype)
        return flat(jnp.concatenate([right, gap, left], 1))

    strips = [flat(above), flat(below), sides(right[:n], left[:n])]
    return jnp.concatenate(strips, 0), sides(right[n:], left[n:])


def place(wide, centre, strips, width, rows, cols):
    lanes = strips.shape[-1]
    n = width * cols
    if centre is not None:
        wide[width : width + rows, 0:cols, :] = centre.reshape(rows, cols, lanes)
    wide[0:width, 0:cols, :] = strips[0:n].reshape(width, cols, lanes)
    wide[width + rows :, 0:cols, :] = strips[n : 2 * n].reshape(width, cols, lanes)
    wide[:, cols:, :] = strips[2 * n :].reshape(rows + 2 * width, WIDE - cols, lanes)


def normalize(x):
    center = x - jnp.mean(x, -1, keepdims=True)
    ratio = lax.rsqrt(jnp.mean(center * center, -1, keepdims=True) + EPS)
    return center * ratio, ratio


def normalize_back(x, grad):
    scaled, ratio = normalize(x)
    return (
        grad
        - jnp.mean(grad, -1, keepdims=True)
        - scaled * jnp.mean(grad * scaled, -1, keepdims=True)
    ) * ratio


A0 = 0.7978845608028654
A1 = A0 * 0.044715


def gelu_half(x):
    inner = A0 + A1 * (x * x)
    return inner, 0.5 + 0.5 * jnp.tanh(x * inner)


def gelu(x):
    return x * gelu_half(x)[1]


def gelu_slope(x):
    inner, half = gelu_half(x)
    value = x * half
    return half + (value - value * half) * (6.0 * inner - 4.0 * A0)


def dot(a, b):
    return jnp.dot(a, b, preferred_element_type=F32)


def dot_nt(a, b):
    return lax.dot_general(a, b, (((1,), (1,)), ((), ())), preferred_element_type=F32)


def dot_tn(a, b):
    return lax.dot_general(a, b, (((0,), (0,)), ((), ())), preferred_element_type=F32)


def in_hbm(*arrays):
    return [pltpu.with_memory_space_constraint(a, pltpu.HBM) for a in arrays]


def roll(x, by):
    return pltpu.roll(x, by % x.shape[0], 0)


def expand_kernel(apply, x_ref, we_ref, *refs):
    act_out, normed = refs[-2:]

    @pl.when(pl.program_id(0) == 0)
    def _():
        normed[...] = normalize(x_ref[...].astype(F32))[0].astype(BF)

    for tile in range(0, x_ref.shape[0], 128):
        at = slice(tile, tile + 128)
        act_out[at, :] = apply(dot(normed[at, :], we_ref[...])).astype(BF)


def expand_block(x, w_expand, apply, part, parts, held=None):
    tokens, width = x.shape
    hid = w_expand.shape[1]
    lanes = 512
    steps = hid // lanes // parts
    held = [] if held is None else [held]
    return pl.pallas_call(
        functools.partial(expand_kernel, apply),
        name=apply.__name__ + "_expand",
        grid=(steps,),
        in_specs=[
            pl.BlockSpec((tokens, width), lambda j: (0, 0)),
            pl.BlockSpec((width, lanes), lambda j: (0, j + part * steps)),
            *[pl.BlockSpec(memory_space=pl.ANY) for _ in held],
        ],
        out_specs=pl.BlockSpec((tokens, lanes), lambda j: (0, j + part * steps)),
        out_shape=pltpu.HBM((tokens, hid), BF),
        scratch_shapes=[pltpu.VMEM((tokens, width), BF)],
        input_output_aliases={2: 0} if held else {},
        compiler_params=pltpu.CompilerParams(vmem_limit_bytes=8 * MIB),
        cost_estimate=pl.CostEstimate(
            flops=8 * 512 * 512 * 2048, bytes_accessed=3 * 2**20, transcendentals=2**19
        ),
    )(*in_hbm(x, w_expand), *held)


FORWARD = 512


def forward_kernel(
    x_hbm, strips_ref, go_hbm, act_ref, we_ref, wd_ref, wp_ref,
    mid_out, resid_out, send_out,
    normed, edge, acc, x_ref, go_ref, sems,
):
    step = pl.program_id(0)
    rows, cols = 16, 32
    width = x_ref.shape[1]
    load_x = pltpu.make_async_copy(x_hbm, x_ref, sems.at[0])
    load_go = pltpu.make_async_copy(go_hbm, go_ref, sems.at[1])

    @pl.when(step == 0)
    def _():
        load_x.start()
        load_go.start()
        every = normalize(strips_ref[...].astype(F32))[0]
        sides = 4 * cols + 8
        near = [every[cols : 3 * cols], every[sides : sides + 8 * (rows + 2)]]
        normed[...] = jnp.concatenate(near, 0).astype(BF)

    edge[...] = gelu(dot(normed[...], we_ref[...]))
    for lo in range(0, FORWARD, 128):
        lanes = slice(lo, lo + 128)
        taps = [wd_ref[k : k + 1, lanes].astype(F32) for k in range(9)]

        def line(r):
            if r == 0:
                centre = edge[0:cols, lanes]
            elif r == rows + 1:
                centre = edge[cols : 2 * cols, lanes]
            else:
                centre = act_ref[(r - 1) * cols : r * cols, lanes].astype(F32)
            side = edge[2 * cols + 8 * r : 2 * cols + 8 * (r + 1), lanes]
            whole = jnp.concatenate([centre, side], 0)
            return roll(whole, 1)[0:cols], centre, roll(whole, -1)[0:cols]

        lines = [line(0), line(1)]
        for r in range(rows):
            lines = lines[-2:] + [line(r + 2)]
            conv = sum(lines[k // 3][k % 3] * taps[k] for k in range(9))
            mid_out[r * cols : (r + 1) * cols, lanes] = gelu(conv).astype(BF)
        if lo % 256:
            at = slice(lo - 128, lo + 128)
            part = dot(mid_out[:, at], wp_ref[at, :])
            product = part if lo == 128 else product + part

    @pl.when(step == 0)
    def _():
        acc[...] = product

    @pl.when(step > 0)
    def _():
        acc[...] += product

    @pl.when(step == pl.num_programs(0) - 1)
    def _():
        load_x.wait()
        resid = (x_ref[...].astype(F32) + acc[...]).astype(BF)
        resid_out[...] = resid
        send_out[:, 0:width] = normalize(resid.astype(F32))[0].astype(BF)
        load_go.wait()
        send_out[:, width:] = go_ref[...]


def forward_block(x, strips, go, act, w_expand, w_depthwise, w_project):
    tokens, width = x.shape
    hid = w_expand.shape[1]
    rows, cols = 16, 32
    near = 2 * cols + 8 * (rows + 2)
    anywhere = pl.BlockSpec(memory_space=pl.ANY)
    whole = lambda a: pl.BlockSpec(a.shape, lambda j: (0,) * a.ndim)
    return pl.pallas_call(
        forward_kernel,
        name="mbconv_forward",
        grid=(hid // FORWARD,),
        in_specs=[
            anywhere, whole(strips), anywhere,
            pl.BlockSpec((tokens, FORWARD), lambda j: (0, j)),
            pl.BlockSpec((width, FORWARD), lambda j: (0, j)),
            pl.BlockSpec((9, FORWARD), lambda j: (0, j)),
            pl.BlockSpec((FORWARD, width), lambda j: (j, 0)),
        ],
        out_specs=[
            pl.BlockSpec((tokens, FORWARD), lambda j: (0, j)),
            pl.BlockSpec((tokens, width), lambda j: (0, 0)),
            pl.BlockSpec((tokens, 2 * width), lambda j: (0, 0)),
        ],
        out_shape=[
            pltpu.HBM((tokens, hid), BF),
            pltpu.HBM((tokens, width), BF),
            pltpu.HBM((tokens, 2 * width), BF),
        ],
        scratch_shapes=[
            pltpu.VMEM((near, width), BF),
            pltpu.VMEM((near, FORWARD), F32),
            pltpu.VMEM((tokens, width), F32),
            pltpu.VMEM((tokens, width), BF),
            pltpu.VMEM((tokens, width), BF),
            pltpu.SemaphoreType.DMA((2,)),
        ],
        compiler_params=pltpu.CompilerParams(vmem_limit_bytes=18 * MIB),
        cost_estimate=pl.CostEstimate(
            flops=2 * 700 * 512 * 2048, bytes_accessed=10 * 2**20, transcendentals=2**20
        ),
    )(*in_hbm(x), strips, *in_hbm(go, act, w_expand, w_depthwise, w_project))


SLOPES = 512


def slopes_kernel(
    strips_ref, centre_ref, we_ref, wd_ref, wp_ref,
    act_out, slope_out, resid_out,
    normed, edge, beside, acc,
):
    rows, cols = 16, 32

    @pl.when(pl.program_id(0) == 0)
    def _():
        acc[...] = jnp.zeros(acc.shape, F32)
        normed[...] = normalize(strips_ref[...].astype(F32))[0].astype(BF)

    edge[...] = gelu(dot(normed[...], we_ref[...]))
    for lo in range(0, SLOPES, 128):
        lanes = slice(lo, lo + 128)
        taps = [wd_ref[k : k + 1, lanes].astype(F32) for k in range(9)]

        def line(r):
            if r < 2:
                centre = edge[r * cols : (r + 1) * cols, lanes]
            elif r < rows + 2:
                centre = centre_ref[(r - 2) * cols : (r - 1) * cols, lanes].astype(F32)
            else:
                centre = edge[(r - rows) * cols : (r - rows + 1) * cols, lanes]
            side = edge[4 * cols + 8 * r : 4 * cols + 8 * (r + 1), lanes]
            return jnp.concatenate([centre, side], 0)

        lines = [line(0), line(1)]
        held = None
        for r in range(rows + 2):
            lines = lines[-2:] + [line(r + 2)]
            sums = [sum(lines[i] * taps[3 * i + j] for i in range(3)) for j in range(3)]
            conv = sums[1] + roll(sums[0], 1) + roll(sums[2], -1)
            slope = gelu_slope(conv)
            if 1 <= r <= rows:
                beside[8 * (r - 1) : 8 * r, lanes] = gelu(conv[cols:])
            if r % 2:
                at = slice((r - 1) * WIDE, (r + 1) * WIDE)
                act_out[at, lanes] = jnp.concatenate(lines[:2], 0).astype(BF)
                slope_out[at, lanes] = jnp.concatenate([held, slope], 0).astype(BF)
            held = slope
    acc[...] += dot(beside[...].astype(BF), wp_ref[...])

    @pl.when(pl.program_id(0) == pl.num_programs(0) - 1)
    def _():
        at = 2 * (2 * cols) + 2 * 8
        resid_out[...] = (strips_ref[at : at + 8 * rows, :].astype(F32) + acc[...]).astype(BF)


def slopes_block(strips, centre, w_expand, w_depthwise, w_project):
    tokens, hid = centre.shape
    width = strips.shape[1]
    rows = 16
    wide = (rows + 2) * WIDE
    return pl.pallas_call(
        slopes_kernel,
        name="gelu_slopes",
        grid=(hid // SLOPES,),
        in_specs=[
            pl.BlockSpec(strips.shape, lambda j: (0, 0)),
            pl.BlockSpec((tokens, SLOPES), lambda j: (0, j)),
            pl.BlockSpec((width, SLOPES), lambda j: (0, j)),
            pl.BlockSpec((9, SLOPES), lambda j: (0, j)),
            pl.BlockSpec((SLOPES, width), lambda j: (j, 0)),
        ],
        out_specs=[
            pl.BlockSpec((wide, SLOPES), lambda j: (0, j)),
            pl.BlockSpec((wide, SLOPES), lambda j: (0, j)),
            pl.BlockSpec((8 * rows, width), lambda j: (0, 0)),
        ],
        out_shape=[
            pltpu.HBM((wide, hid), BF),
            pltpu.HBM((wide, hid), BF),
            pltpu.HBM((8 * rows, width), BF),
        ],
        scratch_shapes=[
            pltpu.VMEM(strips.shape, BF),
            pltpu.VMEM((strips.shape[0], SLOPES), F32),
            pltpu.VMEM((8 * rows, SLOPES), F32),
            pltpu.VMEM((8 * rows, width), F32),
        ],
        compiler_params=pltpu.CompilerParams(vmem_limit_bytes=18 * MIB),
        cost_estimate=pl.CostEstimate(
            flops=2 * 10**10, bytes_accessed=12 * 2**20, transcendentals=3 * 2**20
        ),
    )(strips, *in_hbm(centre, w_expand, w_depthwise, w_project))


def attention_kernel(
    col_ref, in_ref, wq_hbm, wo_hbm, send_hbm, gq_hbm, att_hbm,
    wq, wo, qkv, gatt, att, gq, send, gqb, attended, edge, sems,
):
    tokens, width = attended.shape
    groups = 8
    members = tokens // groups
    quads = width // 128
    scale = HDIM ** (-0.5)
    load_wo = pltpu.make_async_copy(wo_hbm, wo, sems.at[0])
    load_wq = pltpu.make_async_copy(wq_hbm, wq, sems.at[1])
    load_wo.start()
    load_wq.start()

    def put(ref, at, value):
        value = value.astype(BF).astype(F32)
        for quad in range(quads):
            ref[at + quad] = value[:, quad * 128 : (quad + 1) * 128]

    load_wo.wait()
    put(gatt, 0, dot_nt(in_ref[:, width:], wo[...]))
    load_wq.wait()
    for part in range(3):
        lanes = slice(part * width, (part + 1) * width)
        put(qkv, part * quads, dot(in_ref[:, 0:width], wq[:, lanes]))
    per = 128 // HDIM
    head = lax.broadcasted_iota(jnp.int32, (members, 128), 1) // HDIM

    def spread(v):
        return jnp.concatenate([jnp.where(head == h, v, 0.0) for h in range(per)], 0).astype(BF)

    def gather(v):
        out = jnp.where(head == 0, v[0:members], 0.0)
        for h in range(1, per):
            out = jnp.where(head == h, v[h * members : (h + 1) * members], out)
        return out

    def one_group(g, _):
        at = pl.ds(g, members, stride=groups)
        every = range(quads)
        q = [spread(qkv[i, at, :]) for i in every]
        k = [qkv[quads + i, at, :].astype(BF) for i in every]
        v = [qkv[2 * quads + i, at, :].astype(BF) for i in every]
        do = [spread(gatt[i, at, :]) for i in every]
        scores = [dot_nt(k[i], q[i]) * scale for i in every]
        dp = [dot_nt(v[i], do[i]) for i in every]
        p = [jnp.exp(s - jnp.max(s, 0, keepdims=True)) for s in scores]
        p = [e * (1.0 / jnp.sum(e, 0, keepdims=True)) for e in p]
        pb = [e.astype(BF) for e in p]
        ds = [
            (p[i] * (dp[i] - jnp.sum(p[i] * dp[i], 0, keepdims=True)) * scale).astype(BF)
            for i in every
        ]
        for i in every:
            att[i, at, :] = gather(dot_tn(pb[i], v[i]))
            gq[i, at, :] = gather(dot_tn(ds[i], k[i]))
            gq[quads + i, at, :] = dot(ds[i], q[i])
            gq[2 * quads + i, at, :] = dot(pb[i], do[i])
        return 0

    lax.fori_loop(0, groups, one_group, 0)
    attended[...] = jnp.concatenate([att[i] for i in range(quads)], 1).astype(BF)
    store_att = pltpu.make_async_copy(attended, att_hbm, sems.at[2])
    store_att.start()
    gqb[...] = jnp.concatenate([gq[i] for i in range(3 * quads)], 1).astype(BF)
    store_gq = pltpu.make_async_copy(gqb, gq_hbm, sems.at[3])
    store_gq.start()
    grad = dot_nt(gqb[...], wq[...])
    send[:, width : 2 * width] = grad.astype(BF)
    put(gatt, 0, grad)
    place = lax.broadcasted_iota(jnp.int32, (members, 128), 0) % 8
    last = col_ref[0] % 4 == 3
    for i in range(quads):
        first_col = gatt[i, pl.ds(0, members, stride=groups), :]
        last_col = gatt[i, pl.ds(groups - 1, members, stride=groups), :]
        to_left = jnp.where(place == 7, 0.0, roll(first_col, -1))
        to_right = jnp.where(place == 0, 0.0, roll(last_col, 1))
        found = jnp.where(last, to_right, to_left)
        edge[pl.ds(2 * i, members, stride=groups), :] = found
        edge[pl.ds(2 * i + 1, members, stride=groups), :] = pltpu.roll(found, 64, 1)
    send[:, 2 * width :] = edge[...].astype(BF)
    send[:, 0:width] = dot(attended[...], wo[...]).astype(BF)
    store_send = pltpu.make_async_copy(send, send_hbm, sems.at[4])
    store_send.start()
    for store in [store_att, store_gq, store_send]:
        store.wait()


def attention_block(col, arrived, w_qkv, w_out):
    tokens = arrived.shape[0]
    width = w_out.shape[0]
    anywhere = pl.BlockSpec(memory_space=pl.ANY)
    return pl.pallas_call(
        attention_kernel,
        name="grid_attention",
        in_specs=[
            pl.BlockSpec(memory_space=pltpu.SMEM), pl.BlockSpec(memory_space=pltpu.VMEM), anywhere, anywhere
        ],
        out_specs=[anywhere] * 3,
        out_shape=[
            pltpu.HBM((tokens, 2 * width + 128), BF),
            pltpu.HBM((tokens, 3 * width), BF),
            pltpu.HBM((tokens, width), BF),
        ],
        scratch_shapes=[
            pltpu.VMEM((width, 3 * width), BF),
            pltpu.VMEM((width, width), BF),
            pltpu.VMEM((3 * width // 128, tokens, 128), F32),
            pltpu.VMEM((width // 128, tokens, 128), F32),
            pltpu.VMEM((width // 128, tokens, 128), F32),
            pltpu.VMEM((3 * width // 128, tokens, 128), F32),
            pltpu.VMEM((tokens, 2 * width + 128), BF),
            pltpu.VMEM((tokens, 3 * width), BF),
            pltpu.VMEM((tokens, width), BF),
            pltpu.VMEM((tokens, 128), F32),
            pltpu.SemaphoreType.DMA((5,)),
        ],
        compiler_params=pltpu.CompilerParams(vmem_limit_bytes=24 * MIB),
        cost_estimate=pl.CostEstimate(
            flops=2 * 512 * 512 * 512 * 8, bytes_accessed=7 * 2**20, transcendentals=2**20
        ),
    )(col, arrived, *in_hbm(w_qkv, w_out))


def residual_kernel(
    core_ref, home_ref, resid_ref, go_ref, resid_s_ref, go_s_ref, mid_hbm,
    out_ref, gr_ref, side_out, first_out, last_out, mine_out, other_out,
    packed, side, mid, full, sems,
):
    steps, _, lanes = mid.shape
    loads = [
        pltpu.make_async_copy(mid_hbm.at[:, pl.ds(lanes * i, lanes)], mid.at[i], sems.at[i])
        for i in range(steps)
    ]
    for load in loads:
        load.start()
    residual_step(
        home_ref, resid_ref, go_ref, resid_s_ref, go_s_ref,
        out_ref, gr_ref, side_out, first_out, last_out, packed, side,
    )
    half = 128
    for i in range(steps):
        loads[i].wait()
        full[...] = dot_tn(mid[i], gr_ref[...])
        for j in range(lanes // (2 * half)):
            at = i * lanes // 2 + j * half
            own = pl.multiple_of((2 * j + core_ref[0]) * half, half)
            other = pl.multiple_of((2 * j + 1 - core_ref[0]) * half, half)
            mine_out[at : at + half, :] = full[pl.ds(own, half), :]
            other_out[at : at + half, :] = full[pl.ds(other, half), :].astype(BF)


def residual_step(
    home_ref, resid_ref, go_ref, resid_s_ref, go_s_ref, out_ref, gr_ref, side_out, first_out, last_out,
    packed, side,
):
    tokens, width = resid_ref.shape
    rows, cols = 16, 32
    resid = resid_ref[...].astype(F32)
    out_ref[...] = (resid + home_ref[:, 0:width].astype(F32)).astype(BF)
    back = normalize_back(resid, home_ref[:, width : 2 * width].astype(F32))
    gr = (go_ref[...].astype(F32) + back).astype(BF)
    gr_ref[...] = gr
    packed[...] = home_ref[:, 2 * width :].astype(F32)
    side[...] = jnp.zeros(side.shape, F32)
    low = lax.broadcasted_iota(jnp.int32, (rows, 128), 1) < 64
    for i in range(width // 128):
        for at, start in ((0, 0), (7, cols - 8)):
            even = packed[pl.ds(start + 2 * i, rows, stride=cols), :]
            odd = packed[pl.ds(start + 2 * i + 1, rows, stride=cols), :]
            side[i, pl.ds(at, rows, stride=8), :] = jnp.where(low, even, pltpu.roll(odd, 64, 1))
    grad = jnp.concatenate([side[i] for i in range(width // 128)], 1)
    back = normalize_back(resid_s_ref[...].astype(F32), grad)
    gr_s = (go_s_ref[...].astype(F32) + back).astype(BF).astype(F32)
    side_out[...] = gr_s.astype(BF)
    none = jnp.zeros((8, width), F32)
    own = gr.astype(F32)
    first_out[...] = jnp.concatenate([own[0:cols], gr_s[0:8], none], 0).astype(BF)
    last_out[...] = jnp.concatenate([own[tokens - cols :], gr_s[8 * rows - 8 :], none], 0).astype(BF)


def residual_block(core, home, resid, go, resid_s, go_s, mid):
    tokens, width = resid.shape
    hid = mid.shape[1]
    lanes = 512
    beside = resid_s.shape[0]
    shapes = [(tokens, width), (tokens, width), (beside, width), (48, width), (48, width)]
    vmem = pl.BlockSpec(memory_space=pltpu.VMEM)
    return pl.pallas_call(
        residual_kernel,
        name="residual_project",
        in_specs=[
            pl.BlockSpec(memory_space=pltpu.SMEM), *[vmem] * 5, pl.BlockSpec(memory_space=pl.ANY)
        ],
        out_specs=[vmem] * 7,
        out_shape=[
            *[jax.ShapeDtypeStruct(shape, BF) for shape in shapes],
            jax.ShapeDtypeStruct((hid // 2, width), F32),
            jax.ShapeDtypeStruct((hid // 2, width), BF),
        ],
        scratch_shapes=[
            pltpu.VMEM((tokens, 128), F32),
            pltpu.VMEM((width // 128, beside, 128), F32),
            pltpu.VMEM((hid // lanes, tokens, lanes), BF),
            pltpu.VMEM((lanes, width), F32),
            pltpu.SemaphoreType.DMA((hid // lanes,)),
        ],
        compiler_params=pltpu.CompilerParams(vmem_limit_bytes=20 * MIB),
        cost_estimate=pl.CostEstimate(
            flops=2 * 512 * 512 * 2048, bytes_accessed=7 * 2**20, transcendentals=0
        ),
    )(core, home, *in_hbm(resid, go, resid_s), go_s, *in_hbm(mid))


def pack(rows, width):
    blocks = rows.reshape(8, 2, 8, -1)
    low, high = [blocks[:, i].reshape(64, -1) for i in range(2)]
    more = low[:, width:] + pltpu.roll(high[:, width:], 64, 1)
    return jnp.concatenate([low[:, :width], high[:, :width], more], 1)


BACK = 512


def backward_kernel(
    core_ref, x_ref, gr_ref, above_ref, below_ref, side_ref, act_ref, slope_c_ref, slope_e_ref,
    wd_ref, wp_ref,
    gpre, mine_out, other_out,
    wide, grad_wide, normed, gmid, full, taps_t,
):
    rows, cols = 16, 32
    width = x_ref.shape[1]

    @pl.when(pl.program_id(0) == 0)
    def _():
        wide[0] = above_ref[0:WIDE, :].astype(F32)
        wide[rows + 1] = below_ref[0:WIDE, :].astype(F32)
        wide[1 : 1 + rows, 0:cols, :] = gr_ref[...].astype(F32).reshape(rows, cols, width)
        wide[1 : 1 + rows, cols:, :] = side_ref[...].astype(F32).reshape(rows, 8, width)
        grad_wide[...] = wide[...].reshape(grad_wide.shape).astype(BF)
        normed[...] = normalize(x_ref[...].astype(F32))[0].astype(BF)
        taps_t[...] = jnp.zeros(taps_t.shape, F32)

    def seen(whole):
        return roll(whole, 1)[0:cols], whole[0:cols], roll(whole, -1)[0:cols]

    for lo in range(0, BACK, 128):
        lanes = slice(lo, lo + 128)
        if lo % 256 == 0:
            both = slice(lo, lo + 256)
            gm = dot_nt(grad_wide[...], wp_ref[both, :]) * slope_c_ref[:, both].astype(F32)
            gmid[:, :, both] = gm.reshape(rows + 2, WIDE, 256)
        taps = [wd_ref[k : k + 1, lanes].astype(F32) for k in range(9)]
        lines = [seen(gmid[0, :, lanes]), seen(gmid[1, :, lanes])]
        for r in range(rows):
            lines = lines[-2:] + [seen(gmid[r + 2, :, lanes])]
            grad_act = sum(lines[2 - k // 3][2 - k % 3] * taps[k] for k in range(9))
            at = slice(r * cols, (r + 1) * cols)
            gpre[at, lanes] = (grad_act * slope_e_ref[at, lanes].astype(F32)).astype(BF)
        sums = [None] * 9
        lines = []
        for r in range(-2, rows):
            if r % 2 == 0:
                pair = act_ref[(r + 2) * WIDE : (r + 4) * WIDE, lanes].astype(F32)
            lines = lines[-2:] + [seen(pair[r % 2 * WIDE : (r % 2 + 1) * WIDE])]
            if r >= 0:
                own = gmid[r + 1, 0:cols, lanes]
                for k in range(9):
                    prod = jnp.sum((lines[k // 3][k % 3] * own).reshape(cols // 8, 8, 128), 0)
                    sums[k] = prod if r == 0 else sums[k] + prod
        for k in range(9):
            taps_t[k : k + 1, lanes] = jnp.sum(sums[k], 0, keepdims=True)
        if lo % 256:
            both = slice(lo - 128, lo + 128)
            full[both, 0:width] = dot_tn(gpre[:, both], normed[...])
            full[both, width:] = taps_t[:, both].T
            for out, core in ((mine_out, core_ref[0]), (other_out, 1 - core_ref[0])):
                at = pl.multiple_of(core * 128 + (lo - 128), 128)
                rows_out = pack(full[pl.ds(at, 128), :], width)
                out[(lo - 128) // 4 : (lo + 128) // 4, :] = rows_out.astype(out.dtype)


def backward_block(core, x, gr, near, act, slope_c, slope_e, w_depthwise, w_project):
    tokens, width = x.shape
    hid = w_project.shape[0]
    rows, cols = 16, 32
    whole = lambda a: pl.BlockSpec(a.shape, lambda j, c: (0,) * a.ndim)
    return pl.pallas_call(
        backward_kernel,
        name="mbconv_backward",
        grid_spec=pltpu.PrefetchScalarGridSpec(
            num_scalar_prefetch=1,
            grid=(hid // BACK,),
            in_specs=[
                whole(x), whole(gr), *[whole(a) for a in near],
                pl.BlockSpec(((rows + 2) * WIDE, BACK), lambda j, c: (0, j)),
                pl.BlockSpec(((rows + 2) * WIDE, BACK), lambda j, c: (0, j)),
                pl.BlockSpec((tokens, BACK), lambda j, c: (0, j)),
                pl.BlockSpec((9, BACK), lambda j, c: (0, j)),
                pl.BlockSpec((BACK, width), lambda j, c: (j, 0)),
            ],
            out_specs=[
                pl.BlockSpec((tokens, BACK), lambda j, c: (0, j)),
                pl.BlockSpec((BACK // 4, 2 * width + 128), lambda j, c: (j, 0)),
                pl.BlockSpec((BACK // 4, 2 * width + 128), lambda j, c: (j, 0)),
            ],
            scratch_shapes=[
                pltpu.VMEM((rows + 2, WIDE, width), F32),
                pltpu.VMEM(((rows + 2) * WIDE, width), BF),
                pltpu.VMEM((tokens, width), BF),
                pltpu.VMEM((rows + 2, WIDE, BACK), F32),
                pltpu.VMEM((BACK, width + 128), F32),
                pltpu.VMEM((128, BACK), F32),
            ],
        ),
        out_shape=[
            pltpu.HBM((tokens, hid), BF),
            jax.ShapeDtypeStruct((hid // 4, 2 * width + 128), F32),
            jax.ShapeDtypeStruct((hid // 4, 2 * width + 128), BF),
        ],
        compiler_params=pltpu.CompilerParams(vmem_limit_bytes=24 * MIB),
        cost_estimate=pl.CostEstimate(
            flops=16 * 512 * 512 * 2048, bytes_accessed=20 * 2**20, transcendentals=2**20
        ),
    )(core, *in_hbm(x), gr, *near, *in_hbm(act, slope_c, slope_e, w_depthwise, w_project))


def input_kernel(gpre_ref, we_ref, x_ref, gr_ref, gx_out):
    back = normalize_back(x_ref[...].astype(F32), dot_nt(gpre_ref[...], we_ref[...]))
    gx_out[...] = (gr_ref[...].astype(F32) + back).astype(BF)


def input_grads(gpre, w_expand, x, gr):
    tokens, width = x.shape
    hid = w_expand.shape[1]
    tile = 128
    return pl.pallas_call(
        input_kernel,
        name="grad_input",
        grid=(tokens // tile,),
        in_specs=[
            pl.BlockSpec((tile, hid), lambda i: (i, 0)),
            pl.BlockSpec((width, hid), lambda i: (0, 0)),
            pl.BlockSpec((tile, width), lambda i: (i, 0)),
            pl.BlockSpec((tile, width), lambda i: (i, 0)),
        ],
        out_specs=pl.BlockSpec((tile, width), lambda i: (i, 0)),
        out_shape=jax.ShapeDtypeStruct((tokens, width), BF),
        compiler_params=pltpu.CompilerParams(vmem_limit_bytes=12 * MIB),
        cost_estimate=pl.CostEstimate(
            flops=4 * 512 * 512 * 2048, bytes_accessed=6 * 2**20, transcendentals=0
        ),
    )(*in_hbm(gpre, w_expand, x, gr))


def finish_kernel(parts_ref, expand_out, depth_out):
    total = jnp.sum(parts_ref[...].astype(F32), 0)
    own, width = expand_out.shape
    expand_out[0 : own // 2, :] = total[:, 0:width]
    expand_out[own // 2 :, :] = total[:, width : 2 * width]
    more = total[:, 2 * width :]
    rows = [more, pltpu.roll(more, 64, 1), jnp.zeros((128 - own, 128), F32)]
    depth_out[...] = jnp.concatenate(rows, 0).T[0:9, 0:own]


def finish(parts):
    own, width = 2 * parts.shape[1], (parts.shape[2] - 128) // 2
    return pl.pallas_call(
        finish_kernel,
        name="last_sum",
        out_shape=[
            pltpu.HBM((own, width), F32),
            pltpu.HBM((9, own), F32),
        ],
        compiler_params=pltpu.CompilerParams(vmem_limit_bytes=10 * MIB),
    )(parts)


def attention_grads_kernel(
    core_ref, arrived_ref, gqkv_ref, att_ref, mine_out, other_out, qkv, outp, half_q, half_o, full
):
    width = att_ref.shape[1]
    qkv[...] = dot_tn(gqkv_ref[...], arrived_ref[:, 0:width])
    outp[...] = dot_tn(arrived_ref[:, width:], att_ref[...])
    nq, no = qkv.shape[0] // 16, outp.shape[0] // 16
    for j in range(8):
        for own in (True, False):
            core = core_ref[0] if own else 1 - core_ref[0]
            half_q[...] = qkv[pl.ds(pl.multiple_of((2 * j + core) * nq, 8), nq), :]
            half_o[...] = outp[pl.ds(pl.multiple_of((2 * j + core) * no, 8), no), :]
            for k in range(8):
                full[16 * k : 16 * k + 12, :] = half_q[12 * k : 12 * k + 12, :]
                full[16 * k + 12 : 16 * k + 16, :] = half_o[4 * k : 4 * k + 4, :]
            at = slice(128 * j, 128 * j + 128)
            if own:
                mine_out[at, :] = full[...]
            else:
                other_out[at, :] = full[...].astype(BF)


def attention_grads(core, arrived, gqkv, attended):
    tokens, width = attended.shape
    vmem = pl.BlockSpec(memory_space=pltpu.VMEM)
    return pl.pallas_call(
        attention_grads_kernel,
        name="attention_grads",
        in_specs=[pl.BlockSpec(memory_space=pltpu.SMEM), vmem, vmem, vmem],
        out_specs=[vmem, vmem],
        out_shape=[
            jax.ShapeDtypeStruct((1024, width), F32),
            jax.ShapeDtypeStruct((1024, width), BF),
        ],
        scratch_shapes=[
            pltpu.VMEM((3 * width, width), F32),
            pltpu.VMEM((width, width), F32),
            pltpu.VMEM((96, width), F32),
            pltpu.VMEM((32, width), F32),
            pltpu.VMEM((128, width), F32),
        ],
        compiler_params=pltpu.CompilerParams(vmem_limit_bytes=14 * MIB),
        cost_estimate=pl.CostEstimate(
            flops=8 * 512 * 512 * 512, bytes_accessed=8 * 2**20, transcendentals=0
        ),
    )(core, *in_hbm(arrived, gqkv, attended))


def add_pair(mine, other):
    got = lax.ppermute(other, AX, other_core())
    return (mine + got.astype(F32)).astype(BF).reshape(64, mine.shape[0] // 64, -1)


def body(block_input, w_expand, w_depthwise, w_project, w_qkv, w_out, grad_out):
    _, rows, cols, width = block_input.shape
    tokens = rows * cols
    core = (lax.axis_index("row") % 2).astype(jnp.int32).reshape(1)
    col = lax.axis_index("col").astype(jnp.int32).reshape(1)
    image = block_input[0]
    x = image.reshape(tokens, width)
    go = grad_out[0].reshape(tokens, width)
    act0 = expand_block(x, w_expand, gelu, 0, 2)
    centre = expand_block(x, w_expand, gelu, 1, 2, act0)
    strips, go_side = halo(image, 2, act0, grad_out[0])
    mid, resid, send = forward_block(x, strips, go, centre, w_expand, w_depthwise, w_project)
    arrived = across_chips(send.reshape(64, 8, 2 * width)).reshape(tokens, 2 * width)
    slopes = slopes_block(strips, centre, w_expand, w_depthwise, w_project)
    arrived, (act, slope_c, resid_side) = lax.optimization_barrier((arrived, slopes))
    back, gqkv, attended = attention_block(col, arrived, w_qkv, w_out)
    home = across_chips(back.reshape(64, 8, -1)).reshape(tokens, -1)
    slope_e = expand_block(x, w_expand, gelu_slope, 0, 1)
    attention_pair = add_pair(*attention_grads(core, arrived, gqkv, attended))
    home, slope_e = lax.optimization_barrier((home, slope_e))
    out, gr, side, first_row, last_row, mine, other = residual_block(
        core, home, resid, go, resid_side, go_side, mid
    )
    above, below = shift(last_row, "row", 1), shift(first_row, "row", -1)
    project_pair = add_pair(mine, other)
    first = jnp.concatenate([project_pair, attention_pair], 1)
    above, below, first = lax.optimization_barrier((above, below, first))
    first = across_chips(first)
    gpre, mine, other = backward_block(
        core, x, gr, (above, below, side), act, slope_c, slope_e, w_depthwise, w_project
    )
    gx = input_grads(gpre, w_expand, x, gr)
    second = add_pair(mine, other)
    second, first = lax.optimization_barrier((second, first))
    grad_expand, grad_depth = finish(across_chips(second))
    first = jnp.sum(first.astype(F32), 0)
    return (
        out.reshape(1, rows, cols, width),
        gx.reshape(1, rows, cols, width),
        grad_expand.T,
        grad_depth,
        first[:16].T,
        first[16:28].T,
        first[28:].T,
    )


def solution(mesh):
    tokens = P(None, "row", "col", None)
    split = P(None, AX)
    return jax.shard_map(
        body,
        mesh=mesh,
        in_specs=(tokens, P(), P(), P(), P(), P(), tokens),
        out_specs=(tokens, tokens, split, split, split, split, split),
        check_vma=False,
    )
```

```python
import functools
import itertools

import jax
import jax.numpy as jnp
from jax import lax
from jax.experimental import pallas as pl
from jax.experimental.pallas import tpu as pltpu
from jax.sharding import PartitionSpec as P

HEADS = 16
HDIM = 32
EPS = 1e-05
BF = jnp.bfloat16
F32 = jnp.float32
AX = ("row", "col")
WIDE = 40
CHUNK = 256
MIB = 2**20

SIZES = dict(y_lo=2, z=4, core=2, x=4, y_hi=2)
STRIDES = dict(y_lo=64, z=16, core=8, x=2, y_hi=1)
CHIPS = ("y_lo", "z", "x", "y_hi")


def device_groups(axes):
    rest = [a for a in SIZES if a not in axes]
    found = []
    for at in itertools.product(*[range(SIZES[a]) for a in rest]):
        base = sum(v * STRIDES[a] for v, a in zip(at, rest))
        found.append(
            [
                base + sum(v * STRIDES[a] for v, a in zip(m, axes))
                for m in itertools.product(*[range(SIZES[a]) for a in axes])
            ]
        )
    return found


def other_core():
    return [(d, d ^ STRIDES["core"]) for d in range(128)]


def across_chips(x):
    return lax.all_to_all(x, AX, 0, 0, tiled=True, axis_index_groups=device_groups(CHIPS))


def shift(x, axis, step):
    n = lax.axis_size(axis)
    pairs = [(i, i + step) for i in range(n) if 0 <= i + step < n]
    return lax.ppermute(x, axis, pairs)


def halo(x, width, ahead, beside):
    rows, cols, chans = x.shape
    above = shift(x[rows - width :], "row", 1)
    below = shift(x[:width], "row", -1)
    above, below, _ = lax.optimization_barrier((above, below, ahead))
    flat = lambda v: v.reshape(-1, chans)

    def column(at):
        parts = [above[:, at], x[:, at], below[:, at], beside[:, at]]
        return jnp.concatenate([flat(p) for p in parts], 0)

    left = shift(column(slice(cols - width, cols)), "col", 1)
    right = shift(column(slice(0, width)), "col", -1)
    n = (rows + 2 * width) * width

    def sides(right, left):
        right, left = [v.reshape(-1, width, chans) for v in (right, left)]
        gap = jnp.zeros((right.shape[0], 8 - 2 * width, chans), x.dtype)
        return flat(jnp.concatenate([right, gap, left], 1))

    strips = [flat(above), flat(below), sides(right[:n], left[:n])]
    return jnp.concatenate(strips, 0), sides(right[n:], left[n:])


def place(wide, centre, strips, width, rows, cols):
    lanes = strips.shape[-1]
    n = width * cols
    if centre is not None:
        wide[width : width + rows, 0:cols, :] = centre.reshape(rows, cols, lanes)
    wide[0:width, 0:cols, :] = strips[0:n].reshape(width, cols, lanes)
    wide[width + rows :, 0:cols, :] = strips[n : 2 * n].reshape(width, cols, lanes)
    wide[:, cols:, :] = strips[2 * n :].reshape(rows + 2 * width, WIDE - cols, lanes)


def normalize(x):
    center = x - jnp.mean(x, -1, keepdims=True)
    ratio = lax.rsqrt(jnp.mean(center * center, -1, keepdims=True) + EPS)
    return center * ratio, ratio


def normalize_back(x, grad):
    scaled, ratio = normalize(x)
    return (
        grad
        - jnp.mean(grad, -1, keepdims=True)
        - scaled * jnp.mean(grad * scaled, -1, keepdims=True)
    ) * ratio


A0 = 0.7978845608028654
A1 = A0 * 0.044715


def gelu_half(x):
    inner = A0 + A1 * (x * x)
    return inner, 0.5 + 0.5 * jnp.tanh(x * inner)


def gelu(x):
    return x * gelu_half(x)[1]


def gelu_slope(x):
    inner, half = gelu_half(x)
    value = x * half
    return half + (value - value * half) * (6.0 * inner - 4.0 * A0)


def dot(a, b):
    return jnp.dot(a, b, preferred_element_type=F32)


def dot_nt(a, b):
    return lax.dot_general(a, b, (((1,), (1,)), ((), ())), preferred_element_type=F32)


def dot_tn(a, b):
    return lax.dot_general(a, b, (((0,), (0,)), ((), ())), preferred_element_type=F32)


def in_hbm(*arrays):
    return [pltpu.with_memory_space_constraint(a, pltpu.HBM) for a in arrays]


def roll(x, by):
    return pltpu.roll(x, by % x.shape[0], 0)


def expand_kernel(apply, x_ref, we_ref, *refs):
    act_out, normed = refs[-2:]

    @pl.when(pl.program_id(0) == 0)
    def _():
        normed[...] = normalize(x_ref[...].astype(F32))[0].astype(BF)

    for tile in range(0, x_ref.shape[0], 128):
        at = slice(tile, tile + 128)
        act_out[at, :] = apply(dot(normed[at, :], we_ref[...])).astype(BF)


def expand_block(x, w_expand, apply, part, parts, held=None):
    tokens, width = x.shape
    hid = w_expand.shape[1]
    lanes = 512
    steps = hid // lanes // parts
    held = [] if held is None else [held]
    return pl.pallas_call(
        functools.partial(expand_kernel, apply),
        name=apply.__name__ + "_expand",
        grid=(steps,),
        in_specs=[
            pl.BlockSpec((tokens, width), lambda j: (0, 0)),
            pl.BlockSpec((width, lanes), lambda j: (0, j + part * steps)),
            *[pl.BlockSpec(memory_space=pl.ANY) for _ in held],
        ],
        out_specs=pl.BlockSpec((tokens, lanes), lambda j: (0, j + part * steps)),
        out_shape=pltpu.HBM((tokens, hid), BF),
        scratch_shapes=[pltpu.VMEM((tokens, width), BF)],
        input_output_aliases={2: 0} if held else {},
        compiler_params=pltpu.CompilerParams(vmem_limit_bytes=8 * MIB),
        cost_estimate=pl.CostEstimate(
            flops=8 * 512 * 512 * 2048, bytes_accessed=3 * 2**20, transcendentals=2**19
        ),
    )(*in_hbm(x, w_expand), *held)


FORWARD = 512


def forward_kernel(
    x_hbm, strips_ref, go_hbm, act_ref, we_ref, wd_ref, wp_ref,
    mid_out, resid_out, send_out,
    normed, edge, acc, x_ref, go_ref, sems,
):
    step = pl.program_id(0)
    rows, cols = 16, 32
    width = x_ref.shape[1]
    load_x = pltpu.make_async_copy(x_hbm, x_ref, sems.at[0])
    load_go = pltpu.make_async_copy(go_hbm, go_ref, sems.at[1])

    @pl.when(step == 0)
    def _():
        load_x.start()
        load_go.start()
        every = normalize(strips_ref[...].astype(F32))[0]
        sides = 4 * cols + 8
        near = [every[cols : 3 * cols], every[sides : sides + 8 * (rows + 2)]]
        normed[...] = jnp.concatenate(near, 0).astype(BF)

    edge[...] = gelu(dot(normed[...], we_ref[...]))
    for lo in range(0, FORWARD, 128):
        lanes = slice(lo, lo + 128)
        taps = [wd_ref[k : k + 1, lanes].astype(F32) for k in range(9)]

        def line(r):
            if r == 0:
                centre = edge[0:cols, lanes]
            elif r == rows + 1:
                centre = edge[cols : 2 * cols, lanes]
            else:
                centre = act_ref[(r - 1) * cols : r * cols, lanes].astype(F32)
            side = edge[2 * cols + 8 * r : 2 * cols + 8 * (r + 1), lanes]
            whole = jnp.concatenate([centre, side], 0)
            return roll(whole, 1)[0:cols], centre, roll(whole, -1)[0:cols]

        lines = [line(0), line(1)]
        for r in range(rows):
            lines = lines[-2:] + [line(r + 2)]
            conv = sum(lines[k // 3][k % 3] * taps[k] for k in range(9))
            mid_out[r * cols : (r + 1) * cols, lanes] = gelu(conv).astype(BF)
        if lo % 256:
            at = slice(lo - 128, lo + 128)
            part = dot(mid_out[:, at], wp_ref[at, :])
            product = part if lo == 128 else product + part

    @pl.when(step == 0)
    def _():
        acc[...] = product

    @pl.when(step > 0)
    def _():
        acc[...] += product

    @pl.when(step == pl.num_programs(0) - 1)
    def _():
        load_x.wait()
        resid = (x_ref[...].astype(F32) + acc[...]).astype(BF)
        resid_out[...] = resid
        send_out[:, 0:width] = normalize(resid.astype(F32))[0].astype(BF)
        load_go.wait()
        send_out[:, width:] = go_ref[...]


def forward_block(x, strips, go, act, w_expand, w_depthwise, w_project):
    tokens, width = x.shape
    hid = w_expand.shape[1]
    rows, cols = 16, 32
    near = 2 * cols + 8 * (rows + 2)
    anywhere = pl.BlockSpec(memory_space=pl.ANY)
    whole = lambda a: pl.BlockSpec(a.shape, lambda j: (0,) * a.ndim)
    return pl.pallas_call(
        forward_kernel,
        name="mbconv_forward",
        grid=(hid // FORWARD,),
        in_specs=[
            anywhere, whole(strips), anywhere,
            pl.BlockSpec((tokens, FORWARD), lambda j: (0, j)),
            pl.BlockSpec((width, FORWARD), lambda j: (0, j)),
            pl.BlockSpec((9, FORWARD), lambda j: (0, j)),
            pl.BlockSpec((FORWARD, width), lambda j: (j, 0)),
        ],
        out_specs=[
            pl.BlockSpec((tokens, FORWARD), lambda j: (0, j)),
            pl.BlockSpec((tokens, width), lambda j: (0, 0)),
            pl.BlockSpec((tokens, 2 * width), lambda j: (0, 0)),
        ],
        out_shape=[
            pltpu.HBM((tokens, hid), BF),
            pltpu.HBM((tokens, width), BF),
            pltpu.HBM((tokens, 2 * width), BF),
        ],
        scratch_shapes=[
            pltpu.VMEM((near, width), BF),
            pltpu.VMEM((near, FORWARD), F32),
            pltpu.VMEM((tokens, width), F32),
            pltpu.VMEM((tokens, width), BF),
            pltpu.VMEM((tokens, width), BF),
            pltpu.SemaphoreType.DMA((2,)),
        ],
        compiler_params=pltpu.CompilerParams(vmem_limit_bytes=18 * MIB),
        cost_estimate=pl.CostEstimate(
            flops=2 * 700 * 512 * 2048, bytes_accessed=10 * 2**20, transcendentals=2**20
        ),
    )(*in_hbm(x), strips, *in_hbm(go, act, w_expand, w_depthwise, w_project))


SLOPES = 512


def slopes_kernel(
    strips_ref, centre_ref, we_ref, wd_ref, wp_ref,
    act_out, slope_out, resid_out,
    normed, edge, beside, acc,
):
    rows, cols = 16, 32

    @pl.when(pl.program_id(0) == 0)
    def _():
        acc[...] = jnp.zeros(acc.shape, F32)
        normed[...] = normalize(strips_ref[...].astype(F32))[0].astype(BF)

    edge[...] = gelu(dot(normed[...], we_ref[...]))
    for lo in range(0, SLOPES, 128):
        lanes = slice(lo, lo + 128)
        taps = [wd_ref[k : k + 1, lanes].astype(F32) for k in range(9)]

        def line(r):
            if r < 2:
                centre = edge[r * cols : (r + 1) * cols, lanes]
            elif r < rows + 2:
                centre = centre_ref[(r - 2) * cols : (r - 1) * cols, lanes].astype(F32)
            else:
                centre = edge[(r - rows) * cols : (r - rows + 1) * cols, lanes]
            side = edge[4 * cols + 8 * r : 4 * cols + 8 * (r + 1), lanes]
            return jnp.concatenate([centre, side], 0)

        lines = [line(0), line(1)]
        held = None
        for r in range(rows + 2):
            lines = lines[-2:] + [line(r + 2)]
            sums = [sum(lines[i] * taps[3 * i + j] for i in range(3)) for j in range(3)]
            conv = sums[1] + roll(sums[0], 1) + roll(sums[2], -1)
            slope = gelu_slope(conv)
            if 1 <= r <= rows:
                beside[8 * (r - 1) : 8 * r, lanes] = gelu(conv[cols:])
            if r % 2:
                at = slice((r - 1) * WIDE, (r + 1) * WIDE)
                act_out[at, lanes] = jnp.concatenate(lines[:2], 0).astype(BF)
                slope_out[at, lanes] = jnp.concatenate([held, slope], 0).astype(BF)
            held = slope
    acc[...] += dot(beside[...].astype(BF), wp_ref[...])

    @pl.when(pl.program_id(0) == pl.num_programs(0) - 1)
    def _():
        at = 2 * (2 * cols) + 2 * 8
        resid_out[...] = (strips_ref[at : at + 8 * rows, :].astype(F32) + acc[...]).astype(BF)


def slopes_block(strips, centre, w_expand, w_depthwise, w_project):
    tokens, hid = centre.shape
    width = strips.shape[1]
    rows = 16
    wide = (rows + 2) * WIDE
    return pl.pallas_call(
        slopes_kernel,
        name="gelu_slopes",
        grid=(hid // SLOPES,),
        in_specs=[
            pl.BlockSpec(strips.shape, lambda j: (0, 0)),
            pl.BlockSpec((tokens, SLOPES), lambda j: (0, j)),
            pl.BlockSpec((width, SLOPES), lambda j: (0, j)),
            pl.BlockSpec((9, SLOPES), lambda j: (0, j)),
            pl.BlockSpec((SLOPES, width), lambda j: (j, 0)),
        ],
        out_specs=[
            pl.BlockSpec((wide, SLOPES), lambda j: (0, j)),
            pl.BlockSpec((wide, SLOPES), lambda j: (0, j)),
            pl.BlockSpec((8 * rows, width), lambda j: (0, 0)),
        ],
        out_shape=[
            pltpu.HBM((wide, hid), BF),
            pltpu.HBM((wide, hid), BF),
            pltpu.HBM((8 * rows, width), BF),
        ],
        scratch_shapes=[
            pltpu.VMEM(strips.shape, BF),
            pltpu.VMEM((strips.shape[0], SLOPES), F32),
            pltpu.VMEM((8 * rows, SLOPES), F32),
            pltpu.VMEM((8 * rows, width), F32),
        ],
        compiler_params=pltpu.CompilerParams(vmem_limit_bytes=18 * MIB),
        cost_estimate=pl.CostEstimate(
            flops=2 * 10**10, bytes_accessed=12 * 2**20, transcendentals=3 * 2**20
        ),
    )(strips, *in_hbm(centre, w_expand, w_depthwise, w_project))


def attention_kernel(
    col_ref, in_ref, wq_hbm, wo_hbm, send_hbm, gq_hbm, att_hbm,
    wq, wo, qkv, gatt, att, gq, send, gqb, attended, edge, sems,
):
    tokens, width = attended.shape
    groups = 8
    members = tokens // groups
    quads = width // 128
    scale = HDIM ** (-0.5)
    load_wo = pltpu.make_async_copy(wo_hbm, wo, sems.at[0])
    load_wq = pltpu.make_async_copy(wq_hbm, wq, sems.at[1])
    load_wo.start()
    load_wq.start()

    def put(ref, at, value):
        value = value.astype(BF).astype(F32)
        for quad in range(quads):
            ref[at + quad] = value[:, quad * 128 : (quad + 1) * 128]

    load_wo.wait()
    put(gatt, 0, dot_nt(in_ref[:, width:], wo[...]))
    load_wq.wait()
    for part in range(3):
        lanes = slice(part * width, (part + 1) * width)
        put(qkv, part * quads, dot(in_ref[:, 0:width], wq[:, lanes]))
    per = 128 // HDIM
    head = lax.broadcasted_iota(jnp.int32, (members, 128), 1) // HDIM

    def spread(v):
        return jnp.concatenate([jnp.where(head == h, v, 0.0) for h in range(per)], 0).astype(BF)

    def gather(v):
        out = jnp.where(head == 0, v[0:members], 0.0)
        for h in range(1, per):
            out = jnp.where(head == h, v[h * members : (h + 1) * members], out)
        return out

    def one_group(g, _):
        at = pl.ds(g, members, stride=groups)
        every = range(quads)
        q = [spread(qkv[i, at, :]) for i in every]
        k = [qkv[quads + i, at, :].astype(BF) for i in every]
        v = [qkv[2 * quads + i, at, :].astype(BF) for i in every]
        do = [spread(gatt[i, at, :]) for i in every]
        scores = [dot_nt(k[i], q[i]) * scale for i in every]
        dp = [dot_nt(v[i], do[i]) for i in every]
        p = [jnp.exp(s - jnp.max(s, 0, keepdims=True)) for s in scores]
        p = [e * (1.0 / jnp.sum(e, 0, keepdims=True)) for e in p]
        pb = [e.astype(BF) for e in p]
        ds = [
            (p[i] * (dp[i] - jnp.sum(p[i] * dp[i], 0, keepdims=True)) * scale).astype(BF)
            for i in every
        ]
        for i in every:
            att[i, at, :] = gather(dot_tn(pb[i], v[i]))
            gq[i, at, :] = gather(dot_tn(ds[i], k[i]))
            gq[quads + i, at, :] = dot(ds[i], q[i])
            gq[2 * quads + i, at, :] = dot(pb[i], do[i])
        return 0

    lax.fori_loop(0, groups, one_group, 0, unroll=True)
    attended[...] = jnp.concatenate([att[i] for i in range(quads)], 1).astype(BF)
    store_att = pltpu.make_async_copy(attended, att_hbm, sems.at[2])
    store_att.start()
    gqb[...] = jnp.concatenate([gq[i] for i in range(3 * quads)], 1).astype(BF)
    store_gq = pltpu.make_async_copy(gqb, gq_hbm, sems.at[3])
    store_gq.start()
    grad = dot_nt(gqb[...], wq[...])
    send[:, width : 2 * width] = grad.astype(BF)
    put(gatt, 0, grad)
    place = lax.broadcasted_iota(jnp.int32, (members, 128), 0) % 8
    last = col_ref[0] % 4 == 3
    for i in range(quads):
        first_col = gatt[i, pl.ds(0, members, stride=groups), :]
        last_col = gatt[i, pl.ds(groups - 1, members, stride=groups), :]
        to_left = jnp.where(place == 7, 0.0, roll(first_col, -1))
        to_right = jnp.where(place == 0, 0.0, roll(last_col, 1))
        found = jnp.where(last, to_right, to_left)
        edge[pl.ds(2 * i, members, stride=groups), :] = found
        edge[pl.ds(2 * i + 1, members, stride=groups), :] = pltpu.roll(found, 64, 1)
    send[:, 2 * width :] = edge[...].astype(BF)
    send[:, 0:width] = dot(attended[...], wo[...]).astype(BF)
    store_send = pltpu.make_async_copy(send, send_hbm, sems.at[4])
    store_send.start()
    for store in [store_att, store_gq, store_send]:
        store.wait()


def attention_block(col, arrived, w_qkv, w_out):
    tokens = arrived.shape[0]
    width = w_out.shape[0]
    anywhere = pl.BlockSpec(memory_space=pl.ANY)
    return pl.pallas_call(
        attention_kernel,
        name="grid_attention",
        in_specs=[
            pl.BlockSpec(memory_space=pltpu.SMEM), pl.BlockSpec(memory_space=pltpu.VMEM), anywhere, anywhere
        ],
        out_specs=[anywhere] * 3,
        out_shape=[
            pltpu.HBM((tokens, 2 * width + 128), BF),
            pltpu.HBM((tokens, 3 * width), BF),
            pltpu.HBM((tokens, width), BF),
        ],
        scratch_shapes=[
            pltpu.VMEM((width, 3 * width), BF),
            pltpu.VMEM((width, width), BF),
            pltpu.VMEM((3 * width // 128, tokens, 128), F32),
            pltpu.VMEM((width // 128, tokens, 128), F32),
            pltpu.VMEM((width // 128, tokens, 128), F32),
            pltpu.VMEM((3 * width // 128, tokens, 128), F32),
            pltpu.VMEM((tokens, 2 * width + 128), BF),
            pltpu.VMEM((tokens, 3 * width), BF),
            pltpu.VMEM((tokens, width), BF),
            pltpu.VMEM((tokens, 128), F32),
            pltpu.SemaphoreType.DMA((5,)),
        ],
        compiler_params=pltpu.CompilerParams(vmem_limit_bytes=24 * MIB),
        cost_estimate=pl.CostEstimate(
            flops=2 * 512 * 512 * 512 * 8, bytes_accessed=7 * 2**20, transcendentals=2**20
        ),
    )(col, arrived, *in_hbm(w_qkv, w_out))


def residual_kernel(
    core_ref, home_ref, resid_ref, go_ref, resid_s_ref, go_s_ref, mid_hbm,
    out_ref, gr_ref, side_out, first_out, last_out, mine_out, other_out,
    packed, side, mid, full, sems,
):
    steps, _, lanes = mid.shape
    loads = [
        pltpu.make_async_copy(mid_hbm.at[:, pl.ds(lanes * i, lanes)], mid.at[i], sems.at[i])
        for i in range(steps)
    ]
    for load in loads:
        load.start()
    residual_step(
        home_ref, resid_ref, go_ref, resid_s_ref, go_s_ref,
        out_ref, gr_ref, side_out, first_out, last_out, packed, side,
    )
    half = 128
    for i in range(steps):
        loads[i].wait()
        full[...] = dot_tn(mid[i], gr_ref[...])
        for j in range(lanes // (2 * half)):
            at = i * lanes // 2 + j * half
            own = pl.multiple_of((2 * j + core_ref[0]) * half, half)
            other = pl.multiple_of((2 * j + 1 - core_ref[0]) * half, half)
            mine_out[at : at + half, :] = full[pl.ds(own, half), :]
            other_out[at : at + half, :] = full[pl.ds(other, half), :].astype(BF)


def residual_step(
    home_ref, resid_ref, go_ref, resid_s_ref, go_s_ref, out_ref, gr_ref, side_out, first_out, last_out,
    packed, side,
):
    tokens, width = resid_ref.shape
    rows, cols = 16, 32
    resid = resid_ref[...].astype(F32)
    out_ref[...] = (resid + home_ref[:, 0:width].astype(F32)).astype(BF)
    back = normalize_back(resid, home_ref[:, width : 2 * width].astype(F32))
    gr = (go_ref[...].astype(F32) + back).astype(BF)
    gr_ref[...] = gr
    packed[...] = home_ref[:, 2 * width :].astype(F32)
    side[...] = jnp.zeros(side.shape, F32)
    low = lax.broadcasted_iota(jnp.int32, (rows, 128), 1) < 64
    for i in range(width // 128):
        for at, start in ((0, 0), (7, cols - 8)):
            even = packed[pl.ds(start + 2 * i, rows, stride=cols), :]
            odd = packed[pl.ds(start + 2 * i + 1, rows, stride=cols), :]
            side[i, pl.ds(at, rows, stride=8), :] = jnp.where(low, even, pltpu.roll(odd, 64, 1))
    grad = jnp.concatenate([side[i] for i in range(width // 128)], 1)
    back = normalize_back(resid_s_ref[...].astype(F32), grad)
    gr_s = (go_s_ref[...].astype(F32) + back).astype(BF).astype(F32)
    side_out[...] = gr_s.astype(BF)
    none = jnp.zeros((8, width), F32)
    own = gr.astype(F32)
    first_out[...] = jnp.concatenate([own[0:cols], gr_s[0:8], none], 0).astype(BF)
    last_out[...] = jnp.concatenate([own[tokens - cols :], gr_s[8 * rows - 8 :], none], 0).astype(BF)


def residual_block(core, home, resid, go, resid_s, go_s, mid):
    tokens, width = resid.shape
    hid = mid.shape[1]
    lanes = 512
    beside = resid_s.shape[0]
    shapes = [(tokens, width), (tokens, width), (beside, width), (48, width), (48, width)]
    vmem = pl.BlockSpec(memory_space=pltpu.VMEM)
    return pl.pallas_call(
        residual_kernel,
        name="residual_project",
        in_specs=[
            pl.BlockSpec(memory_space=pltpu.SMEM), *[vmem] * 5, pl.BlockSpec(memory_space=pl.ANY)
        ],
        out_specs=[vmem] * 7,
        out_shape=[
            *[jax.ShapeDtypeStruct(shape, BF) for shape in shapes],
            jax.ShapeDtypeStruct((hid // 2, width), F32),
            jax.ShapeDtypeStruct((hid // 2, width), BF),
        ],
        scratch_shapes=[
            pltpu.VMEM((tokens, 128), F32),
            pltpu.VMEM((width // 128, beside, 128), F32),
            pltpu.VMEM((hid // lanes, tokens, lanes), BF),
            pltpu.VMEM((lanes, width), F32),
            pltpu.SemaphoreType.DMA((hid // lanes,)),
        ],
        compiler_params=pltpu.CompilerParams(vmem_limit_bytes=20 * MIB),
        cost_estimate=pl.CostEstimate(
            flops=2 * 512 * 512 * 2048, bytes_accessed=7 * 2**20, transcendentals=0
        ),
    )(core, home, *in_hbm(resid, go, resid_s), go_s, *in_hbm(mid))


def pack(rows, width):
    blocks = rows.reshape(8, 2, 8, -1)
    low, high = [blocks[:, i].reshape(64, -1) for i in range(2)]
    more = low[:, width:] + pltpu.roll(high[:, width:], 64, 1)
    return jnp.concatenate([low[:, :width], high[:, :width], more], 1)


BACK = 512


def backward_kernel(
    core_ref, x_ref, gr_ref, above_ref, below_ref, side_ref, act_ref, slope_c_ref, slope_e_ref,
    wd_ref, wp_ref,
    gpre, mine_out, other_out,
    wide, grad_wide, normed, gmid, full, taps_t,
):
    rows, cols = 16, 32
    width = x_ref.shape[1]

    @pl.when(pl.program_id(0) == 0)
    def _():
        wide[0] = above_ref[0:WIDE, :].astype(F32)
        wide[rows + 1] = below_ref[0:WIDE, :].astype(F32)
        wide[1 : 1 + rows, 0:cols, :] = gr_ref[...].astype(F32).reshape(rows, cols, width)
        wide[1 : 1 + rows, cols:, :] = side_ref[...].astype(F32).reshape(rows, 8, width)
        grad_wide[...] = wide[...].reshape(grad_wide.shape).astype(BF)
        normed[...] = normalize(x_ref[...].astype(F32))[0].astype(BF)
        taps_t[...] = jnp.zeros(taps_t.shape, F32)

    def seen(whole):
        return roll(whole, 1)[0:cols], whole[0:cols], roll(whole, -1)[0:cols]

    for lo in range(0, BACK, 128):
        lanes = slice(lo, lo + 128)
        if lo % 256 == 0:
            both = slice(lo, lo + 256)
            gm = dot_nt(grad_wide[...], wp_ref[both, :]) * slope_c_ref[:, both].astype(F32)
            gmid[:, :, both] = gm.reshape(rows + 2, WIDE, 256)
        taps = [wd_ref[k : k + 1, lanes].astype(F32) for k in range(9)]
        lines = [seen(gmid[0, :, lanes]), seen(gmid[1, :, lanes])]
        for r in range(rows):
            lines = lines[-2:] + [seen(gmid[r + 2, :, lanes])]
            grad_act = sum(lines[2 - k // 3][2 - k % 3] * taps[k] for k in range(9))
            at = slice(r * cols, (r + 1) * cols)
            gpre[at, lanes] = (grad_act * slope_e_ref[at, lanes].astype(F32)).astype(BF)
        sums = [None] * 9
        lines = []
        for r in range(-2, rows):
            if r % 2 == 0:
                pair = act_ref[(r + 2) * WIDE : (r + 4) * WIDE, lanes].astype(F32)
            lines = lines[-2:] + [seen(pair[r % 2 * WIDE : (r % 2 + 1) * WIDE])]
            if r >= 0:
                own = gmid[r + 1, 0:cols, lanes]
                for k in range(9):
                    prod = jnp.sum((lines[k // 3][k % 3] * own).reshape(cols // 8, 8, 128), 0)
                    sums[k] = prod if r == 0 else sums[k] + prod
        for k in range(9):
            taps_t[k : k + 1, lanes] = jnp.sum(sums[k], 0, keepdims=True)
        if lo % 256:
            both = slice(lo - 128, lo + 128)
            full[both, 0:width] = dot_tn(gpre[:, both], normed[...])
            full[both, width:] = taps_t[:, both].T
            for out, core in ((mine_out, core_ref[0]), (other_out, 1 - core_ref[0])):
                at = pl.multiple_of(core * 128 + (lo - 128), 128)
                rows_out = pack(full[pl.ds(at, 128), :], width)
                out[(lo - 128) // 4 : (lo + 128) // 4, :] = rows_out.astype(out.dtype)


def backward_block(core, x, gr, near, act, slope_c, slope_e, w_depthwise, w_project):
    tokens, width = x.shape
    hid = w_project.shape[0]
    rows, cols = 16, 32
    whole = lambda a: pl.BlockSpec(a.shape, lambda j, c: (0,) * a.ndim)
    return pl.pallas_call(
        backward_kernel,
        name="mbconv_backward",
        grid_spec=pltpu.PrefetchScalarGridSpec(
            num_scalar_prefetch=1,
            grid=(hid // BACK,),
            in_specs=[
                whole(x), whole(gr), *[whole(a) for a in near],
                pl.BlockSpec(((rows + 2) * WIDE, BACK), lambda j, c: (0, j)),
                pl.BlockSpec(((rows + 2) * WIDE, BACK), lambda j, c: (0, j)),
                pl.BlockSpec((tokens, BACK), lambda j, c: (0, j)),
                pl.BlockSpec((9, BACK), lambda j, c: (0, j)),
                pl.BlockSpec((BACK, width), lambda j, c: (j, 0)),
            ],
            out_specs=[
                pl.BlockSpec((tokens, BACK), lambda j, c: (0, j)),
                pl.BlockSpec((BACK // 4, 2 * width + 128), lambda j, c: (j, 0)),
                pl.BlockSpec((BACK // 4, 2 * width + 128), lambda j, c: (j, 0)),
            ],
            scratch_shapes=[
                pltpu.VMEM((rows + 2, WIDE, width), F32),
                pltpu.VMEM(((rows + 2) * WIDE, width), BF),
                pltpu.VMEM((tokens, width), BF),
                pltpu.VMEM((rows + 2, WIDE, BACK), F32),
                pltpu.VMEM((BACK, width + 128), F32),
                pltpu.VMEM((128, BACK), F32),
            ],
        ),
        out_shape=[
            pltpu.HBM((tokens, hid), BF),
            jax.ShapeDtypeStruct((hid // 4, 2 * width + 128), F32),
            jax.ShapeDtypeStruct((hid // 4, 2 * width + 128), BF),
        ],
        compiler_params=pltpu.CompilerParams(vmem_limit_bytes=24 * MIB),
        cost_estimate=pl.CostEstimate(
            flops=16 * 512 * 512 * 2048, bytes_accessed=20 * 2**20, transcendentals=2**20
        ),
    )(core, *in_hbm(x), gr, *near, *in_hbm(act, slope_c, slope_e, w_depthwise, w_project))


def input_kernel(gpre_ref, we_ref, x_ref, gr_ref, gx_out):
    back = normalize_back(x_ref[...].astype(F32), dot_nt(gpre_ref[...], we_ref[...]))
    gx_out[...] = (gr_ref[...].astype(F32) + back).astype(BF)


def input_grads(gpre, w_expand, x, gr):
    tokens, width = x.shape
    hid = w_expand.shape[1]
    tile = 128
    return pl.pallas_call(
        input_kernel,
        name="grad_input",
        grid=(tokens // tile,),
        in_specs=[
            pl.BlockSpec((tile, hid), lambda i: (i, 0)),
            pl.BlockSpec((width, hid), lambda i: (0, 0)),
            pl.BlockSpec((tile, width), lambda i: (i, 0)),
            pl.BlockSpec((tile, width), lambda i: (i, 0)),
        ],
        out_specs=pl.BlockSpec((tile, width), lambda i: (i, 0)),
        out_shape=jax.ShapeDtypeStruct((tokens, width), BF),
        compiler_params=pltpu.CompilerParams(vmem_limit_bytes=12 * MIB),
        cost_estimate=pl.CostEstimate(
            flops=4 * 512 * 512 * 2048, bytes_accessed=6 * 2**20, transcendentals=0
        ),
    )(*in_hbm(gpre, w_expand, x, gr))


def finish_kernel(parts_ref, expand_out, depth_out):
    total = jnp.sum(parts_ref[...].astype(F32), 0)
    own, width = expand_out.shape
    expand_out[0 : own // 2, :] = total[:, 0:width]
    expand_out[own // 2 :, :] = total[:, width : 2 * width]
    more = total[:, 2 * width :]
    rows = [more, pltpu.roll(more, 64, 1), jnp.zeros((128 - own, 128), F32)]
    depth_out[...] = jnp.concatenate(rows, 0).T[0:9, 0:own]


def finish(parts):
    own, width = 2 * parts.shape[1], (parts.shape[2] - 128) // 2
    return pl.pallas_call(
        finish_kernel,
        name="last_sum",
        out_shape=[
            pltpu.HBM((own, width), F32),
            pltpu.HBM((9, own), F32),
        ],
        compiler_params=pltpu.CompilerParams(vmem_limit_bytes=10 * MIB),
    )(parts)


def attention_grads_kernel(
    core_ref, arrived_ref, gqkv_ref, att_ref, mine_out, other_out, qkv, outp, half_q, half_o, full
):
    width = att_ref.shape[1]
    qkv[...] = dot_tn(gqkv_ref[...], arrived_ref[:, 0:width])
    outp[...] = dot_tn(arrived_ref[:, width:], att_ref[...])
    nq, no = qkv.shape[0] // 16, outp.shape[0] // 16
    for j in range(8):
        for own in (True, False):
            core = core_ref[0] if own else 1 - core_ref[0]
            half_q[...] = qkv[pl.ds(pl.multiple_of((2 * j + core) * nq, 8), nq), :]
            half_o[...] = outp[pl.ds(pl.multiple_of((2 * j + core) * no, 8), no), :]
            for k in range(8):
                full[16 * k : 16 * k + 12, :] = half_q[12 * k : 12 * k + 12, :]
                full[16 * k + 12 : 16 * k + 16, :] = half_o[4 * k : 4 * k + 4, :]
            at = slice(128 * j, 128 * j + 128)
            if own:
                mine_out[at, :] = full[...]
            else:
                other_out[at, :] = full[...].astype(BF)


def attention_grads(core, arrived, gqkv, attended):
    tokens, width = attended.shape
    vmem = pl.BlockSpec(memory_space=pltpu.VMEM)
    return pl.pallas_call(
        attention_grads_kernel,
        name="attention_grads",
        in_specs=[pl.BlockSpec(memory_space=pltpu.SMEM), vmem, vmem, vmem],
        out_specs=[vmem, vmem],
        out_shape=[
            jax.ShapeDtypeStruct((1024, width), F32),
            jax.ShapeDtypeStruct((1024, width), BF),
        ],
        scratch_shapes=[
            pltpu.VMEM((3 * width, width), F32),
            pltpu.VMEM((width, width), F32),
            pltpu.VMEM((96, width), F32),
            pltpu.VMEM((32, width), F32),
            pltpu.VMEM((128, width), F32),
        ],
        compiler_params=pltpu.CompilerParams(vmem_limit_bytes=14 * MIB),
        cost_estimate=pl.CostEstimate(
            flops=8 * 512 * 512 * 512, bytes_accessed=8 * 2**20, transcendentals=0
        ),
    )(core, *in_hbm(arrived, gqkv, attended))


def add_pair(mine, other):
    got = lax.ppermute(other, AX, other_core())
    return (mine + got.astype(F32)).astype(BF).reshape(64, mine.shape[0] // 64, -1)


def body(block_input, w_expand, w_depthwise, w_project, w_qkv, w_out, grad_out):
    _, rows, cols, width = block_input.shape
    tokens = rows * cols
    core = (lax.axis_index("row") % 2).astype(jnp.int32).reshape(1)
    col = lax.axis_index("col").astype(jnp.int32).reshape(1)
    image = block_input[0]
    x = image.reshape(tokens, width)
    go = grad_out[0].reshape(tokens, width)
    act0 = expand_block(x, w_expand, gelu, 0, 2)
    centre = expand_block(x, w_expand, gelu, 1, 2, act0)
    strips, go_side = halo(image, 2, act0, grad_out[0])
    mid, resid, send = forward_block(x, strips, go, centre, w_expand, w_depthwise, w_project)
    arrived = across_chips(send.reshape(64, 8, 2 * width)).reshape(tokens, 2 * width)
    slopes = slopes_block(strips, centre, w_expand, w_depthwise, w_project)
    arrived, (act, slope_c, resid_side) = lax.optimization_barrier((arrived, slopes))
    back, gqkv, attended = attention_block(col, arrived, w_qkv, w_out)
    home = across_chips(back.reshape(64, 8, -1)).reshape(tokens, -1)
    slope_e = expand_block(x, w_expand, gelu_slope, 0, 1)
    attention_pair = add_pair(*attention_grads(core, arrived, gqkv, attended))
    home, slope_e = lax.optimization_barrier((home, slope_e))
    out, gr, side, first_row, last_row, mine, other = residual_block(
        core, home, resid, go, resid_side, go_side, mid
    )
    above, below = shift(last_row, "row", 1), shift(first_row, "row", -1)
    project_pair = add_pair(mine, other)
    first = jnp.concatenate([project_pair, attention_pair], 1)
    above, below, first = lax.optimization_barrier((above, below, first))
    first = across_chips(first)
    gpre, mine, other = backward_block(
        core, x, gr, (above, below, side), act, slope_c, slope_e, w_depthwise, w_project
    )
    gx = input_grads(gpre, w_expand, x, gr)
    second = add_pair(mine, other)
    second, first = lax.optimization_barrier((second, first))
    grad_expand, grad_depth = finish(across_chips(second))
    first = jnp.sum(first.astype(F32), 0)
    return (
        out.reshape(1, rows, cols, width),
        gx.reshape(1, rows, cols, width),
        grad_expand.T,
        grad_depth,
        first[:16].T,
        first[16:28].T,
        first[28:].T,
    )


def solution(mesh):
    tokens = P(None, "row", "col", None)
    split = P(None, AX)
    return jax.shard_map(
        body,
        mesh=mesh,
        in_specs=(tokens, P(), P(), P(), P(), P(), tokens),
        out_specs=(tokens, tokens, split, split, split, split, split),
        check_vma=False,
    )
```
